32 devices in a mesh: section: 2 (over y), grp: 4 (over z), shard: 4 (over x, core).
Axes of the slice: x: 2, y: 2, z: 4, core: 2. Of those that a mesh axis runs over, the one named last changes fastest.
Arguments:
- start: bfloat16 [32, 256, 1152], P(('grp', 'shard')), may hold values from -6 to 6
- out_grad: bfloat16 [32, 256, 1152], P(('grp', 'shard')), may hold values from -6 to 6
- extra_images: int32 [16], P(('grp', 'shard')), may hold values from 0 to 1
- timesteps: int32 [32], P(('grp', 'shard')), may hold values from 0 to 999
- labels: int32 [32], P(('grp', 'shard')), may hold values from 0 to 999
- embed_table: float32 [2000, 1152], P(None, 'section'), may hold values from -6 to 6
- w_qkv: float32 [2, 1152, 3456], P('section', 'shard'), may hold values from -0.1875 to 0.1875
- w_out: float32 [2, 1152, 1152], P('section', 'shard'), may hold values from -0.75 to 0.75
- w_gu: float32 [2, 1152, 6144], P('section', 'shard'), may hold values from -0.1875 to 0.1875
- w_ada: float32 [2, 1152, 6912], P('section', 'shard'), may hold values from -0.1875 to 0.1875
- w_down: float32 [2, 3072, 1152], P('section', None, 'shard'), may hold values from -0.109375 to 0.109375
- small_params: float32 [2, 11664], P('section', 'shard'), may hold values from -0.35 to 1.25, as said below
- feature_moments: float32 [2, 5, 1152], P('section', None, 'shard'), may hold values from 409 to 8192
- other_moments: float32 [2, 20736], P('section'), may hold values from 409 to 8192
- small_moment: float32 [2, 11664], P('section', 'shard'), may hold values from 819 to 32768
Outputs:
- section_out: bfloat16 [2, 32, 256, 1152], P('section', ('grp', 'shard'))
- section_in_grad: bfloat16 [2, 32, 256, 1152], P('section', ('grp', 'shard'))
- cond_grad: float32 [32, 1152], P(('grp', 'shard'), 'section')
- grad_qkv: float32 [2, 1152, 3456], P('section', 'shard')
- grad_out: float32 [2, 1152, 1152], P('section', 'shard')
- grad_gu: float32 [2, 1152, 6144], P('section', 'shard')
- grad_ada: float32 [2, 1152, 6912], P('section', 'shard')
- grad_down: float32 [2, 3072, 1152], P('section', None, 'shard')
- grad_small: float32 [2, 11664], P('section', 'shard')
- new_qkv: float32 [2, 1152, 3456], P('section', 'shard')
- new_out: float32 [2, 1152, 1152], P('section', 'shard')
- new_gu: float32 [2, 1152, 6144], P('section', 'shard')
- new_ada: float32 [2, 1152, 6912], P('section', 'shard')
- new_down: float32 [2, 3072, 1152], P('section', None, 'shard')
- new_small: float32 [2, 11664], P('section', 'shard')
- new_feature_moments: float32 [2, 5, 1152], P('section', None, 'shard')
- new_other_moments: float32 [2, 20736], P('section')
- new_small_moment: float32 [2, 11664], P('section', 'shard')
The draws below stay inside these ranges and needn't reach their ends.
Inputs may be any that keep to these rules, and one draw needn't show every extreme that they name: A device's first extra_images + 1 micro-batches hold live images, the rest padding. `small_params`: biases lie within 0.35 of zero, gains between 0.75 and 1.25.
All inputs are finite; a program needn't handle non-finite values.
Results may differ from the reference program's by a relative error of at most 0.024.
Values may be sent and summed in bfloat16 or wider, within the bound.
A program may use at most 384 MiB of HBM per device.

```python
import math
from functools import partial
import jax
import jax.numpy as jnp
import numpy as np
from jax import lax

D = 1152
HEADS = 16
FF = 3072
CLASSES = 1000
GRID = 16
MB = 2
TIMESTEPS = 1000
HEAD_DIM = 72
LEN = 256
IMAGES = 32
TABLE = 2000
SMALL = 11664
OTHER = 20736
N_GRP = 4
N_SHARD = 4


def draw_small_params(key, part):
    key = jax.random.fold_in(key, 11)
    first_key, second_key = jax.random.split(key)
    biases = 0.35 * jax.random.uniform(first_key, (2, 10 * D), jnp.float32, -1.0, 1.0)
    gains = 1.0 + 0.25 * jax.random.uniform(second_key, (2, 2 * HEAD_DIM), jnp.float32, -1.0, 1.0)
    return jnp.concatenate([biases, gains], axis=1)


def plant(result, rng, smallest, high):
    longest = result.shape.index(max(result.shape))
    spots = []
    for shift in (0, 1):
        where = [jax.random.randint(jax.random.fold_in(rng, axis), (), 0, length) for axis, length in enumerate(result.shape)]
        where[longest] = (where[longest] + shift) % result.shape[longest]
        spots.append(tuple(where))
    return result.at[spots[0]].set(smallest).at[spots[1]].set(high)


def block_levels(own_key, shape, cuts, low, top_value):
    factor_of = 1.0
    for position, shards_of in cuts:
        draws = jax.random.uniform(jax.random.fold_in(jax.random.fold_in(own_key, 6), position), (shards_of,), jnp.float32, low / len(cuts), top_value / len(cuts))
        factor_of = factor_of * jnp.repeat(jnp.exp(draws), shape[position] // shards_of).reshape((-1,) + (1,) * (len(shape) - 1 - position))
    return factor_of


def cumulative_ranks(amount, slope):
    portions = [(1 << 20) // math.isqrt(grade ** slope) + 1 for grade in range(1, amount + 1)]
    scale = 1 + sum(portions) // (1 << 30)
    return np.cumsum(np.array([max(1, weight // scale) for weight in portions]))


def skewed_ids(key, dims, number_of, slope):
    listing = cumulative_ranks(number_of, slope)
    pick = jax.random.randint(jax.random.fold_in(key, 1), dims, 0, int(listing[number_of - 1]))
    grade = jnp.searchsorted(jnp.asarray(listing, jnp.int32), pick, side="right")
    return jax.random.permutation(jax.random.fold_in(key, 2), number_of)[grade].astype(jnp.int32)


def noise(stream_key, dims, scale, most, shards=(), kind=jnp.bfloat16):
    entries = scale * jax.random.normal(stream_key, dims, jnp.float32)
    if shards:
        entries = entries * block_levels(stream_key, dims, shards, -0.22, 0.18)
    return jnp.clip(entries, -most, most).astype(kind)


def setup_inputs(seed: int = 0) -> dict:
    key_of = jax.random.split(jax.random.key(seed), 16)
    start = noise(key_of[0], (IMAGES, LEN, D), 1.0, 6.0, ((0, 16),))
    out_grad = noise(key_of[1], (IMAGES, LEN, D), 1.0, 6.0, ((0, 16),))
    extra_images = plant(skewed_ids(key_of[2], (N_GRP * N_SHARD,), MB, 2), jax.random.fold_in(key_of[2], 3), 0, MB - 1).astype(jnp.int32)
    timesteps = plant(jax.random.randint(key_of[3], (IMAGES,), 0, TIMESTEPS), jax.random.fold_in(key_of[3], 1), 0, TIMESTEPS - 1).astype(jnp.int32)
    labels = plant(jax.random.randint(key_of[4], (IMAGES,), 0, CLASSES), jax.random.fold_in(key_of[4], 1), 0, CLASSES - 1).astype(jnp.int32)
    embed_table = noise(key_of[5], (TABLE, D), 1.0, 6.0, ((1, 2),), jnp.float32)
    w_qkv = noise(key_of[6], (2, D, 3 * D), D ** -0.5, 0.1875, ((0, 2), (1, 4)), jnp.float32)
    w_out = noise(key_of[7], (2, D, D), HEAD_DIM ** -0.5, 0.75, ((0, 2), (1, 4)), jnp.float32)
    w_gu = noise(key_of[8], (2, D, 2 * FF), D ** -0.5, 0.1875, ((0, 2), (1, 4)), jnp.float32)
    w_ada = noise(key_of[9], (2, D, 6 * D), D ** -0.5, 0.1875, ((0, 2), (1, 4)), jnp.float32)
    w_down = noise(key_of[10], (2, FF, D), FF ** -0.5, 0.109375, ((0, 2), (2, 4)), jnp.float32)
    small_params = draw_small_params(jax.random.fold_in(key_of[15], 71), 0)
    feature_moments = jnp.clip(jnp.exp(math.log(8192.0) - 2.997198 * jax.random.uniform(key_of[12], (2, 5, D), jnp.float32) ** block_levels(key_of[12], (2, 5, D), ((0, 2), (2, 4)), -0.2, 0.2)), 409.0, 8192.0)
    other_moments = jnp.clip(jnp.exp(math.log(8192.0) - 2.997198 * jax.random.uniform(key_of[13], (2, OTHER), jnp.float32) ** block_levels(key_of[13], (2, OTHER), ((0, 2),), -0.2, 0.2)), 409.0, 8192.0)
    small_moment = jnp.clip(jnp.exp(math.log(32768.0) - 3.6891236 * jax.random.uniform(key_of[14], (2, SMALL), jnp.float32) ** block_levels(key_of[14], (2, SMALL), ((0, 2), (1, 4)), -0.2, 0.2)), 819.0, 32768.0)
    return {"start": start, "out_grad": out_grad, "extra_images": extra_images, "timesteps": timesteps, "labels": labels, "embed_table": embed_table, "w_qkv": w_qkv, "w_out": w_out, "w_gu": w_gu, "w_ada": w_ada, "w_down": w_down, "small_params": small_params, "feature_moments": feature_moments, "other_moments": other_moments, "small_moment": small_moment}


EPS = 1e-06
TINY = 1e-30
RATE = 0.04
RATE_SMALL = 0.05
DECAY = 0.5

@jax.custom_vjp
def low(v):
    return lax.optimization_barrier(v.astype(jnp.bfloat16)).astype(jnp.float32)

@jax.custom_vjp
def low_back(v):
    return v

def low_keep(v):
    return (low(v), None)

def low_pass(kept, grad):
    return (grad,)

def back_keep(v):
    return (v, None)

def back_low(kept, grad):
    return (low(grad),)
low.defvjp(low_keep, low_pass)
low_back.defvjp(back_keep, back_low)

def high_dot(left, right):
    return jnp.dot(left, right, precision=lax.Precision.HIGHEST)

def rms_norm(values):
    return values * lax.rsqrt(lax.optimization_barrier(jnp.mean(values * values, axis=-1, keepdims=True)) + EPS)

def rope_tables():
    quarter = HEAD_DIM // 4
    tokens = jnp.arange(LEN)
    row_place = (tokens // GRID).astype(jnp.float32)
    col_place = (tokens % GRID).astype(jnp.float32)
    inverse = 10000.0 ** (-jnp.arange(quarter).astype(jnp.float32) / quarter)
    row_angle = row_place[:, None] * inverse[None, :]
    col_angle = col_place[:, None] * inverse[None, :]
    angles = jnp.concatenate([row_angle, row_angle, col_angle, col_angle], axis=1)
    return (jnp.cos(angles)[:, None, :], jnp.sin(angles)[:, None, :])

def rotate_pairs(values):
    shaped = values.reshape(values.shape[:-1] + (2, 2, HEAD_DIM // 4))
    turned = jnp.stack([-shaped[..., 1, :], shaped[..., 0, :]], axis=-2)
    return turned.reshape(values.shape)

def rotary(values, cosines, sines):
    return values * cosines + rotate_pairs(values) * sines

def split_small(small):
    return (small[:3 * D], small[3 * D:4 * D], small[4 * D:10 * D], small[10 * D:10 * D + HEAD_DIM], small[10 * D + HEAD_DIM:])

def image_layer(matrices, smalls, cosines, sines, image_item):
    xin, modrow = image_item
    w_qkv, w_out, w_gu, w_down = matrices
    b_qkv, b_out, q_gain, k_gain = smalls
    shift1, scale1, gate1, shift2, scale2, gate2 = jnp.split(modrow, 6)
    attn_in = low(rms_norm(xin) * (1.0 + scale1) + shift1)
    projected = low_back(high_dot(attn_in, w_qkv) + b_qkv)
    query_heads = low(rotary(rms_norm(projected[:, :D].reshape(LEN, HEADS, HEAD_DIM)) * q_gain, cosines, sines))
    key_heads = low(rotary(rms_norm(projected[:, D:2 * D].reshape(LEN, HEADS, HEAD_DIM)) * k_gain, cosines, sines))
    value_heads = low(projected[:, 2 * D:].reshape(LEN, HEADS, HEAD_DIM))
    scores = low_back(jnp.einsum('qhe,khe->hqk', query_heads, key_heads, precision=lax.Precision.HIGHEST) * HEAD_DIM ** (-0.5))
    probs_low = low(jax.nn.softmax(scores, axis=-1))
    mixed = jnp.einsum('hqk,khe->qhe', probs_low, value_heads, precision=lax.Precision.HIGHEST).reshape(LEN, D)
    mixed = low_back(low(mixed))
    branch = low_back(high_dot(mixed, w_out) + b_out)
    middle = xin + gate1 * branch
    ffn_in = low(rms_norm(middle) * (1.0 + scale2) + shift2)
    gate_up = low_back(high_dot(ffn_in, w_gu))
    hidden = low(jax.nn.silu(gate_up[:, :FF]) * gate_up[:, FF:])
    return middle + gate2 * low_back(high_dot(hidden, w_down))

def forward(parameters, entering, condition, probe_zero):
    matrices, w_ada, small_params = parameters
    cosines, sines = rope_tables()
    activated = low(jax.nn.silu(condition))
    checked = jax.checkpoint(image_layer)
    current = entering
    middle = entering
    for level in range(2):
        smalls = split_small(low(small_params[level]))
        modulation = low_back(high_dot(activated, low(w_ada[level])) + smalls[2])
        weights = tuple((low(matrix[level]) for matrix in matrices))
        layer_smalls = (smalls[0], smalls[1], smalls[3], smalls[4])
        current = lax.map(partial(checked, weights, layer_smalls, cosines, sines), (current, modulation))
        if level == 0:
            middle = low_back(low(current)) + probe_zero
            current = middle
    return (current, middle)

def factored_update(previous, gradient, row_state, col_state):
    square = gradient * gradient + TINY
    row_new = DECAY * row_state + (1.0 - DECAY) * lax.optimization_barrier(jnp.mean(square, axis=2))
    col_new = DECAY * col_state + (1.0 - DECAY) * lax.optimization_barrier(jnp.mean(square, axis=1))
    second = row_new[:, :, None] * col_new[:, None, :] / lax.optimization_barrier(jnp.mean(row_new, axis=1))[:, None, None]
    return (previous - RATE * gradient * lax.rsqrt(second), row_new, col_new)

def reference(start, out_grad, extra_images, timesteps, labels, embed_table, w_qkv, w_out, w_gu, w_ada, w_down, small_params, feature_moments, other_moments, small_moment):
    image_ids = jnp.arange(IMAGES)
    owners = image_ids // MB
    places = image_ids % MB
    live_mask = (places < extra_images[owners] + 1).astype(jnp.float32)[:, None, None]
    condition = embed_table[timesteps] + embed_table[TIMESTEPS + labels]
    entering = start.astype(jnp.float32)
    parameters = ((w_qkv, w_out, w_gu, w_down), w_ada, small_params)
    probe_zero = jnp.zeros_like(entering)
    (final_out, middle), pull_back = jax.vjp(forward, parameters, entering, condition, probe_zero)
    gradients, entering_grad, cond_grad, probe_grad = pull_back((out_grad.astype(jnp.float32) * live_mask, jnp.zeros_like(middle)))
    (grad_qkv, grad_out, grad_gu, grad_down), grad_ada, grad_small = gradients
    section_out = jnp.stack([middle * live_mask, final_out * live_mask]).astype(jnp.bfloat16)
    section_in_grad = jnp.stack([entering_grad, probe_grad]).astype(jnp.bfloat16)
    widths = (3 * D, D, 2 * FF, 6 * D, FF)
    wide_old = (w_qkv, w_out, w_gu, w_ada, jnp.swapaxes(w_down, 1, 2))
    wide_grads = (grad_qkv, grad_out, grad_gu, grad_ada, jnp.swapaxes(grad_down, 1, 2))
    new_wide = []
    new_rows = []
    new_cols = []
    offset = 0
    for index in range(5):
        updated, row_new, col_new = factored_update(wide_old[index], wide_grads[index], feature_moments[:, index], other_moments[:, offset:offset + widths[index]])
        new_wide.append(updated)
        new_rows.append(row_new)
        new_cols.append(col_new)
        offset += widths[index]
    small_new = DECAY * small_moment + (1.0 - DECAY) * (grad_small * grad_small + TINY)
    new_small = small_params - RATE_SMALL * grad_small * lax.rsqrt(small_new)
    return (section_out, section_in_grad, cond_grad, grad_qkv, grad_out, grad_gu, grad_ada, grad_down, grad_small, new_wide[0], new_wide[1], new_wide[2], new_wide[3], jnp.swapaxes(new_wide[4], 1, 2), new_small, jnp.stack(new_rows, axis=1), jnp.concatenate(new_cols, axis=1), small_new)
```

```python
import functools

import jax
import jax.numpy as jnp
from jax import lax
from jax.experimental import pallas as pl
from jax.experimental.pallas import tpu as pltpu
from jax.sharding import PartitionSpec as P

HEADS = 16
FF = 3072
GRID = 16
MB = 2
TIMESTEPS = 1000
HEAD_DIM = 72
LEN = 256


EPS = 1e-06
TINY = 1e-30
RATE = 0.04
RATE_SMALL = 0.05
DECAY = 0.5


def passed_along(block, axis, distance):
    devices = range(lax.axis_size(axis))
    route = [(i - distance, i) for i in devices if i - distance in devices]
    return lax.ppermute(block, axis, route)


def rope_tables():
    quarter = HEAD_DIM // 4
    tokens = jnp.arange(LEN)
    row_place = (tokens // GRID).astype(jnp.float32)
    col_place = (tokens % GRID).astype(jnp.float32)
    inverse = 10000.0 ** (-jnp.arange(quarter).astype(jnp.float32) / quarter)
    row_angle = row_place[:, None] * inverse[None, :]
    col_angle = col_place[:, None] * inverse[None, :]
    angles = jnp.concatenate([row_angle, row_angle, col_angle, col_angle], axis=1)
    return (jnp.cos(angles)[:, None, :], jnp.sin(angles)[:, None, :])


def rotate_pairs(values):
    shaped = values.reshape(values.shape[:-1] + (2, 2, HEAD_DIM // 4))
    turned = jnp.stack([-shaped[..., 1, :], shaped[..., 0, :]], axis=-2)
    return turned.reshape(values.shape)


def rotary(values, tables):
    return values * tables[0] + rotate_pairs(values) * tables[1]


def rotary_back(values, tables):
    return values * tables[0] - rotate_pairs(values * tables[1])


def norm_rate(values):
    return lax.rsqrt(jnp.mean(values * values, axis=-1, keepdims=True) + EPS)


def norm_back(unit, rate, incoming):
    return rate * (incoming - unit * jnp.mean(incoming * unit, axis=-1, keepdims=True))


def dot_back(incoming, matrix):
    return lax.dot_general(
        incoming, matrix, (((1,), (1,)), ((), ())), preferred_element_type=jnp.float32
    )


def layer_forward(xin, modrow, matrices, smalls, tables):
    w_qkv, w_out, w_gu, w_down = matrices
    b_qkv, b_out, q_gain, k_gain = smalls
    model_width = xin.shape[-1]
    shift1, scale1, gate1, shift2, scale2, gate2 = jnp.split(modrow, 6)
    rate1 = norm_rate(xin)
    norm1 = xin * rate1
    in_attn = (norm1 * (1.0 + scale1) + shift1).astype(jnp.bfloat16)
    projected = jnp.dot(in_attn, w_qkv, preferred_element_type=jnp.float32) + b_qkv
    q_raw = projected[:, :model_width].reshape(LEN, HEADS, HEAD_DIM)
    k_raw = projected[:, model_width : 2 * model_width].reshape(LEN, HEADS, HEAD_DIM)
    v_low = projected[:, 2 * model_width :].reshape(LEN, HEADS, HEAD_DIM).astype(jnp.bfloat16)
    q_rate = norm_rate(q_raw)
    q_unit = q_raw * q_rate
    k_rate = norm_rate(k_raw)
    k_unit = k_raw * k_rate
    q_low = rotary(q_unit * q_gain, tables).astype(jnp.bfloat16)
    k_low = rotary(k_unit * k_gain, tables).astype(jnp.bfloat16)
    scores = jnp.einsum(
        "qhe,khe->hqk", q_low, k_low, preferred_element_type=jnp.float32
    ) * HEAD_DIM ** (-0.5)
    probs = jax.nn.softmax(scores, axis=-1)
    probs_low = probs.astype(jnp.bfloat16)
    mixed = jnp.einsum("hqk,khe->qhe", probs_low, v_low, preferred_element_type=jnp.float32)
    mixed_low = mixed.reshape(LEN, model_width).astype(jnp.bfloat16)
    proj = jnp.dot(mixed_low, w_out, preferred_element_type=jnp.float32) + b_out
    middle = xin + gate1 * proj
    rate2 = norm_rate(middle)
    norm2 = middle * rate2
    in_ffn = (norm2 * (1.0 + scale2) + shift2).astype(jnp.bfloat16)
    gate_up = jnp.dot(in_ffn, w_gu, preferred_element_type=jnp.float32)
    gate_pre = gate_up[:, :FF]
    up_part = gate_up[:, FF:]
    hid_low = (jax.nn.silu(gate_pre) * up_part).astype(jnp.bfloat16)
    ffn = dot_back(hid_low, w_down)
    return {
        "modrow": modrow,
        "rate1": rate1,
        "norm1": norm1,
        "in_attn": in_attn,
        "q_unit": q_unit,
        "q_rate": q_rate,
        "k_unit": k_unit,
        "k_rate": k_rate,
        "q_low": q_low,
        "k_low": k_low,
        "v_low": v_low,
        "probs": probs,
        "probs_low": probs_low,
        "mixed_low": mixed_low,
        "proj": proj,
        "rate2": rate2,
        "norm2": norm2,
        "in_ffn": in_ffn,
        "gate_pre": gate_pre,
        "up_part": up_part,
        "hid_low": hid_low,
        "ffn": ffn,
        "result": middle + gate2 * ffn,
    }


def layer_backward(parts, incoming, matrices, smalls, tables):
    w_qkv, w_out, w_gu, w_down = matrices
    b_qkv, b_out, q_gain, k_gain = smalls
    shift1, scale1, gate1, shift2, scale2, gate2 = jnp.split(parts["modrow"], 6)
    d_ffn = (gate2 * incoming).astype(jnp.bfloat16)
    d_gate2 = jnp.sum(incoming * parts["ffn"], axis=0)
    d_hid = jnp.dot(d_ffn, w_down, preferred_element_type=jnp.float32)
    gate_pre = parts["gate_pre"]
    sigma = jax.nn.sigmoid(gate_pre)
    d_gate_pre = d_hid * parts["up_part"] * sigma * (1.0 + gate_pre * (1.0 - sigma))
    d_gu = jnp.concatenate([d_gate_pre, d_hid * gate_pre * sigma], axis=1).astype(jnp.bfloat16)
    d_in_ffn = dot_back(d_gu, w_gu)
    d_scale2 = jnp.sum(d_in_ffn * parts["norm2"], axis=0)
    d_shift2 = jnp.sum(d_in_ffn, axis=0)
    d_middle = incoming + norm_back(parts["norm2"], parts["rate2"], d_in_ffn * (1.0 + scale2))
    d_proj = (gate1 * d_middle).astype(jnp.bfloat16)
    d_gate1 = jnp.sum(d_middle * parts["proj"], axis=0)
    d_mixed = dot_back(d_proj, w_out).astype(jnp.bfloat16).reshape(LEN, HEADS, HEAD_DIM)
    d_probs = jnp.einsum(
        "qhe,khe->hqk", d_mixed, parts["v_low"], preferred_element_type=jnp.float32
    )
    d_value = jnp.einsum(
        "hqk,qhe->khe", parts["probs_low"], d_mixed, preferred_element_type=jnp.float32
    )
    probs = parts["probs"]
    d_scores = (probs * (d_probs - jnp.sum(probs * d_probs, axis=-1, keepdims=True))).astype(
        jnp.bfloat16
    )
    d_q_rot = HEAD_DIM ** (-0.5) * jnp.einsum(
        "hqk,khe->qhe", d_scores, parts["k_low"], preferred_element_type=jnp.float32
    )
    d_k_rot = HEAD_DIM ** (-0.5) * jnp.einsum(
        "hqk,qhe->khe", d_scores, parts["q_low"], preferred_element_type=jnp.float32
    )
    d_q_norm = rotary_back(d_q_rot, tables)
    d_k_norm = rotary_back(d_k_rot, tables)
    d_q_gain = jnp.sum(d_q_norm * parts["q_unit"], axis=(0, 1))
    d_k_gain = jnp.sum(d_k_norm * parts["k_unit"], axis=(0, 1))
    d_query = norm_back(parts["q_unit"], parts["q_rate"], d_q_norm * q_gain)
    d_key = norm_back(parts["k_unit"], parts["k_rate"], d_k_norm * k_gain)
    d_qkv = jnp.concatenate(
        [d_query.reshape(LEN, -1), d_key.reshape(LEN, -1), d_value.reshape(LEN, -1)], axis=1
    ).astype(jnp.bfloat16)
    d_in_attn = dot_back(d_qkv, w_qkv)
    d_scale1 = jnp.sum(d_in_attn * parts["norm1"], axis=0)
    d_shift1 = jnp.sum(d_in_attn, axis=0)
    d_entering = d_middle + norm_back(parts["norm1"], parts["rate1"], d_in_attn * (1.0 + scale1))
    d_mod = jnp.concatenate([d_shift1, d_scale1, d_gate1, d_shift2, d_scale2, d_gate2]).astype(
        jnp.bfloat16
    )
    d_small = jnp.concatenate(
        [
            jnp.sum(d_qkv.astype(jnp.float32), axis=0),
            jnp.sum(d_proj.astype(jnp.float32), axis=0),
            d_q_gain,
            d_k_gain,
        ]
    )
    return {
        "d_entering": d_entering,
        "d_qkv": d_qkv,
        "d_proj": d_proj,
        "d_gu": d_gu,
        "d_mod": d_mod,
        "d_ffn": d_ffn,
        "d_small": d_small,
    }


CHUNK = 384
AHEAD = 3
LAG = 2
SLOTS = 4
MESH = pl.DeviceIdType.MESH


def place():
    return lax.axis_index("section"), lax.axis_index("grp"), lax.axis_index("shard")


def gather_kernel(chips, block, own_ref, all_ref, here_sem, sib_sem, x_sem, z_sem, f_sem):
    sec, grp, me = place()
    core = me % 2
    chip = me // 2
    half = grp % 2
    count = own_ref.shape[0] // block
    width = own_ref.shape[1] // 2
    sibling = (sec, grp, me ^ 1)
    across = (sec, grp ^ 1, me)

    barrier = pltpu.get_barrier_semaphore()
    pl.semaphore_signal(barrier, inc=1, device_id=sibling, device_id_type=MESH)
    pl.semaphore_signal(barrier, inc=1, device_id=across, device_id_type=MESH)
    for k in range(1, chips):
        pl.semaphore_signal(
            barrier, inc=1, device_id=(sec, grp, 2 * (chip ^ k) + core), device_id_type=MESH
        )
    pl.semaphore_wait(barrier, chips + 1)

    def part(step, side):
        lines = pl.ds(pl.multiple_of(step * block, block), block)
        return lines, pl.ds(pl.multiple_of(side * width, 128), width)

    def chip_copy(k, step):
        lines, cols = part(step, half)
        return pltpu.make_async_remote_copy(
            src_ref=own_ref.at[lines, cols],
            dst_ref=all_ref.at[me, lines, cols],
            send_sem=x_sem.at[0, k - 1, step],
            recv_sem=x_sem.at[1, k - 1, step],
            device_id=(sec, grp, 2 * (chip ^ k) + core),
            device_id_type=MESH,
        )

    def chip_arrival(k, step):
        lines, cols = part(step, half)
        owner = 2 * (chip ^ k) + core
        return pltpu.make_async_remote_copy(
            src_ref=own_ref.at[lines, cols],
            dst_ref=all_ref.at[owner, lines, cols],
            send_sem=x_sem.at[0, k - 1, step],
            recv_sem=x_sem.at[1, k - 1, step],
            device_id=(sec, grp, owner),
            device_id_type=MESH,
        )

    def onward(k, step, side, sems, row, target):
        owner = 2 * (chip ^ k) + core
        lines, cols = part(step, side)
        region = all_ref.at[owner, lines, cols]
        return pltpu.make_async_remote_copy(
            src_ref=region,
            dst_ref=region,
            send_sem=sems.at[0, row, step],
            recv_sem=sems.at[1, row, step],
            device_id=target,
            device_id_type=MESH,
        )

    def from_sibling(k, step, side, row):
        owner = 2 * (chip ^ k) + 1 - core
        lines, cols = part(step, side)
        region = all_ref.at[owner, lines, cols]
        return pltpu.make_async_remote_copy(
            src_ref=region,
            dst_ref=region,
            send_sem=f_sem.at[0, row, step],
            recv_sem=f_sem.at[1, row, step],
            device_id=sibling,
            device_id_type=MESH,
        )

    def beside(step):
        lines = pl.ds(pl.multiple_of(step * block, block), block)
        return pltpu.make_async_remote_copy(
            src_ref=own_ref.at[lines],
            dst_ref=all_ref.at[me, lines],
            send_sem=sib_sem.at[0, step],
            recv_sem=sib_sem.at[1, step],
            device_id=sibling,
            device_id_type=MESH,
        )

    def start_chip(step):
        for k in range(1, chips):
            chip_copy(k, step).start()

    for step in range(AHEAD):
        start_chip(step)
    here = pltpu.make_async_copy(own_ref, all_ref.at[me], here_sem)
    here.start()

    def relay(step, carry):
        @pl.when(step < count)
        def _():
            for k in range(1, chips):
                chip_arrival(k, step).wait_recv()
                onward(k, step, half, z_sem, k - 1, across).start()
                onward(k, step, half, f_sem, 2 * (k - 1), sibling).start()
                chip_copy(k, step).wait_send()
            beside(step).start()

        @pl.when(step + AHEAD < count)
        def _():
            start_chip(step + AHEAD)

        @pl.when(step >= LAG)
        def _():
            for k in range(1, chips):
                onward(k, step - LAG, 1 - half, z_sem, k - 1, across).wait_recv()
                onward(k, step - LAG, 1 - half, f_sem, 2 * (k - 1) + 1, sibling).start()
                onward(k, step - LAG, half, z_sem, k - 1, across).wait_send()

        return carry

    lax.fori_loop(0, count + LAG, relay, 0)

    def finish(step, carry):
        for k in range(1, chips):
            onward(k, step, half, f_sem, 2 * (k - 1), sibling).wait_send()
            onward(k, step, 1 - half, f_sem, 2 * (k - 1) + 1, sibling).wait_send()
            from_sibling(k, step, half, 2 * (k - 1)).wait_recv()
            from_sibling(k, step, 1 - half, 2 * (k - 1) + 1).wait_recv()
        beside(step).wait()
        return carry

    lax.fori_loop(0, count, finish, 0)
    here.wait()


def gather_rows(own):
    shards = lax.axis_size("shard")
    chips = shards // 2
    rows, width = own.shape
    block = 16 if rows % 16 == 0 else rows
    count = rows // block
    return pl.pallas_call(
        functools.partial(gather_kernel, chips, block),
        out_shape=jax.ShapeDtypeStruct((shards, rows, width), own.dtype),
        in_specs=[pl.BlockSpec(memory_space=pltpu.VMEM)],
        out_specs=pl.BlockSpec(memory_space=pl.ANY),
        scratch_shapes=[
            pltpu.SemaphoreType.DMA,
            pltpu.SemaphoreType.DMA((2, count)),
            pltpu.SemaphoreType.DMA((2, chips - 1, count)),
            pltpu.SemaphoreType.DMA((2, chips - 1, count)),
            pltpu.SemaphoreType.DMA((2, 2 * (chips - 1), count)),
        ],
        compiler_params=pltpu.CompilerParams(
            collective_id=0, has_side_effects=True, vmem_limit_bytes=32 * 1024 * 1024
        ),
        cost_estimate=pl.CostEstimate(flops=0, bytes_accessed=300_000_000, transcendentals=0),
        name="gather_rows",
    )(own)


def reduce_kernel(
    shards,
    groups,
    firsts,
    left_ref,
    right0,
    right1,
    right2,
    right3,
    sum_ref,
    rowsq_ref,
    colsq_ref,
    right_buf,
    send1,
    keep1,
    recv1,
    send2,
    recv2,
    keep2,
    keep3,
    send3,
    recv3,
    final,
    recv5,
    right_sem,
    sem1,
    sem2,
    sem3,
    sem5,
    out_sem,
):
    rights = (right0, right1, right2, right3)
    chips = shards // 2
    total = sum_ref.shape[1] // CHUNK
    sec, grp, me = place()
    core = me % 2
    chip = me // 2
    middle = groups // 2
    lower = grp < middle
    depth = jnp.where(lower, middle - 1 - grp, grp - middle)
    inner = jnp.where(lower, grp + 1, grp - 1)
    outer = jnp.where(lower, grp - 1, grp + 1)
    has_outer = depth < middle - 1
    sibling = (sec, grp, me ^ 1)

    barrier = pltpu.get_barrier_semaphore()
    pl.semaphore_signal(barrier, inc=1, device_id=sibling, device_id_type=MESH)
    for k in range(1, chips):
        pl.semaphore_signal(
            barrier, inc=1, device_id=(sec, grp, 2 * (chip ^ k) + core), device_id_type=MESH
        )
    pl.semaphore_signal(barrier, inc=1, device_id=(sec, inner, me), device_id_type=MESH)

    @pl.when(has_outer)
    def _():
        pl.semaphore_signal(barrier, inc=1, device_id=(sec, outer, me), device_id_type=MESH)

    pl.semaphore_wait(barrier, chips + 1 + jnp.where(has_outer, 1, 0))

    def which(item):
        place_of = 0
        for first in firsts[1:]:
            place_of = place_of + jnp.where(item >= first, 1, 0)
        return place_of

    def fetch(item):
        slot = item % 3
        for index, right in enumerate(rights):
            last = firsts[index + 1] if index + 1 < len(firsts) else total

            @pl.when((item >= firsts[index]) & (item < last))
            def _():
                start = pl.multiple_of((item - firsts[index]) * CHUNK, CHUNK)
                pltpu.make_async_copy(
                    right.at[:, pl.ds(start, CHUNK)], right_buf.at[slot], right_sem.at[slot]
                ).start()

    def arrived(item):
        slot = item % 3
        pltpu.make_async_copy(
            right0.at[:, pl.ds(0, CHUNK)], right_buf.at[slot], right_sem.at[slot]
        ).wait()

    def copy1(item):
        slot = item % SLOTS
        return pltpu.make_async_remote_copy(
            src_ref=send1.at[slot],
            dst_ref=recv1.at[slot],
            send_sem=sem1.at[0, slot],
            recv_sem=sem1.at[1, slot],
            device_id=sibling,
            device_id_type=MESH,
        )

    def copy2(item, k):
        slot = item % SLOTS
        return pltpu.make_async_remote_copy(
            src_ref=send2.at[slot, k - 1],
            dst_ref=recv2.at[slot, k - 1],
            send_sem=sem2.at[0, slot, k - 1],
            recv_sem=sem2.at[1, slot, k - 1],
            device_id=(sec, grp, 2 * (chip ^ k) + core),
            device_id_type=MESH,
        )

    def copy3(item, kind):
        slot = item % SLOTS
        return pltpu.make_async_remote_copy(
            src_ref=send3.at[slot],
            dst_ref=recv3.at[kind, slot],
            send_sem=sem3.at[0, 0, slot],
            recv_sem=sem3.at[1, kind, slot],
            device_id=(sec, inner, me),
            device_id_type=MESH,
        )

    def copy5(item):
        slot = item % SLOTS
        return pltpu.make_async_remote_copy(
            src_ref=final.at[slot],
            dst_ref=recv5.at[slot],
            send_sem=sem5.at[0, slot],
            recv_sem=sem5.at[1, slot],
            device_id=(sec, outer, me),
            device_id_type=MESH,
        )

    def copy_out(item):
        slot = item % SLOTS
        start = pl.multiple_of(item * CHUNK, CHUNK)
        return pltpu.make_async_copy(
            final.at[slot], sum_ref.at[:, pl.ds(start, CHUNK)], out_sem.at[slot]
        )

    send_kind = jnp.where(depth == 0, 1, 0)
    lag3 = 2 + middle - 1 - depth
    lag5 = middle + 2 + depth
    rowsq_ref[...] = jnp.zeros_like(rowsq_ref)
    fetch(0)
    fetch(1)

    def step(tick, carry):
        item0 = tick

        @pl.when(item0 < total)
        def _():
            slot = item0 % SLOTS

            @pl.when(item0 >= SLOTS)
            def _():
                copy1(item0 - SLOTS).wait_send()

            @pl.when(item0 + 2 < total)
            def _():
                fetch(item0 + 2)

            arrived(item0)
            matrix = which(item0)

            def multiply(k, carry):
                right = right_buf[item0 % 3]
                theirs = jnp.dot(
                    left_ref[matrix, 2 * k + 1 - core], right, preferred_element_type=jnp.float32
                )
                send1[slot, k] = theirs.astype(jnp.bfloat16)
                keep1[item0 % 2, k] = jnp.dot(
                    left_ref[matrix, 2 * k + core], right, preferred_element_type=jnp.float32
                )
                return carry

            lax.fori_loop(0, chips, multiply, 0)
            copy1(item0).start()

        item1 = tick - 1

        @pl.when((item1 >= 0) & (item1 < total))
        def _():
            slot = item1 % SLOTS
            copy1(item1).wait_recv()

            @pl.when(item1 >= SLOTS)
            def _():
                for k in range(1, chips):
                    copy2(item1 - SLOTS, k).wait_send()

            for k in range(1, chips):
                other = chip ^ k
                send2[slot, k - 1] = (
                    keep1[item1 % 2, other] + recv1[slot, other].astype(jnp.float32)
                ).astype(jnp.bfloat16)
                copy2(item1, k).start()
            keep2[item1 % 2] = keep1[item1 % 2, chip] + recv1[slot, chip].astype(jnp.float32)

        item2 = tick - 2

        @pl.when((item2 >= 0) & (item2 < total))
        def _():
            slot = item2 % SLOTS
            value = keep2[item2 % 2]
            for k in range(1, chips):
                copy2(item2, k).wait_recv()
                value = value + recv2[slot, k - 1].astype(jnp.float32)
            keep3[item2 % (middle + 1)] = value

        item3 = tick - lag3

        @pl.when((item3 >= 0) & (item3 < total))
        def _():
            slot = item3 % SLOTS

            @pl.when(item3 >= SLOTS)
            def _():
                copy3(item3 - SLOTS, send_kind).wait_send()

            @pl.when(has_outer)
            def _():
                copy3(item3, 0).wait_recv()
                send3[slot] = (
                    keep3[item3 % (middle + 1)] + recv3[0, slot].astype(jnp.float32)
                ).astype(jnp.bfloat16)

            @pl.when(jnp.logical_not(has_outer))
            def _():
                send3[slot] = keep3[item3 % (middle + 1)].astype(jnp.bfloat16)

            copy3(item3, send_kind).start()

        item5 = tick - lag5

        @pl.when((item5 >= 0) & (item5 < total))
        def _():
            slot = item5 % SLOTS

            @pl.when(item5 >= SLOTS)
            def _():
                copy_out(item5 - SLOTS).wait()

                @pl.when(has_outer)
                def _():
                    copy5(item5 - SLOTS).wait_send()

            @pl.when(depth == 0)
            def _():
                copy3(item5, 1).wait_recv()
                final[slot] = (
                    send3[slot].astype(jnp.float32) + recv3[1, slot].astype(jnp.float32)
                ).astype(jnp.bfloat16)

            @pl.when(depth > 0)
            def _():
                copy5(item5).wait_recv()
                final[slot] = recv5[slot]

            @pl.when(has_outer)
            def _():
                copy5(item5).start()

            copy_out(item5).start()
            value = final[slot].astype(jnp.float32)
            square = value * value + TINY
            folded = square[:, :128]
            for start in range(128, CHUNK, 128):
                folded = folded + square[:, start : start + 128]
            matrix = which(item5)
            rowsq_ref[matrix] = rowsq_ref[matrix] + folded
            colsq_ref[item5] = jnp.sum(square, axis=0, keepdims=True)

        return carry

    lax.fori_loop(0, total + groups + 1, step, 0)

    def drain(offset, carry):
        item = total - SLOTS + offset
        copy1(item).wait_send()
        for k in range(1, chips):
            copy2(item, k).wait_send()
        copy3(item, send_kind).wait_send()
        copy_out(item).wait()

        @pl.when(has_outer)
        def _():
            copy5(item).wait_send()

        return carry

    lax.fori_loop(0, SLOTS, drain, 0)


def reduce_grads(left, rights):
    shards = lax.axis_size("shard")
    groups = lax.axis_size("grp")
    chips = shards // 2
    middle = groups // 2
    matrices, _, rows, tokens = left.shape
    widths = [right.shape[1] for right in rights]
    width = sum(widths)
    firsts = [sum(widths[:index]) // CHUNK for index in range(matrices)]
    low, high = jnp.bfloat16, jnp.float32
    block = (rows, CHUNK)
    return pl.pallas_call(
        functools.partial(reduce_kernel, shards, groups, firsts),
        out_shape=(
            jax.ShapeDtypeStruct((rows, width), low),
            jax.ShapeDtypeStruct((matrices, rows, 128), high),
            jax.ShapeDtypeStruct((width // CHUNK, 1, CHUNK), high),
        ),
        in_specs=[pl.BlockSpec(memory_space=pltpu.VMEM)]
        + [pl.BlockSpec(memory_space=pl.ANY)] * matrices,
        out_specs=(
            pl.BlockSpec(memory_space=pl.ANY),
            pl.BlockSpec(memory_space=pltpu.VMEM),
            pl.BlockSpec(memory_space=pltpu.VMEM),
        ),
        scratch_shapes=[
            pltpu.VMEM((3, tokens, CHUNK), low),
            pltpu.VMEM((SLOTS, chips) + block, low),
            pltpu.VMEM((2, chips) + block, high),
            pltpu.VMEM((SLOTS, chips) + block, low),
            pltpu.VMEM((SLOTS, chips - 1) + block, low),
            pltpu.VMEM((SLOTS, chips - 1) + block, low),
            pltpu.VMEM((2,) + block, high),
            pltpu.VMEM((middle + 1,) + block, high),
            pltpu.VMEM((SLOTS,) + block, low),
            pltpu.VMEM((2, SLOTS) + block, low),
            pltpu.VMEM((SLOTS,) + block, low),
            pltpu.VMEM((SLOTS,) + block, low),
            pltpu.SemaphoreType.DMA((3,)),
            pltpu.SemaphoreType.DMA((2, SLOTS)),
            pltpu.SemaphoreType.DMA((2, SLOTS, chips - 1)),
            pltpu.SemaphoreType.DMA((2, 2, SLOTS)),
            pltpu.SemaphoreType.DMA((2, SLOTS)),
            pltpu.SemaphoreType.DMA((SLOTS,)),
        ],
        compiler_params=pltpu.CompilerParams(
            collective_id=1, has_side_effects=True, vmem_limit_bytes=48 * 1024 * 1024
        ),
        cost_estimate=pl.CostEstimate(flops=0, bytes_accessed=600_000_000, transcendentals=0),
        name="reduce_grads",
    )(left, *rights)


def body(
    start,
    out_grad,
    extra_images,
    timesteps,
    labels,
    embed_table,
    w_qkv,
    w_out,
    w_gu,
    w_ada,
    w_down,
    small_params,
    feature_moments,
    other_moments,
    small_moment,
):
    model_width = start.shape[-1]
    section_index = lax.axis_index("section")
    shard_index = lax.axis_index("shard")
    group_index = lax.axis_index("grp")
    sections = lax.axis_size("section")
    shards = lax.axis_size("shard")
    groups = lax.axis_size("grp")
    rows = w_qkv.shape[1]
    low = jnp.bfloat16
    high = jnp.float32
    widths = (3 * model_width, model_width, 2 * FF, FF)
    starts = (0, widths[0], widths[0] + widths[1], widths[0] + widths[1] + widths[2])
    own = jnp.concatenate([w_qkv[0], w_out[0], w_gu[0], w_down[0].T], axis=1).astype(low)
    everything = gather_rows(own).reshape(model_width, sum(widths))
    matrices = tuple(
        everything[:, first : first + width] for first, width in zip(starts, widths)
    )
    ada_low = w_ada[0].astype(low)
    small_all = lax.all_gather(small_params[0].astype(low), "shard", axis=0, tiled=True)
    small_all = small_all.astype(high)
    b_qkv = small_all[: 3 * model_width]
    b_out = small_all[3 * model_width : 4 * model_width]
    b_ada = small_all[4 * model_width : 10 * model_width]
    q_gain = small_all[10 * model_width : 10 * model_width + HEAD_DIM]
    k_gain = small_all[10 * model_width + HEAD_DIM :]
    smalls = (b_qkv, b_out, q_gain, k_gain)
    tables = rope_tables()
    half_cond = embed_table[timesteps] + embed_table[TIMESTEPS + labels]
    cond_all = lax.all_gather(half_cond, ("section", "shard"))
    cond_all = cond_all.reshape(sections, shards * MB, half_cond.shape[1])
    cond_all = cond_all.transpose(1, 0, 2).reshape(shards * MB, model_width)
    act_all = jax.nn.silu(cond_all).astype(low)
    condition = lax.dynamic_slice_in_dim(cond_all, shard_index * MB, MB, 0)
    act_low = lax.dynamic_slice_in_dim(act_all, shard_index * MB, MB, 0)
    act_columns = lax.dynamic_slice_in_dim(act_all, shard_index * rows, rows, 1)
    partial_mod = jnp.dot(act_columns, ada_low, preferred_element_type=high)
    modulation = lax.psum_scatter(partial_mod, "shard", scatter_dimension=0, tiled=True) + b_ada
    image_count = extra_images[0] + 1
    slot_ids = jnp.arange(MB)
    live_mask = (slot_ids < image_count).astype(low)
    tick_count = MB + 1
    received = jnp.zeros((LEN, model_width), low)
    inputs = []
    outputs = []
    for tick in range(tick_count):
        entering = jnp.where(section_index == 0, start[min(tick, MB - 1)], received)
        micro = jnp.clip(tick - section_index, 0, MB - 1)
        parts = layer_forward(entering.astype(high), modulation[micro], matrices, smalls, tables)
        leaving = parts["result"].astype(low)
        inputs.append(entering)
        outputs.append(leaving)
        if tick < MB:
            received = passed_along(leaving, "section", 1)
    section_out = (
        lax.dynamic_slice_in_dim(jnp.stack(outputs), section_index, MB, 0)
        * live_mask[:, None, None]
    )
    input_stack = jnp.stack(inputs)
    back_received = jnp.zeros((LEN, model_width), low)
    in_grads = []
    pieces = []
    mod_rows = []
    small_total = jnp.zeros((4 * model_width + 2 * HEAD_DIM,), high)
    for tick in range(tick_count):
        micro_raw = tick - 1 + section_index
        usable = ((micro_raw >= 0) & (micro_raw < MB) & (micro_raw < image_count)).astype(high)
        micro = jnp.clip(micro_raw, 0, MB - 1)
        source = jnp.clip(tick - 1 + 2 * section_index, 0, MB)
        own_grad = out_grad[min(tick, MB - 1)].astype(high)
        incoming = jnp.where(section_index == 1, own_grad, back_received.astype(high)) * usable
        parts = layer_forward(
            input_stack[source].astype(high), modulation[micro], matrices, smalls, tables
        )
        result = layer_backward(parts, incoming, matrices, smalls, tables)
        d_entering = result["d_entering"].astype(low)
        in_grads.append(d_entering)
        if tick < MB:
            back_received = passed_along(d_entering, "section", -1)
        mod_rows.append(result["d_mod"])
        small_total = small_total + result["d_small"]
        pieces.append(
            (
                (parts["in_attn"], result["d_qkv"]),
                (parts["mixed_low"], result["d_proj"]),
                (parts["in_ffn"], result["d_gu"]),
                (result["d_ffn"], parts["hid_low"]),
            )
        )
    is_first = section_index == 0

    def both_live(index, side):
        kept = [pieces[tick][index][side] for tick in range(tick_count)]
        return jnp.concatenate([jnp.where(is_first, kept[2], kept[0]), kept[1]], axis=0)

    left = jnp.stack(
        [both_live(index, 0).T.reshape(shards, rows, MB * LEN) for index in range(4)]
    )
    rights = [both_live(index, 1) for index in range(4)]
    d_mod = jnp.stack(
        [
            jnp.where(is_first, mod_rows[1], mod_rows[0]),
            jnp.where(is_first, mod_rows[2], mod_rows[1]),
        ]
    )
    packed = jnp.concatenate([d_mod.reshape(-1), act_low.reshape(-1), small_total.astype(low)])
    spread = lax.all_gather(packed, ("grp", "shard"))
    sum_low, row_squares, column_squares = reduce_grads(left, rights)
    mod_count = MB * 6 * model_width
    act_count = MB * model_width
    all_mod = spread[:, :mod_count].reshape(groups * shards * MB, 6 * model_width)
    every_act = spread[:, mod_count : mod_count + act_count]
    every_act = every_act.reshape(groups * shards * MB, model_width)
    small_sum = jnp.sum(spread[:, mod_count + act_count :].astype(high), axis=0)
    small_vector = jnp.concatenate(
        [
            small_sum[: 4 * model_width],
            jnp.sum(all_mod.astype(high), axis=0),
            small_sum[4 * model_width :],
        ]
    )
    small_rows = small_params.shape[1]
    small_grad = lax.dynamic_slice_in_dim(small_vector, shard_index * small_rows, small_rows, 0)
    grad_ada = lax.dot_general(
        lax.dynamic_slice_in_dim(every_act, shard_index * rows, rows, 1),
        all_mod,
        (((0,), (0,)), ((), ())),
        preferred_element_type=high,
    )
    group_mod = lax.dynamic_slice_in_dim(all_mod, group_index * shards * MB, shards * MB, 0)
    act_part = lax.all_gather(dot_back(group_mod, ada_low), ("section", "shard"))
    act_part = act_part.reshape(sections, shards, shards * MB, rows)
    act_part = jnp.sum(lax.dynamic_slice_in_dim(act_part, shard_index * MB, MB, 2), axis=0)
    act_grad = act_part.transpose(1, 0, 2).reshape(MB, model_width)
    sigma = jax.nn.sigmoid(condition)
    cond_term = act_grad * sigma * (1.0 + condition * (1.0 - sigma))
    cond_grad = lax.dynamic_slice_in_dim(
        cond_term, section_index * half_cond.shape[1], half_cond.shape[1], 1
    )
    section_in_grad = lax.dynamic_slice_in_dim(jnp.stack(in_grads), 1 - section_index, MB, 0)

    ada_square = grad_ada * grad_ada + TINY
    row_sums = jnp.sum(row_squares, axis=-1)
    wide = (widths[0], widths[1], widths[2], 6 * model_width, widths[3])
    row_means = [
        row_sums[0] / wide[0],
        row_sums[1] / wide[1],
        row_sums[2] / wide[2],
        jnp.sum(ada_square, axis=1) / wide[3],
        row_sums[3] / wide[4],
    ]
    feature_new = DECAY * feature_moments[0] + (1.0 - DECAY) * jnp.stack(row_means)
    column_flat = column_squares.reshape(-1)
    column_own = jnp.concatenate(
        [column_flat[: starts[3]], jnp.sum(ada_square, axis=0), column_flat[starts[3] :]]
    )
    column_all, feature_total = lax.psum((column_own, jnp.sum(feature_new, axis=1)), "shard")
    other_new = DECAY * other_moments[0] + (1.0 - DECAY) * column_all / model_width
    gradient = sum_low.astype(high)
    grads = [
        gradient[:, : starts[1]],
        gradient[:, starts[1] : starts[2]],
        gradient[:, starts[2] : starts[3]],
        grad_ada,
        gradient[:, starts[3] :],
    ]
    masters = (w_qkv[0], w_out[0], w_gu[0], w_ada[0], w_down[0].T)
    feature_scale = lax.rsqrt(feature_new / (feature_total / model_width)[:, None])
    other_scale = lax.rsqrt(other_new)
    new_wide = []
    lower = 0
    for index in range(5):
        upper = lower + wide[index]
        new_wide.append(
            masters[index]
            - RATE
            * grads[index]
            * feature_scale[index][:, None]
            * other_scale[None, lower:upper]
        )
        lower = upper
    small_new = DECAY * small_moment[0] + (1.0 - DECAY) * (small_grad * small_grad + TINY)
    new_small = small_params[0] - RATE_SMALL * small_grad * lax.rsqrt(small_new)
    return (
        section_out[None],
        section_in_grad[None],
        cond_grad,
        grads[0][None],
        grads[1][None],
        grads[2][None],
        grads[3][None],
        grads[4].T[None],
        small_grad[None],
        new_wide[0][None],
        new_wide[1][None],
        new_wide[2][None],
        new_wide[3][None],
        new_wide[4].T[None],
        new_small[None],
        feature_new[None],
        other_new[None],
        small_new[None],
    )


def solution(mesh):
    in_specs = (
        P(("grp", "shard"), None, None),
        P(("grp", "shard"), None, None),
        P(("grp", "shard")),
        P(("grp", "shard")),
        P(("grp", "shard")),
        P(None, "section"),
        P("section", "shard", None),
        P("section", "shard", None),
        P("section", "shard", None),
        P("section", "shard", None),
        P("section", None, "shard"),
        P("section", "shard"),
        P("section", None, "shard"),
        P("section", None),
        P("section", "shard"),
    )
    out_specs = (
        P("section", ("grp", "shard"), None, None),
        P("section", ("grp", "shard"), None, None),
        P(("grp", "shard"), "section"),
        P("section", "shard", None),
        P("section", "shard", None),
        P("section", "shard", None),
        P("section", "shard", None),
        P("section", None, "shard"),
        P("section", "shard"),
        P("section", "shard", None),
        P("section", "shard", None),
        P("section", "shard", None),
        P("section", "shard", None),
        P("section", None, "shard"),
        P("section", "shard"),
        P("section", None, "shard"),
        P("section", None),
        P("section", "shard"),
    )
    return jax.shard_map(body, mesh=mesh, in_specs=in_specs, out_specs=out_specs, check_vma=False)
```

```python
import functools

import jax
import jax.numpy as jnp
import numpy as np
from jax import lax
from jax.experimental import pallas as pl
from jax.experimental.pallas import tpu as pltpu
from jax.sharding import PartitionSpec as P

HEADS = 16
FF = 3072
GRID = 16
MB = 2
TIMESTEPS = 1000
HEAD_DIM = 72
LEN = 256


EPS = 1e-06
TINY = 1e-30
RATE = 0.04
RATE_SMALL = 0.05
DECAY = 0.5
CHUNK = 384
AHEAD = 3
LAG = 2
SLOTS = 4
MESH = pl.DeviceIdType.MESH
RING = 10
ROWS = 32
NT = (((1,), (1,)), ((), ()))
TN = (((0,), (0,)), ((), ()))
PAD = 128


def passed_along(block, axis, distance):
    devices = range(lax.axis_size(axis))
    route = [(i - distance, i) for i in devices if i - distance in devices]
    return lax.ppermute(block, axis, route)


def rope_tables(model_width):
    quarter = HEAD_DIM // 4
    tokens = np.arange(LEN)
    inverse = np.float32(10000.0) ** (-np.arange(quarter).astype(np.float32) / quarter)
    row_angle = (tokens // GRID).astype(np.float32)[:, None] * inverse[None, :]
    col_angle = (tokens % GRID).astype(np.float32)[:, None] * inverse[None, :]
    angles = np.concatenate([row_angle, row_angle, col_angle, col_angle], axis=1)
    lane = np.arange(HEAD_DIM) % (HEAD_DIM // 2)
    sines = np.sin(angles)
    first = np.where(lane < quarter, -sines, 0.0)
    second = np.where(lane >= quarter, sines, 0.0)
    count = model_width // HEAD_DIM
    return tuple(
        jnp.asarray(np.tile(table, (1, count)), jnp.float32)
        for table in (np.cos(angles), first, second)
    )


def head_members(model_width):
    owner = np.arange(model_width)[:, None] // HEAD_DIM
    return jnp.asarray(owner == np.arange(PAD)[None, :], jnp.bfloat16)


def dot_back(incoming, matrix):
    return mul(incoming, matrix, NT)


def place():
    return lax.axis_index("section"), lax.axis_index("grp"), lax.axis_index("shard")


def gather_kernel(chips, own_ref, all_ref, here_sem, sib_sem, x_sem, z_sem, f_sem):
    sec, grp, me = place()
    core = me % 2
    chip = me // 2
    half = grp % 2
    count = own_ref.shape[0] // 2
    sibling = (sec, grp, me ^ 1)
    across = (sec, grp ^ 1, me)

    barrier = pltpu.get_barrier_semaphore()
    pl.semaphore_signal(barrier, inc=1, device_id=sibling, device_id_type=MESH)
    pl.semaphore_signal(barrier, inc=1, device_id=across, device_id_type=MESH)
    for k in range(1, chips):
        pl.semaphore_signal(
            barrier, inc=1, device_id=(sec, grp, 2 * (chip ^ k) + core), device_id_type=MESH
        )
    pl.semaphore_wait(barrier, chips + 1)

    def chip_copy(k, step):
        piece = 2 * step + half
        return pltpu.make_async_remote_copy(
            src_ref=own_ref.at[piece],
            dst_ref=all_ref.at[piece, me],
            send_sem=x_sem.at[0, k - 1, step],
            recv_sem=x_sem.at[1, k - 1, step],
            device_id=(sec, grp, 2 * (chip ^ k) + core),
            device_id_type=MESH,
        )

    def chip_arrival(k, step):
        piece = 2 * step + half
        owner = 2 * (chip ^ k) + core
        return pltpu.make_async_remote_copy(
            src_ref=own_ref.at[piece],
            dst_ref=all_ref.at[piece, owner],
            send_sem=x_sem.at[0, k - 1, step],
            recv_sem=x_sem.at[1, k - 1, step],
            device_id=(sec, grp, owner),
            device_id_type=MESH,
        )

    def onward(k, step, side, sems, row, target):
        owner = 2 * (chip ^ k) + core
        region = all_ref.at[2 * step + side, owner]
        return pltpu.make_async_remote_copy(
            src_ref=region,
            dst_ref=region,
            send_sem=sems.at[0, row, step],
            recv_sem=sems.at[1, row, step],
            device_id=target,
            device_id_type=MESH,
        )

    def from_sibling(k, step, side, row):
        owner = 2 * (chip ^ k) + 1 - core
        region = all_ref.at[2 * step + side, owner]
        return pltpu.make_async_remote_copy(
            src_ref=region,
            dst_ref=region,
            send_sem=f_sem.at[0, row, step],
            recv_sem=f_sem.at[1, row, step],
            device_id=sibling,
            device_id_type=MESH,
        )

    def beside(step):
        pair = pl.ds(2 * step, 2)
        return pltpu.make_async_remote_copy(
            src_ref=own_ref.at[pair],
            dst_ref=all_ref.at[pair, me],
            send_sem=sib_sem.at[0, step],
            recv_sem=sib_sem.at[1, step],
            device_id=sibling,
            device_id_type=MESH,
        )

    def start_chip(step):
        for k in range(1, chips):
            chip_copy(k, step).start()

    for step in range(AHEAD):
        start_chip(step)
    here = pltpu.make_async_copy(own_ref, all_ref.at[:, me], here_sem)
    here.start()

    def relay(step, carry):
        @pl.when(step < count)
        def _():
            for k in range(1, chips):
                chip_arrival(k, step).wait_recv()
                onward(k, step, half, z_sem, k - 1, across).start()
                onward(k, step, half, f_sem, 2 * (k - 1), sibling).start()
                chip_copy(k, step).wait_send()
            beside(step).start()

        @pl.when(step + AHEAD < count)
        def _():
            start_chip(step + AHEAD)

        @pl.when(step >= LAG)
        def _():
            for k in range(1, chips):
                onward(k, step - LAG, 1 - half, z_sem, k - 1, across).wait_recv()
                onward(k, step - LAG, 1 - half, f_sem, 2 * (k - 1) + 1, sibling).start()
                onward(k, step - LAG, half, z_sem, k - 1, across).wait_send()

        return carry

    lax.fori_loop(0, count + LAG, relay, 0)

    def finish(step, carry):
        for k in range(1, chips):
            onward(k, step, half, f_sem, 2 * (k - 1), sibling).wait_send()
            onward(k, step, 1 - half, f_sem, 2 * (k - 1) + 1, sibling).wait_send()
            from_sibling(k, step, half, 2 * (k - 1)).wait_recv()
            from_sibling(k, step, 1 - half, 2 * (k - 1) + 1).wait_recv()
        beside(step).wait()
        return carry

    lax.fori_loop(0, count, finish, 0)
    here.wait()


def gather_rows(own):
    shards = lax.axis_size("shard")
    chips = shards // 2
    chunks, rows, width = own.shape
    count = chunks // 2
    return pl.pallas_call(
        functools.partial(gather_kernel, chips),
        out_shape=jax.ShapeDtypeStruct((chunks, shards, rows, width), own.dtype),
        in_specs=[pl.BlockSpec(memory_space=pltpu.VMEM)],
        out_specs=pl.BlockSpec(memory_space=pl.ANY),
        scratch_shapes=[
            pltpu.SemaphoreType.DMA,
            pltpu.SemaphoreType.DMA((2, count)),
            pltpu.SemaphoreType.DMA((2, chips - 1, count)),
            pltpu.SemaphoreType.DMA((2, chips - 1, count)),
            pltpu.SemaphoreType.DMA((2, 2 * (chips - 1), count)),
        ],
        compiler_params=pltpu.CompilerParams(
            collective_id=0, has_side_effects=True, vmem_limit_bytes=32 * 1024 * 1024
        ),
        cost_estimate=pl.CostEstimate(flops=0, bytes_accessed=300_000_000, transcendentals=0),
        name="gather_rows",
    )(own)


def reduce_kernel(shards, groups, firsts, *refs):
    matrices = len(firsts)
    left_refs = refs[:MB]
    right_refs = refs[MB : MB + MB * matrices]
    (
        sum_ref,
        rowsq_ref,
        colsq_ref,
        right_buf,
        send1,
        keep1,
        recv1,
        send2,
        recv2,
        keep2,
        keep3,
        send3,
        recv3,
        final,
        recv5,
        right_sem,
        sem1,
        sem2,
        sem3,
        sem5,
        out_sem,
    ) = refs[MB + MB * matrices :]
    chips = shards // 2
    total = sum_ref.shape[1] // CHUNK
    sec, grp, me = place()
    core = me % 2
    chip = me // 2
    middle = groups // 2
    lower = grp < middle
    depth = jnp.where(lower, middle - 1 - grp, grp - middle)
    inner = jnp.where(lower, grp + 1, grp - 1)
    outer = jnp.where(lower, grp - 1, grp + 1)
    has_outer = depth < middle - 1
    sibling = (sec, grp, me ^ 1)

    barrier = pltpu.get_barrier_semaphore()
    pl.semaphore_signal(barrier, inc=1, device_id=sibling, device_id_type=MESH)
    for k in range(1, chips):
        pl.semaphore_signal(
            barrier, inc=1, device_id=(sec, grp, 2 * (chip ^ k) + core), device_id_type=MESH
        )
    pl.semaphore_signal(barrier, inc=1, device_id=(sec, inner, me), device_id_type=MESH)

    @pl.when(has_outer)
    def _():
        pl.semaphore_signal(barrier, inc=1, device_id=(sec, outer, me), device_id_type=MESH)

    pl.semaphore_wait(barrier, chips + 1 + jnp.where(has_outer, 1, 0))

    def which(item):
        place_of = 0
        for first in firsts[1:]:
            place_of = place_of + jnp.where(item >= first, 1, 0)
        return place_of

    def right_copy(item, micro, matrix):
        slot = item % 3
        start = pl.multiple_of((item - firsts[matrix]) * CHUNK, CHUNK)
        return pltpu.make_async_copy(
            right_refs[micro * matrices + matrix].at[:, pl.ds(start, CHUNK)],
            right_buf.at[slot, micro],
            right_sem.at[slot, micro],
        )

    def fetch(item):
        for matrix in range(matrices):
            last = firsts[matrix + 1] if matrix + 1 < matrices else total

            @pl.when((item >= firsts[matrix]) & (item < last))
            def _():
                for micro in range(MB):
                    right_copy(item, micro, matrix).start()

    def arrived(item):
        for micro in range(MB):
            slot = item % 3
            pltpu.make_async_copy(
                right_refs[0].at[:, pl.ds(0, CHUNK)],
                right_buf.at[slot, micro],
                right_sem.at[slot, micro],
            ).wait()

    def copy1(item):
        slot = item % SLOTS
        return pltpu.make_async_remote_copy(
            src_ref=send1.at[slot],
            dst_ref=recv1.at[slot],
            send_sem=sem1.at[0, slot],
            recv_sem=sem1.at[1, slot],
            device_id=sibling,
            device_id_type=MESH,
        )

    def copy2(item, k):
        slot = item % SLOTS
        return pltpu.make_async_remote_copy(
            src_ref=send2.at[slot, k - 1],
            dst_ref=recv2.at[slot, k - 1],
            send_sem=sem2.at[0, slot, k - 1],
            recv_sem=sem2.at[1, slot, k - 1],
            device_id=(sec, grp, 2 * (chip ^ k) + core),
            device_id_type=MESH,
        )

    def copy3(item, kind):
        slot = item % SLOTS
        return pltpu.make_async_remote_copy(
            src_ref=send3.at[slot],
            dst_ref=recv3.at[kind, slot],
            send_sem=sem3.at[0, 0, slot],
            recv_sem=sem3.at[1, kind, slot],
            device_id=(sec, inner, me),
            device_id_type=MESH,
        )

    def copy5(item):
        slot = item % SLOTS
        return pltpu.make_async_remote_copy(
            src_ref=final.at[slot],
            dst_ref=recv5.at[slot],
            send_sem=sem5.at[0, slot],
            recv_sem=sem5.at[1, slot],
            device_id=(sec, outer, me),
            device_id_type=MESH,
        )

    def copy_out(item):
        slot = item % SLOTS
        start = pl.multiple_of(item * CHUNK, CHUNK)
        return pltpu.make_async_copy(
            final.at[slot], sum_ref.at[:, pl.ds(start, CHUNK)], out_sem.at[slot]
        )

    send_kind = jnp.where(depth == 0, 1, 0)
    lag3 = 2 + middle - 1 - depth
    lag5 = middle + 2 + depth
    rowsq_ref[...] = jnp.zeros_like(rowsq_ref)
    fetch(0)
    fetch(1)

    def step(tick, carry):
        item0 = tick

        @pl.when(item0 < total)
        def _():
            slot = item0 % SLOTS

            @pl.when(item0 >= SLOTS)
            def _():
                copy1(item0 - SLOTS).wait_send()

            @pl.when(item0 + 2 < total)
            def _():
                fetch(item0 + 2)

            arrived(item0)
            matrix = which(item0)

            def product(shard):
                value = 0.0
                for micro in range(MB):
                    value = value + jnp.dot(
                        left_refs[micro][matrix, shard],
                        right_buf[item0 % 3, micro],
                        preferred_element_type=jnp.float32,
                    )
                return value

            def multiply(k, carry):
                send1[slot, k] = product(2 * k + 1 - core).astype(jnp.bfloat16)
                keep1[item0 % 2, k] = product(2 * k + core)
                return carry

            lax.fori_loop(0, chips, multiply, 0)
            copy1(item0).start()

        item1 = tick - 1

        @pl.when((item1 >= 0) & (item1 < total))
        def _():
            slot = item1 % SLOTS
            copy1(item1).wait_recv()

            @pl.when(item1 >= SLOTS)
            def _():
                for k in range(1, chips):
                    copy2(item1 - SLOTS, k).wait_send()

            for k in range(1, chips):
                other = chip ^ k
                send2[slot, k - 1] = (
                    keep1[item1 % 2, other] + recv1[slot, other].astype(jnp.float32)
                ).astype(jnp.bfloat16)
                copy2(item1, k).start()
            keep2[item1 % 2] = keep1[item1 % 2, chip] + recv1[slot, chip].astype(jnp.float32)

        item2 = tick - 2

        @pl.when((item2 >= 0) & (item2 < total))
        def _():
            slot = item2 % SLOTS
            value = keep2[item2 % 2]
            for k in range(1, chips):
                copy2(item2, k).wait_recv()
                value = value + recv2[slot, k - 1].astype(jnp.float32)
            keep3[item2 % (middle + 1)] = value

        item3 = tick - lag3

        @pl.when((item3 >= 0) & (item3 < total))
        def _():
            slot = item3 % SLOTS

            @pl.when(item3 >= SLOTS)
            def _():
                copy3(item3 - SLOTS, send_kind).wait_send()

            @pl.when(has_outer)
            def _():
                copy3(item3, 0).wait_recv()
                send3[slot] = (
                    keep3[item3 % (middle + 1)] + recv3[0, slot].astype(jnp.float32)
                ).astype(jnp.bfloat16)

            @pl.when(jnp.logical_not(has_outer))
            def _():
                send3[slot] = keep3[item3 % (middle + 1)].astype(jnp.bfloat16)

            copy3(item3, send_kind).start()

        item5 = tick - lag5

        @pl.when((item5 >= 0) & (item5 < total))
        def _():
            slot = item5 % SLOTS

            @pl.when(item5 >= SLOTS)
            def _():
                copy_out(item5 - SLOTS).wait()

                @pl.when(has_outer)
                def _():
                    copy5(item5 - SLOTS).wait_send()

            @pl.when(depth == 0)
            def _():
                copy3(item5, 1).wait_recv()
                final[slot] = (
                    send3[slot].astype(jnp.float32) + recv3[1, slot].astype(jnp.float32)
                ).astype(jnp.bfloat16)

            @pl.when(depth > 0)
            def _():
                copy5(item5).wait_recv()
                final[slot] = recv5[slot]

            @pl.when(has_outer)
            def _():
                copy5(item5).start()

            copy_out(item5).start()
            value = final[slot].astype(jnp.float32)
            square = value * value + TINY
            folded = square[:, :128]
            for start in range(128, CHUNK, 128):
                folded = folded + square[:, start : start + 128]
            matrix = which(item5)
            rowsq_ref[matrix] = rowsq_ref[matrix] + folded
            colsq_ref[item5] = jnp.sum(square, axis=0, keepdims=True)

        return carry

    lax.fori_loop(0, total + groups + 1, step, 0)

    def drain(offset, carry):
        item = total - SLOTS + offset
        copy1(item).wait_send()
        for k in range(1, chips):
            copy2(item, k).wait_send()
        copy3(item, send_kind).wait_send()
        copy_out(item).wait()

        @pl.when(has_outer)
        def _():
            copy5(item).wait_send()

        return carry

    lax.fori_loop(0, SLOTS, drain, 0)


def reduce_grads(lefts, rights):
    shards = lax.axis_size("shard")
    groups = lax.axis_size("grp")
    chips = shards // 2
    middle = groups // 2
    matrices, _, rows, tokens = lefts[0].shape
    widths = [right.shape[1] for right in rights[0]]
    width = sum(widths)
    firsts = [sum(widths[:index]) // CHUNK for index in range(matrices)]
    low, high = jnp.bfloat16, jnp.float32
    block = (rows, CHUNK)
    return pl.pallas_call(
        functools.partial(reduce_kernel, shards, groups, firsts),
        out_shape=(
            jax.ShapeDtypeStruct((rows, width), low),
            jax.ShapeDtypeStruct((matrices, rows, 128), high),
            jax.ShapeDtypeStruct((width // CHUNK, 1, CHUNK), high),
        ),
        in_specs=[pl.BlockSpec(memory_space=pltpu.VMEM)] * MB
        + [pl.BlockSpec(memory_space=pl.ANY)] * (MB * matrices),
        out_specs=(
            pl.BlockSpec(memory_space=pl.ANY),
            pl.BlockSpec(memory_space=pltpu.VMEM),
            pl.BlockSpec(memory_space=pltpu.VMEM),
        ),
        scratch_shapes=[
            pltpu.VMEM((3, MB, tokens, CHUNK), low),
            pltpu.VMEM((SLOTS, chips) + block, low),
            pltpu.VMEM((2, chips) + block, high),
            pltpu.VMEM((SLOTS, chips) + block, low),
            pltpu.VMEM((SLOTS, chips - 1) + block, low),
            pltpu.VMEM((SLOTS, chips - 1) + block, low),
            pltpu.VMEM((2,) + block, high),
            pltpu.VMEM((middle + 1,) + block, high),
            pltpu.VMEM((SLOTS,) + block, low),
            pltpu.VMEM((2, SLOTS) + block, low),
            pltpu.VMEM((SLOTS,) + block, low),
            pltpu.VMEM((SLOTS,) + block, low),
            pltpu.SemaphoreType.DMA((3, MB)),
            pltpu.SemaphoreType.DMA((2, SLOTS)),
            pltpu.SemaphoreType.DMA((2, SLOTS, chips - 1)),
            pltpu.SemaphoreType.DMA((2, 2, SLOTS)),
            pltpu.SemaphoreType.DMA((2, SLOTS)),
            pltpu.SemaphoreType.DMA((SLOTS,)),
        ],
        compiler_params=pltpu.CompilerParams(
            collective_id=1, has_side_effects=True, vmem_limit_bytes=48 * 1024 * 1024
        ),
        cost_estimate=pl.CostEstimate(flops=0, bytes_accessed=600_000_000, transcendentals=0),
        name="reduce_grads",
    )(*lefts, *[right for group in rights for right in group])


def mul(left, right, form=(((1,), (0,)), ((), ()))):
    return lax.dot_general(left, right, form, preferred_element_type=jnp.float32)


def halves(value):
    upper = value.astype(jnp.bfloat16)
    return upper, (value - upper.astype(jnp.float32)).astype(jnp.bfloat16)


def mul_split(value, right, form=(((1,), (0,)), ((), ()))):
    upper, lower = halves(value)
    return mul(upper, right, form) + mul(lower, right, form)


def by_rows(work, init=0, size=ROWS):
    def step(index, carry):
        return work(pl.ds(pl.multiple_of(index * size, size), size), carry)

    return lax.fori_loop(0, LEN // size, step, init)


def aligned(start, size):
    return pl.ds(pl.multiple_of(start, 128), size)


def rms_rate(value):
    return lax.rsqrt(jnp.mean(value * value, axis=-1, keepdims=True) + EPS)


def turn(value, cosines, first, second):
    width = value.shape[1]
    quarter = HEAD_DIM // 4
    ahead = pltpu.roll(value, width - quarter, 1)
    behind = pltpu.roll(value, quarter, 1)
    return value * cosines, ahead * first + behind * second


def window(head, model_width):
    tile = jnp.minimum(head * HEAD_DIM // 128, model_width // 128 - 2)
    lane = lax.broadcasted_iota(jnp.int32, (1, 256), 1) + tile * 128 - head * HEAD_DIM
    mask = ((lane >= 0) & (lane < HEAD_DIM)).astype(jnp.bfloat16)
    return aligned(tile * 128, 256), mask


def ring_of(weights, ring, sems, order, count):
    def copy(item):
        slot = item % RING
        return pltpu.make_async_copy(weights.at[order(item)], ring.at[slot], sems.at[slot])

    def begin():
        for item in range(RING):
            copy(item).start()

    def ready(item):
        copy(item).wait()
        return item % RING

    def release(item):
        @pl.when(item + RING < count)
        def _():
            copy(item + RING).start()

    return begin, ready, release


def forward_kernel(
    active,
    live,
    x_ref,
    weights,
    mod_ref,
    bias_ref,
    gain_ref,
    cos_ref,
    first_ref,
    second_ref,
    member_ref,
    *rest,
    aliased,
):
    rest = rest[aliased:]
    out_ref, leave_ref, left_out, hid_out, low_out, prob_out, high_out, gu_out = rest[:8]
    (
        ring,
        a_buf,
        qkv,
        low_buf,
        prob,
        high_buf,
        gu_buf,
        hid,
        left,
        acc,
        out_buf,
        leave_buf,
        ring_sem,
        out_sem,
    ) = rest[8:]
    model_width = x_ref.shape[1]
    low, high = jnp.bfloat16, jnp.float32
    heads = model_width // HEAD_DIM
    chunks = weights.shape[0]
    wide = CHUNK

    @pl.when(active[0] == 1)
    def _():
        begin, ready, release = ring_of(weights, ring, ring_sem, lambda item: item, chunks)
        begin()
        copies = []

        def send(source, target):
            copy = pltpu.make_async_copy(source, target, out_sem.at[len(copies)])
            copy.start()
            copies.append(copy)

        shift1, scale1, gate1 = mod_ref[0:1], mod_ref[1:2], mod_ref[2:3]
        shift2, scale2, gate2 = mod_ref[3:4], mod_ref[4:5], mod_ref[5:6]

        def enter(rows, carry):
            x = x_ref[rows].astype(high)
            a_buf[rows] = (x * rms_rate(x) * (1.0 + scale1) + shift1).astype(low)
            return carry

        by_rows(enter)

        def project(item, carry):
            slot = ready(item)
            cols = aligned(item * wide, wide)
            qkv[:, cols] = mul(a_buf[...], ring[slot]) + bias_ref[:, cols]
            release(item)
            return carry

        qkv_chunks = 3 * model_width // wide
        lax.fori_loop(0, qkv_chunks, project, 0)
        left[0] = a_buf[...].T
        send(left.at[0], left_out.at[0])

        member = member_ref[...]
        for index in range(2):
            base = index * model_width
            cols = slice(base, base + model_width)
            raw = qkv[:, cols]
            rate = lax.rsqrt(mul_split(raw * raw, member) * (1.0 / HEAD_DIM) + EPS)
            acc[...] = mul_split(rate, member, NT)

            def turned(rows, carry):
                unit = qkv[rows, cols] * acc[rows]
                high_buf[rows, cols] = unit
                gained = unit * gain_ref[index : index + 1]
                straight, crossed = turn(gained, cos_ref[rows], first_ref[rows], second_ref[rows])
                low_buf[rows, cols] = (straight + crossed).astype(low)
                return carry

            by_rows(turned)
            high_buf[:, 5 * model_width + index * PAD : 5 * model_width + (index + 1) * PAD] = rate

        low_buf[:, 2 * model_width :] = qkv[:, 2 * model_width :].astype(low)
        send(low_buf, low_out)
        acc[...] = jnp.zeros_like(acc)

        def attend(head, carry):
            cols, mask = window(head, model_width)
            tile = cols.start
            q = low_buf[:, cols] * mask
            k = low_buf[:, aligned(model_width + tile, 256)]
            v = low_buf[:, aligned(2 * model_width + tile, 256)] * mask
            scores = mul(k, q, NT) * HEAD_DIM ** (-0.5)
            weight = jnp.exp(scores - jnp.max(scores, axis=0, keepdims=True))
            share = (weight * (1.0 / jnp.sum(weight, axis=0, keepdims=True))).astype(low)
            prob[head] = share
            acc[:, cols] = acc[:, cols] + mul(share, v, TN)
            return carry

        lax.fori_loop(0, heads, attend, 0, unroll=2)
        send(prob, prob_out)
        a_buf[...] = acc[...].astype(low)
        left[1] = a_buf[...].T
        send(left.at[1], left_out.at[1])

        out_chunks = model_width // wide

        def mix(index, carry):
            item = qkv_chunks + index
            slot = ready(item)
            cols = aligned(index * wide, wide)
            acc[:, cols] = mul(a_buf[...], ring[slot]) + bias_ref[
                :, aligned(3 * model_width + index * wide, wide)
            ]
            release(item)
            return carry

        lax.fori_loop(0, out_chunks, mix, 0)

        proj_cols = slice(2 * model_width, 3 * model_width)
        middle_cols = slice(3 * model_width, 4 * model_width)
        ffn_cols = slice(4 * model_width, 5 * model_width)

        def between(rows, carry):
            proj = acc[rows]
            high_buf[rows, proj_cols] = proj
            middle = x_ref[rows].astype(high) + gate1 * proj
            high_buf[rows, middle_cols] = middle
            a_buf[rows] = (middle * rms_rate(middle) * (1.0 + scale2) + shift2).astype(low)
            return carry

        by_rows(between)
        left[2] = a_buf[...].T
        send(left.at[2], left_out.at[2])

        gate_chunks = FF // wide

        def widen(index, carry):
            item = qkv_chunks + out_chunks + 2 * index
            cols = aligned(index * wide, wide)
            slot = ready(item)
            gate = mul(a_buf[...], ring[slot])
            release(item)
            slot = ready(item + 1)
            up = mul(a_buf[...], ring[slot])
            release(item + 1)
            gu_buf[:, cols] = gate
            gu_buf[:, aligned(FF + index * wide, wide)] = up
            hid[:, cols] = (gate * (1.0 / (1.0 + jnp.exp(-gate))) * up).astype(low)
            return carry

        lax.fori_loop(0, gate_chunks, widen, 0)
        send(gu_buf, gu_out)
        send(hid, hid_out)
        acc[...] = jnp.zeros_like(acc)

        def narrow(index, carry):
            item = qkv_chunks + out_chunks + 2 * gate_chunks + index
            slot = ready(item)
            acc[...] += mul(hid[:, aligned(index * wide, wide)], ring[slot], NT)
            release(item)
            return carry

        lax.fori_loop(0, gate_chunks, narrow, 0)

        def leave(rows, carry):
            ffn = acc[rows]
            high_buf[rows, ffn_cols] = ffn
            result = high_buf[rows, middle_cols] + gate2 * ffn
            leave_buf[rows] = result.astype(low)
            out_buf[rows] = (result * live[0]).astype(low)
            return carry

        by_rows(leave)
        send(leave_buf, leave_ref)
        send(out_buf, out_ref)
        send(high_buf, high_out)
        for copy in copies:
            copy.wait()


def layer_shapes(model_width):
    low, high = jnp.bfloat16, jnp.float32
    return [
        ((LEN, model_width), low),
        ((LEN, model_width), low),
        ((4, model_width, LEN), low),
        ((LEN, FF), low),
        ((LEN, 3 * model_width), low),
        ((HEADS, LEN, LEN), low),
        ((LEN, 5 * model_width + 2 * PAD), high),
        ((LEN, 2 * FF), high),
    ]


def run_forward(active, live, x, weights, mod, bias, gain, tables, member, kept):
    model_width = x.shape[1]
    low, high = jnp.bfloat16, jnp.float32
    shapes = layer_shapes(model_width)
    flag = pl.BlockSpec(memory_space=pltpu.SMEM)
    near = pl.BlockSpec(memory_space=pltpu.VMEM)
    far = pl.BlockSpec(memory_space=pl.ANY)
    kept = [] if kept is None else list(kept)
    return pl.pallas_call(
        functools.partial(forward_kernel, aliased=len(kept)),
        out_shape=[jax.ShapeDtypeStruct(shape, kind) for shape, kind in shapes],
        in_specs=[flag, flag, near, far] + [near] * 7 + [far] * len(kept),
        out_specs=[far] * len(shapes),
        input_output_aliases={11 + index: index for index in range(len(kept))},
        scratch_shapes=[
            pltpu.VMEM((RING, model_width, CHUNK), low),
            pltpu.VMEM((LEN, model_width), low),
            pltpu.VMEM((LEN, 3 * model_width), high),
            pltpu.VMEM((LEN, 3 * model_width), low),
            pltpu.VMEM((HEADS, LEN, LEN), low),
            pltpu.VMEM((LEN, 5 * model_width + 2 * PAD), high),
            pltpu.VMEM((LEN, 2 * FF), high),
            pltpu.VMEM((LEN, FF), low),
            pltpu.VMEM((3, model_width, LEN), low),
            pltpu.VMEM((LEN, model_width), high),
            pltpu.VMEM((LEN, model_width), low),
            pltpu.VMEM((LEN, model_width), low),
            pltpu.SemaphoreType.DMA((RING,)),
            pltpu.SemaphoreType.DMA((10,)),
        ],
        compiler_params=pltpu.CompilerParams(vmem_limit_bytes=56 * 1024 * 1024),
        cost_estimate=pl.CostEstimate(flops=0, bytes_accessed=80_000_000, transcendentals=0),
        name="layer_forward",
    )(active, live, x, weights, mod, bias, gain, *tables, member, *kept)


def backward_kernel(
    active,
    live,
    dy_ref,
    x_ref,
    weights,
    mod_ref,
    gain_ref,
    cos_ref,
    first_ref,
    second_ref,
    member_ref,
    low_in,
    prob_in,
    high_in,
    gu_in,
    *rest,
    aliased,
):
    rest = rest[aliased:]
    dx_out, left_out, dqkv_out, dproj_out, dgu_out, dmod_out, sums_out = rest[:7]
    (
        ring,
        dy,
        low_buf,
        prob,
        high_buf,
        gu_buf,
        dgu,
        dqkv,
        small,
        left,
        acc,
        middle_grad,
        mixed_grad,
        turned_q,
        turned_k,
        turned_v,
        dmod,
        sums,
        ring_sem,
        in_sem,
        out_sem,
    ) = rest[7:]
    model_width = x_ref.shape[1]
    low, high = jnp.bfloat16, jnp.float32
    heads = model_width // HEAD_DIM
    chunks = weights.shape[0]
    wide = CHUNK
    qkv_chunks = 3 * model_width // wide
    out_chunks = model_width // wide
    gate_chunks = FF // wide
    base = qkv_chunks + out_chunks

    def order(item):
        index = item // 3
        kind = item % 3
        ffn_item = jnp.where(
            kind == 0, base + 2 * gate_chunks + index, base + 2 * index + kind - 1
        )
        late = item - 3 * gate_chunks
        other = jnp.where(late < out_chunks, qkv_chunks + late, late - out_chunks)
        return jnp.where(late < 0, ffn_item, other)

    @pl.when(active[0] == 1)
    def _():
        begin, ready, release = ring_of(weights, ring, ring_sem, order, chunks)
        loads = [
            pltpu.make_async_copy(source, target, in_sem.at[index])
            for index, (source, target) in enumerate(
                ((high_in, high_buf), (gu_in, gu_buf), (low_in, low_buf), (prob_in, prob))
            )
        ]
        loads[0].start()
        loads[1].start()
        begin()
        loads[2].start()
        loads[3].start()
        copies = []

        def send(source, target):
            copy = pltpu.make_async_copy(source, target, out_sem.at[len(copies)])
            copy.start()
            copies.append(copy)

        scale1, gate1 = mod_ref[1:2], mod_ref[2:3]
        scale2, gate2 = mod_ref[4:5], mod_ref[5:6]
        proj_cols = slice(2 * model_width, 3 * model_width)
        middle_cols = slice(3 * model_width, 4 * model_width)
        ffn_cols = slice(4 * model_width, 5 * model_width)
        nothing = jnp.zeros((1, model_width), high)

        def total(value):
            return jnp.sum(value, axis=0, keepdims=True)

        loads[0].wait()

        def enter(rows, gate_sum):
            incoming = dy_ref[rows].astype(high) * live[0]
            dy[rows] = incoming
            small[rows] = (gate2 * incoming).astype(low)
            return gate_sum + total(incoming * high_buf[rows, ffn_cols])

        dmod[5:6] = by_rows(enter, nothing)
        left[...] = small[...].T
        send(left, left_out.at[3])
        acc[...] = jnp.zeros_like(acc)
        loads[1].wait()

        def ffn_back(index, carry):
            item = 3 * index
            slot = ready(item)
            d_hid = mul(small[...], ring[slot])
            release(item)
            cols = aligned(index * wide, wide)
            cols_up = aligned(FF + index * wide, wide)
            gate = gu_buf[:, cols]
            sigma = 1.0 / (1.0 + jnp.exp(-gate))
            gated = gate * sigma
            d_gate = (d_hid * gu_buf[:, cols_up] * (sigma + gated * (1.0 - sigma))).astype(low)
            d_up = (d_hid * gated).astype(low)
            dgu[:, cols] = d_gate
            dgu[:, cols_up] = d_up
            slot = ready(item + 1)
            part = mul(d_gate, ring[slot], NT)
            release(item + 1)
            slot = ready(item + 2)
            acc[...] += part + mul(d_up, ring[slot], NT)
            release(item + 2)
            return carry

        lax.fori_loop(0, gate_chunks, ffn_back, 0)
        send(dgu, dgu_out)

        def between(rows, carry):
            scale_sum, shift_sum, gate_sum = carry
            middle = high_buf[rows, middle_cols]
            rate = rms_rate(middle)
            unit = middle * rate
            back = acc[rows]
            d_unit = back * (1.0 + scale2)
            grad = dy[rows] + rate * (
                d_unit - unit * jnp.mean(d_unit * unit, axis=-1, keepdims=True)
            )
            middle_grad[rows] = grad
            d_proj = (gate1 * grad).astype(low)
            small[rows] = d_proj
            return (
                scale_sum + total(back * unit),
                shift_sum + total(back),
                gate_sum + total(grad * high_buf[rows, proj_cols]),
            )

        scale_sum, shift_sum, gate_sum = by_rows(between, (nothing,) * 3)
        dmod[4:5] = scale_sum
        dmod[3:4] = shift_sum
        dmod[2:3] = gate_sum
        send(small, dproj_out)

        def proj_sum(rows, carry):
            return carry + total(small[rows].astype(high))

        sums[3:4] = by_rows(proj_sum, nothing)
        acc[...] = jnp.zeros_like(acc)

        def mixed_back(index, carry):
            item = 3 * gate_chunks + index
            slot = ready(item)
            acc[...] += mul(small[:, aligned(index * wide, wide)], ring[slot], NT)
            release(item)
            return carry

        lax.fori_loop(0, out_chunks, mixed_back, 0)
        mixed_grad[...] = acc[...].astype(low)
        loads[2].wait()
        loads[3].wait()
        for buffer in (turned_q, turned_k, turned_v):
            buffer[...] = jnp.zeros_like(buffer)

        def attend_back(head, carry):
            cols, mask = window(head, model_width)
            tile = cols.start
            q = low_buf[:, cols] * mask
            k = low_buf[:, aligned(model_width + tile, 256)] * mask
            v = low_buf[:, aligned(2 * model_width + tile, 256)]
            d_mixed = mixed_grad[:, cols] * mask
            share = prob[head]
            d_share = mul(v, d_mixed, NT)
            wide_share = share.astype(high)
            product = wide_share * d_share
            d_score = (product - wide_share * jnp.sum(product, axis=0, keepdims=True)).astype(low)
            turned_v[:, cols] = turned_v[:, cols] + mul(share, d_mixed)
            turned_k[:, cols] = turned_k[:, cols] + mul(d_score, q)
            turned_q[:, cols] = turned_q[:, cols] + mul(d_score, k, TN)
            return carry

        lax.fori_loop(0, heads, attend_back, 0, unroll=2)
        member = member_ref[...]
        for index, turned in enumerate((turned_q, turned_k)):
            cols = slice(index * model_width, (index + 1) * model_width)

            def unturn(rows, gain_sum):
                straight, crossed = turn(
                    turned[rows] * HEAD_DIM ** (-0.5),
                    cos_ref[rows],
                    first_ref[rows],
                    second_ref[rows],
                )
                d_norm = straight - crossed
                unit = high_buf[rows, cols]
                d_unit = d_norm * gain_ref[index : index + 1]
                turned[rows] = d_unit
                acc[rows] = d_unit * unit
                return gain_sum + total(d_norm * unit)

            sums[4 + index : 5 + index] = by_rows(unturn, nothing)
            level = mul_split(acc[...], member) * (1.0 / HEAD_DIM)
            rate = high_buf[:, 5 * model_width + index * PAD : 5 * model_width + (index + 1) * PAD]
            acc[...] = mul_split(rate * level, member, NT)
            dy[...] = mul_split(rate, member, NT)

            def unscale(rows, carry):
                d_raw = dy[rows] * turned[rows] - high_buf[rows, cols] * acc[rows]
                d_low = d_raw.astype(low)
                dqkv[rows, cols] = d_low
                return carry + total(d_low.astype(high))

            sums[index : index + 1] = by_rows(unscale, nothing)

        def values(rows, carry):
            d_low = turned_v[rows].astype(low)
            dqkv[rows, 2 * model_width :] = d_low
            return carry + total(d_low.astype(high))

        sums[2:3] = by_rows(values, nothing)
        send(dqkv, dqkv_out)
        acc[...] = jnp.zeros_like(acc)

        def project_back(index, carry):
            item = 3 * gate_chunks + out_chunks + index
            slot = ready(item)
            acc[...] += mul(dqkv[:, aligned(index * wide, wide)], ring[slot], NT)
            release(item)
            return carry

        lax.fori_loop(0, qkv_chunks, project_back, 0)

        def leave(rows, carry):
            scale_sum, shift_sum = carry
            x = x_ref[rows].astype(high)
            rate = rms_rate(x)
            unit = x * rate
            back = acc[rows]
            d_unit = back * (1.0 + scale1)
            grad = middle_grad[rows] + rate * (
                d_unit - unit * jnp.mean(d_unit * unit, axis=-1, keepdims=True)
            )
            mixed_grad[rows] = grad.astype(low)
            return scale_sum + total(back * unit), shift_sum + total(back)

        scale_sum, shift_sum = by_rows(leave, (nothing,) * 2)
        dmod[1:2] = scale_sum
        dmod[0:1] = shift_sum
        send(mixed_grad, dx_out)
        send(dmod, dmod_out)
        send(sums, sums_out)
        for copy in copies:
            copy.wait()


def run_backward(active, live, dy, x, weights, mod, gain, tables, member, parts, left, kept):
    model_width = x.shape[1]
    low, high = jnp.bfloat16, jnp.float32
    shapes = [
        ((LEN, model_width), low),
        ((4, model_width, LEN), low),
        ((LEN, 3 * model_width), low),
        ((LEN, model_width), low),
        ((LEN, 2 * FF), low),
        ((8, model_width), high),
        ((8, model_width), high),
    ]
    flag = pl.BlockSpec(memory_space=pltpu.SMEM)
    near = pl.BlockSpec(memory_space=pltpu.VMEM)
    far = pl.BlockSpec(memory_space=pl.ANY)
    if kept is None:
        extra, aliases = [left], {15: 1}
    else:
        extra = list(kept)
        aliases = {15 + index: index for index in range(len(extra))}
    return pl.pallas_call(
        functools.partial(backward_kernel, aliased=len(extra)),
        out_shape=[jax.ShapeDtypeStruct(shape, kind) for shape, kind in shapes],
        in_specs=[flag, flag, near, near, far] + [near] * 6 + [far] * (4 + len(extra)),
        out_specs=[far] * len(shapes),
        input_output_aliases=aliases,
        scratch_shapes=[
            pltpu.VMEM((RING, model_width, CHUNK), low),
            pltpu.VMEM((LEN, model_width), high),
            pltpu.VMEM((LEN, 3 * model_width), low),
            pltpu.VMEM((HEADS, LEN, LEN), low),
            pltpu.VMEM((LEN, 5 * model_width + 2 * PAD), high),
            pltpu.VMEM((LEN, 2 * FF), high),
            pltpu.VMEM((LEN, 2 * FF), low),
            pltpu.VMEM((LEN, 3 * model_width), low),
            pltpu.VMEM((LEN, model_width), low),
            pltpu.VMEM((model_width, LEN), low),
            pltpu.VMEM((LEN, model_width), high),
            pltpu.VMEM((LEN, model_width), high),
            pltpu.VMEM((LEN, model_width), low),
            pltpu.VMEM((LEN, model_width), high),
            pltpu.VMEM((LEN, model_width), high),
            pltpu.VMEM((LEN, model_width), high),
            pltpu.VMEM((8, model_width), high),
            pltpu.VMEM((8, model_width), high),
            pltpu.SemaphoreType.DMA((RING,)),
            pltpu.SemaphoreType.DMA((4,)),
            pltpu.SemaphoreType.DMA((10,)),
        ],
        compiler_params=pltpu.CompilerParams(vmem_limit_bytes=56 * 1024 * 1024),
        cost_estimate=pl.CostEstimate(flops=0, bytes_accessed=120_000_000, transcendentals=0),
        name="layer_backward",
    )(active, live, dy, x, weights, mod, gain, *tables, member, *parts, *extra)


def body(
    start,
    out_grad,
    extra_images,
    timesteps,
    labels,
    embed_table,
    w_qkv,
    w_out,
    w_gu,
    w_ada,
    w_down,
    small_params,
    feature_moments,
    other_moments,
    small_moment,
):
    model_width = start.shape[-1]
    section_index = lax.axis_index("section")
    shard_index = lax.axis_index("shard")
    group_index = lax.axis_index("grp")
    sections = lax.axis_size("section")
    shards = lax.axis_size("shard")
    groups = lax.axis_size("grp")
    rows = w_qkv.shape[1]
    low = jnp.bfloat16
    high = jnp.float32
    widths = (3 * model_width, model_width, 2 * FF, FF)
    starts = (0, widths[0], widths[0] + widths[1], widths[0] + widths[1] + widths[2])
    gate_up = w_gu[0].reshape(rows, 2, FF // CHUNK, CHUNK).transpose(0, 2, 1, 3)
    own = jnp.concatenate(
        [w_qkv[0], w_out[0], gate_up.reshape(rows, 2 * FF), w_down[0].T], axis=1
    ).astype(low)
    own = own.reshape(rows, sum(widths) // CHUNK, CHUNK).transpose(1, 0, 2)
    weights = gather_rows(own).reshape(own.shape[0], model_width, CHUNK)
    ada_low = w_ada[0].astype(low)
    small_all = lax.all_gather(small_params[0].astype(low), "shard", axis=0, tiled=True)
    small_all = small_all.astype(high)
    bias = small_all[None, : 4 * model_width]
    b_ada = small_all[4 * model_width : 10 * model_width]
    gain = jnp.tile(small_all[10 * model_width :].reshape(2, HEAD_DIM), (1, HEADS))
    tables = rope_tables(model_width)
    member = head_members(model_width)
    half_cond = embed_table[timesteps] + embed_table[TIMESTEPS + labels]
    cond_all = lax.all_gather(half_cond, ("section", "shard"))
    cond_all = cond_all.reshape(sections, shards * MB, half_cond.shape[1])
    cond_all = cond_all.transpose(1, 0, 2).reshape(shards * MB, model_width)
    act_all = jax.nn.silu(cond_all).astype(low)
    condition = lax.dynamic_slice_in_dim(cond_all, shard_index * MB, MB, 0)
    act_low = lax.dynamic_slice_in_dim(act_all, shard_index * MB, MB, 0)
    act_columns = lax.dynamic_slice_in_dim(act_all, shard_index * rows, rows, 1)
    partial_mod = jnp.dot(act_columns, ada_low, preferred_element_type=high)
    modulation = lax.psum_scatter(partial_mod, "shard", scatter_dimension=0, tiled=True) + b_ada
    image_count = extra_images[0] + 1
    live = [(jnp.full((1,), micro) < image_count).astype(high) for micro in range(MB)]
    here = [jnp.full((1,), section_index == index, jnp.int32) for index in range(2)]
    mods = [modulation[micro].reshape(6, model_width) for micro in range(MB)]
    fixed = (gain, tables, member)
    kept = []
    received = []
    for micro in range(MB):
        result = run_forward(
            here[0], live[micro], start[micro], weights, mods[micro], bias, *fixed, None
        )
        kept.append(result)
        received.append(passed_along(result[1], "section", 1))
    for micro in range(MB):
        kept[micro] = run_forward(
            here[1], live[micro], received[micro], weights, mods[micro], bias, *fixed, kept[micro]
        )
    section_out = jnp.stack([result[0] for result in kept])
    grads_kept = []
    returned = []
    for micro in range(MB):
        result = run_backward(
            here[1],
            live[micro],
            out_grad[micro],
            received[micro],
            weights,
            mods[micro],
            *fixed,
            kept[micro][4:],
            kept[micro][2],
            None,
        )
        grads_kept.append(result)
        returned.append(passed_along(result[0], "section", -1))
    for micro in range(MB):
        grads_kept[micro] = run_backward(
            here[0],
            live[micro],
            returned[micro],
            start[micro],
            weights,
            mods[micro],
            *fixed,
            kept[micro][4:],
            None,
            grads_kept[micro],
        )
    section_in_grad = jnp.stack([result[0] for result in grads_kept])
    lefts = [result[1].reshape(4, shards, rows, LEN) for result in grads_kept]
    rights = [
        [result[2], result[3], result[4], kept[micro][3]]
        for micro, result in enumerate(grads_kept)
    ]
    d_mod = jnp.stack([result[5][:6].reshape(-1) for result in grads_kept]).astype(low)
    sums = sum(result[6] for result in grads_kept)
    small_total = jnp.concatenate(
        [sums[:4].reshape(-1), jnp.sum(sums[4:6].reshape(2, HEADS, HEAD_DIM), axis=1).reshape(-1)]
    )
    packed = jnp.concatenate([d_mod.reshape(-1), act_low.reshape(-1), small_total.astype(low)])
    spread = lax.all_gather(packed, ("grp", "shard"))
    sum_low, row_squares, column_squares = reduce_grads(lefts, rights)
    mod_count = MB * 6 * model_width
    act_count = MB * model_width
    all_mod = spread[:, :mod_count].reshape(groups * shards * MB, 6 * model_width)
    every_act = spread[:, mod_count : mod_count + act_count]
    every_act = every_act.reshape(groups * shards * MB, model_width)
    small_sum = jnp.sum(spread[:, mod_count + act_count :].astype(high), axis=0)
    small_vector = jnp.concatenate(
        [
            small_sum[: 4 * model_width],
            jnp.sum(all_mod.astype(high), axis=0),
            small_sum[4 * model_width :],
        ]
    )
    small_rows = small_params.shape[1]
    small_grad = lax.dynamic_slice_in_dim(small_vector, shard_index * small_rows, small_rows, 0)
    grad_ada = lax.dot_general(
        lax.dynamic_slice_in_dim(every_act, shard_index * rows, rows, 1),
        all_mod,
        (((0,), (0,)), ((), ())),
        preferred_element_type=high,
    )
    group_mod = lax.dynamic_slice_in_dim(all_mod, group_index * shards * MB, shards * MB, 0)
    act_part = lax.all_gather(dot_back(group_mod, ada_low), ("section", "shard"))
    act_part = act_part.reshape(sections, shards, shards * MB, rows)
    act_part = jnp.sum(lax.dynamic_slice_in_dim(act_part, shard_index * MB, MB, 2), axis=0)
    act_grad = act_part.transpose(1, 0, 2).reshape(MB, model_width)
    sigma = jax.nn.sigmoid(condition)
    cond_term = act_grad * sigma * (1.0 + condition * (1.0 - sigma))
    cond_grad = lax.dynamic_slice_in_dim(
        cond_term, section_index * half_cond.shape[1], half_cond.shape[1], 1
    )

    ada_square = grad_ada * grad_ada + TINY
    row_sums = jnp.sum(row_squares, axis=-1)
    wide = (widths[0], widths[1], widths[2], 6 * model_width, widths[3])
    row_means = [
        row_sums[0] / wide[0],
        row_sums[1] / wide[1],
        row_sums[2] / wide[2],
        jnp.sum(ada_square, axis=1) / wide[3],
        row_sums[3] / wide[4],
    ]
    feature_new = DECAY * feature_moments[0] + (1.0 - DECAY) * jnp.stack(row_means)
    column_flat = column_squares.reshape(-1)
    column_own = jnp.concatenate(
        [column_flat[: starts[3]], jnp.sum(ada_square, axis=0), column_flat[starts[3] :]]
    )
    column_all, feature_total = lax.psum((column_own, jnp.sum(feature_new, axis=1)), "shard")
    other_new = DECAY * other_moments[0] + (1.0 - DECAY) * column_all / model_width
    gradient = sum_low.astype(high)
    grads = [
        gradient[:, : starts[1]],
        gradient[:, starts[1] : starts[2]],
        gradient[:, starts[2] : starts[3]],
        grad_ada,
        gradient[:, starts[3] :],
    ]
    masters = (w_qkv[0], w_out[0], w_gu[0], w_ada[0], w_down[0].T)
    feature_scale = lax.rsqrt(feature_new / (feature_total / model_width)[:, None])
    other_scale = lax.rsqrt(other_new)
    new_wide = []
    lower = 0
    for index in range(5):
        upper = lower + wide[index]
        new_wide.append(
            masters[index]
            - RATE
            * grads[index]
            * feature_scale[index][:, None]
            * other_scale[None, lower:upper]
        )
        lower = upper
    small_new = DECAY * small_moment[0] + (1.0 - DECAY) * (small_grad * small_grad + TINY)
    new_small = small_params[0] - RATE_SMALL * small_grad * lax.rsqrt(small_new)
    return (
        section_out[None],
        section_in_grad[None],
        cond_grad,
        grads[0][None],
        grads[1][None],
        grads[2][None],
        grads[3][None],
        grads[4].T[None],
        small_grad[None],
        new_wide[0][None],
        new_wide[1][None],
        new_wide[2][None],
        new_wide[3][None],
        new_wide[4].T[None],
        new_small[None],
        feature_new[None],
        other_new[None],
        small_new[None],
    )


def solution(mesh):
    in_specs = (
        P(("grp", "shard"), None, None),
        P(("grp", "shard"), None, None),
        P(("grp", "shard")),
        P(("grp", "shard")),
        P(("grp", "shard")),
        P(None, "section"),
        P("section", "shard", None),
        P("section", "shard", None),
        P("section", "shard", None),
        P("section", "shard", None),
        P("section", None, "shard"),
        P("section", "shard"),
        P("section", None, "shard"),
        P("section", None),
        P("section", "shard"),
    )
    out_specs = (
        P("section", ("grp", "shard"), None, None),
        P("section", ("grp", "shard"), None, None),
        P(("grp", "shard"), "section"),
        P("section", "shard", None),
        P("section", "shard", None),
        P("section", "shard", None),
        P("section", "shard", None),
        P("section", None, "shard"),
        P("section", "shard"),
        P("section", "shard", None),
        P("section", "shard", None),
        P("section", "shard", None),
        P("section", "shard", None),
        P("section", None, "shard"),
        P("section", "shard"),
        P("section", None, "shard"),
        P("section", None),
        P("section", "shard"),
    )
    return jax.shard_map(body, mesh=mesh, in_specs=in_specs, out_specs=out_specs, check_vma=False)
```

```python
import functools

import jax
import jax.numpy as jnp
import numpy as np
from jax import lax
from jax.experimental import pallas as pl
from jax.experimental.pallas import tpu as pltpu
from jax.sharding import PartitionSpec as P

HEADS = 16
FF = 3072
GRID = 16
MB = 2
TIMESTEPS = 1000
HEAD_DIM = 72
LEN = 256


EPS = 1e-06
TINY = 1e-30
RATE = 0.04
RATE_SMALL = 0.05
DECAY = 0.5
CHUNK = 384
AHEAD = 3
LAG = 2
SLOTS = 6
HOP = 2
MESH = pl.DeviceIdType.MESH
RING = 10
ROWS = 32
NT = (((1,), (1,)), ((), ()))
TN = (((0,), (0,)), ((), ()))
PAD = 128


def passed_along(block, axis, distance):
    devices = range(lax.axis_size(axis))
    route = [(i - distance, i) for i in devices if i - distance in devices]
    return lax.ppermute(block, axis, route)


def rope_tables(model_width):
    quarter = HEAD_DIM // 4
    tokens = np.arange(LEN)
    inverse = np.float32(10000.0) ** (-np.arange(quarter).astype(np.float32) / quarter)
    row_angle = (tokens // GRID).astype(np.float32)[:, None] * inverse[None, :]
    col_angle = (tokens % GRID).astype(np.float32)[:, None] * inverse[None, :]
    angles = np.concatenate([row_angle, row_angle, col_angle, col_angle], axis=1)
    lane = np.arange(HEAD_DIM) % (HEAD_DIM // 2)
    sines = np.sin(angles)
    first = np.where(lane < quarter, -sines, 0.0)
    second = np.where(lane >= quarter, sines, 0.0)
    count = model_width // HEAD_DIM
    return tuple(
        jnp.asarray(np.tile(table, (1, count)), jnp.float32)
        for table in (np.cos(angles), first, second)
    )


def head_members(model_width):
    owner = np.arange(model_width)[:, None] // HEAD_DIM
    return jnp.asarray(owner == np.arange(PAD)[None, :], jnp.bfloat16)


def dot_back(incoming, matrix):
    return mul(incoming, matrix, NT)


def place():
    return lax.axis_index("section"), lax.axis_index("grp"), lax.axis_index("shard")


def gather_kernel(chips, own_ref, all_ref, here_sem, sib_sem, x_sem, z_sem, f_sem):
    sec, grp, me = place()
    core = me % 2
    chip = me // 2
    half = grp % 2
    count = own_ref.shape[0] // 2
    sibling = (sec, grp, me ^ 1)
    across = (sec, grp ^ 1, me)

    barrier = pltpu.get_barrier_semaphore()
    pl.semaphore_signal(barrier, inc=1, device_id=sibling, device_id_type=MESH)
    pl.semaphore_signal(barrier, inc=1, device_id=across, device_id_type=MESH)
    for k in range(1, chips):
        pl.semaphore_signal(
            barrier, inc=1, device_id=(sec, grp, 2 * (chip ^ k) + core), device_id_type=MESH
        )
    pl.semaphore_wait(barrier, chips + 1)

    def chip_copy(k, step):
        piece = 2 * step + half
        return pltpu.make_async_remote_copy(
            src_ref=own_ref.at[piece],
            dst_ref=all_ref.at[piece, me],
            send_sem=x_sem.at[0, k - 1, step],
            recv_sem=x_sem.at[1, k - 1, step],
            device_id=(sec, grp, 2 * (chip ^ k) + core),
            device_id_type=MESH,
        )

    def chip_arrival(k, step):
        piece = 2 * step + half
        owner = 2 * (chip ^ k) + core
        return pltpu.make_async_remote_copy(
            src_ref=own_ref.at[piece],
            dst_ref=all_ref.at[piece, owner],
            send_sem=x_sem.at[0, k - 1, step],
            recv_sem=x_sem.at[1, k - 1, step],
            device_id=(sec, grp, owner),
            device_id_type=MESH,
        )

    def onward(k, step, side, sems, row, target):
        owner = 2 * (chip ^ k) + core
        region = all_ref.at[2 * step + side, owner]
        return pltpu.make_async_remote_copy(
            src_ref=region,
            dst_ref=region,
            send_sem=sems.at[0, row, step],
            recv_sem=sems.at[1, row, step],
            device_id=target,
            device_id_type=MESH,
        )

    def from_sibling(k, step, side, row):
        owner = 2 * (chip ^ k) + 1 - core
        region = all_ref.at[2 * step + side, owner]
        return pltpu.make_async_remote_copy(
            src_ref=region,
            dst_ref=region,
            send_sem=f_sem.at[0, row, step],
            recv_sem=f_sem.at[1, row, step],
            device_id=sibling,
            device_id_type=MESH,
        )

    def beside(step):
        pair = pl.ds(2 * step, 2)
        return pltpu.make_async_remote_copy(
            src_ref=own_ref.at[pair],
            dst_ref=all_ref.at[pair, me],
            send_sem=sib_sem.at[0, step],
            recv_sem=sib_sem.at[1, step],
            device_id=sibling,
            device_id_type=MESH,
        )

    def start_chip(step):
        for k in range(1, chips):
            chip_copy(k, step).start()

    for step in range(AHEAD):
        start_chip(step)
    here = pltpu.make_async_copy(own_ref, all_ref.at[:, me], here_sem)
    here.start()

    def relay(step, carry):
        @pl.when(step < count)
        def _():
            for k in range(1, chips):
                chip_arrival(k, step).wait_recv()
                onward(k, step, half, z_sem, k - 1, across).start()
                onward(k, step, half, f_sem, 2 * (k - 1), sibling).start()
                chip_copy(k, step).wait_send()
            beside(step).start()

        @pl.when(step + AHEAD < count)
        def _():
            start_chip(step + AHEAD)

        @pl.when(step >= LAG)
        def _():
            for k in range(1, chips):
                onward(k, step - LAG, 1 - half, z_sem, k - 1, across).wait_recv()
                onward(k, step - LAG, 1 - half, f_sem, 2 * (k - 1) + 1, sibling).start()
                onward(k, step - LAG, half, z_sem, k - 1, across).wait_send()

        return carry

    lax.fori_loop(0, count + LAG, relay, 0)

    def finish(step, carry):
        for k in range(1, chips):
            onward(k, step, half, f_sem, 2 * (k - 1), sibling).wait_send()
            onward(k, step, 1 - half, f_sem, 2 * (k - 1) + 1, sibling).wait_send()
            from_sibling(k, step, half, 2 * (k - 1)).wait_recv()
            from_sibling(k, step, 1 - half, 2 * (k - 1) + 1).wait_recv()
        beside(step).wait()
        return carry

    lax.fori_loop(0, count, finish, 0)
    here.wait()


def gather_rows(own):
    shards = lax.axis_size("shard")
    chips = shards // 2
    chunks, rows, width = own.shape
    count = chunks // 2
    return pl.pallas_call(
        functools.partial(gather_kernel, chips),
        out_shape=jax.ShapeDtypeStruct((chunks, shards, rows, width), own.dtype),
        in_specs=[pl.BlockSpec(memory_space=pltpu.VMEM)],
        out_specs=pl.BlockSpec(memory_space=pl.ANY),
        scratch_shapes=[
            pltpu.SemaphoreType.DMA,
            pltpu.SemaphoreType.DMA((2, count)),
            pltpu.SemaphoreType.DMA((2, chips - 1, count)),
            pltpu.SemaphoreType.DMA((2, chips - 1, count)),
            pltpu.SemaphoreType.DMA((2, 2 * (chips - 1), count)),
        ],
        compiler_params=pltpu.CompilerParams(
            collective_id=0, has_side_effects=True, vmem_limit_bytes=32 * 1024 * 1024
        ),
        cost_estimate=pl.CostEstimate(flops=0, bytes_accessed=300_000_000, transcendentals=0),
        name="gather_rows",
    )(own)


def reduce_kernel(shards, groups, firsts, pieces, *refs):
    matrices = len(firsts)
    left_refs, refs = refs[:MB], refs[MB:]
    right_refs, refs = refs[: MB * matrices], refs[MB * matrices :]
    pack_ref, act_ref, ada_ref, tail_ref, refs = *refs[:4], refs[4:]
    sum_refs, refs = refs[:matrices], refs[matrices:]
    (
        rowsq_ref,
        stats_ref,
        total_ref,
        mods_ref,
        acts_ref,
        cond_ref,
        right_buf,
        send1,
        keep1,
        recv1,
        send2,
        recv2,
        keep2,
        keep3,
        send3,
        recv3,
        final,
        recv5,
        spread,
        mods,
        part,
        part_in,
        stats,
        stats_in,
        stats_all,
        right_sem,
        sem1,
        sem2,
        sem3,
        sem5,
        out_sem,
        chip_sem,
        line_sem,
        swap_sem,
        cond_sem,
        stat_sem,
    ) = refs
    chips = shards // 2
    ends = 2 * groups
    rows = rowsq_ref.shape[1]
    bounds = list(firsts) + [sum(ref.shape[1] for ref in sum_refs) // CHUNK]
    total = bounds[-1]
    model_width = mods.shape[2]
    per_group = acts_ref.shape[1]
    low, high = jnp.bfloat16, jnp.float32
    sec, grp, me = place()
    core = me % 2
    chip = me // 2
    middle = groups // 2
    lower = grp < middle
    depth = jnp.where(lower, middle - 1 - grp, grp - middle)
    inner = jnp.where(lower, grp + 1, grp - 1)
    outer = jnp.where(lower, grp - 1, grp + 1)
    has_outer = depth < middle - 1
    sibling = (sec, grp, me ^ 1)
    across = (1 - sec, grp, me)

    def chip_peer(k):
        return (sec, grp, 2 * (chip ^ k) + core)

    barrier = pltpu.get_barrier_semaphore()
    pl.semaphore_signal(barrier, inc=1, device_id=sibling, device_id_type=MESH)
    pl.semaphore_signal(barrier, inc=1, device_id=across, device_id_type=MESH)
    for k in range(1, chips):
        pl.semaphore_signal(barrier, inc=1, device_id=chip_peer(k), device_id_type=MESH)
    pl.semaphore_signal(barrier, inc=1, device_id=(sec, inner, me), device_id_type=MESH)

    @pl.when(has_outer)
    def _():
        pl.semaphore_signal(barrier, inc=1, device_id=(sec, outer, me), device_id_type=MESH)

    pl.semaphore_wait(barrier, chips + 2 + jnp.where(has_outer, 1, 0))

    def which(item):
        matrix = 0
        for first in firsts[1:]:
            matrix = matrix + jnp.where(item >= first, 1, 0)
        return matrix

    def in_matrix(item, matrix):
        return (item >= bounds[matrix]) & (item < bounds[matrix + 1])

    def columns(item, matrix):
        return pl.ds(pl.multiple_of((item - firsts[matrix]) * CHUNK, CHUNK), CHUNK)

    def fetch(item):
        slot = item % 3
        for matrix in range(matrices):

            @pl.when(in_matrix(item, matrix))
            def _():
                for micro in range(MB):
                    pltpu.make_async_copy(
                        right_refs[micro * matrices + matrix].at[:, columns(item, matrix)],
                        right_buf.at[slot, micro],
                        right_sem.at[slot, micro],
                    ).start()

    def arrived(item):
        for micro in range(MB):
            slot = item % 3
            pltpu.make_async_copy(
                right_refs[0].at[:, pl.ds(0, CHUNK)],
                right_buf.at[slot, micro],
                right_sem.at[slot, micro],
            ).wait()

    def remote(source, target, sems, device):
        return pltpu.make_async_remote_copy(
            src_ref=source,
            dst_ref=target,
            send_sem=sems[0],
            recv_sem=sems[1],
            device_id=device,
            device_id_type=MESH,
        )

    def copy1(item):
        slot = item % SLOTS
        sems = (sem1.at[0, slot], sem1.at[1, slot])
        return remote(send1.at[slot], recv1.at[slot], sems, sibling)

    def copy2(item, k):
        slot = item % SLOTS
        sems = (sem2.at[0, slot, k - 1], sem2.at[1, slot, k - 1])
        return remote(send2.at[slot, k - 1], recv2.at[slot, k - 1], sems, chip_peer(k))

    def copy3(item, kind):
        slot = item % SLOTS
        sems = (sem3.at[0, 0, slot], sem3.at[1, kind, slot])
        return remote(send3.at[slot], recv3.at[kind, slot], sems, (sec, inner, me))

    def copy5(item):
        slot = item % ends
        sems = (sem5.at[0, slot], sem5.at[1, slot])
        return remote(final.at[slot], recv5.at[slot], sems, (sec, outer, me))

    def start_out(item):
        slot = item % ends
        for matrix in range(matrices):

            @pl.when(in_matrix(item, matrix))
            def _():
                pltpu.make_async_copy(
                    final.at[slot], sum_refs[matrix].at[:, columns(item, matrix)], out_sem.at[slot]
                ).start()

    def wait_out(item):
        slot = item % ends
        pltpu.make_async_copy(
            final.at[slot], sum_refs[0].at[:, pl.ds(0, CHUNK)], out_sem.at[slot]
        ).wait()

    def chip_spread(k, owner):
        region = spread.at[core, grp, owner]
        sems = (chip_sem.at[0, k - 1], chip_sem.at[1, k - 1])
        return remote(region, region, sems, chip_peer(k))

    def line_spread(side, step, row):
        target = (sec, grp + 1 - 2 * side, me)
        region = spread.at[core, row]
        second = acts_ref.at[row]
        return (
            remote(
                region, region, (line_sem.at[0, side, step, 0], line_sem.at[1, side, step, 0]), target
            ),
            remote(
                second, second, (line_sem.at[0, side, step, 1], line_sem.at[1, side, step, 1]), target
            ),
        )

    def swap_spread(which_core):
        region = spread.at[which_core]
        return remote(region, region, (swap_sem.at[0], swap_sem.at[1]), sibling)

    def cond_across():
        return remote(part, part_in, (cond_sem.at[0, 0], cond_sem.at[1, 0]), across)

    def cond_beside(owner):
        region = cond_ref.at[owner]
        return remote(region, region, (cond_sem.at[0, 1], cond_sem.at[1, 1]), sibling)

    def cond_chip(k, owner):
        region = cond_ref.at[pl.ds(2 * owner, 2)]
        sems = (cond_sem.at[0, 1 + k], cond_sem.at[1, 1 + k])
        return remote(region, region, sems, chip_peer(k))

    def exists(side):
        return (grp < groups - 1) if side == 0 else (grp > 0)

    swap_tick = 2 + 2 * groups
    piece_tick = swap_tick + 2
    cond_tick = piece_tick + pieces

    def beside_the_sum(tick):
        @pl.when(tick == 2)
        def _():
            for k in range(1, chips):
                chip_spread(k, chip ^ k).wait_recv()
            for side in range(2):

                @pl.when(exists(side))
                def _():
                    for copy in line_spread(side, 0, grp):
                        copy.start()

        for step in range(1, groups):

            @pl.when(tick == 2 + 2 * step)
            def _():
                for side in range(2):
                    row = grp - step if side == 0 else grp + step
                    came = (row >= 0) if side == 0 else (row < groups)

                    @pl.when(came)
                    def _():
                        for copy in line_spread(side, step - 1, row):
                            copy.wait_recv()

                    @pl.when(came & exists(side))
                    def _():
                        for copy in line_spread(side, step, row):
                            copy.start()

        @pl.when(tick == swap_tick)
        def _():
            swap_spread(core).start()

        @pl.when(tick == piece_tick)
        def _():
            swap_spread(1 - core).wait_recv()
            mods[...] = jnp.zeros_like(mods)
            total_ref[...] = jnp.zeros_like(total_ref)

            def unpack(index, carry):
                origin = index // (groups * chips)
                row = (index // chips) % groups
                owner = index % chips
                block = spread[origin, row, owner].astype(high)
                total_ref[...] = total_ref[...] + block
                first = row * per_group + (2 * owner + origin) * MB
                for micro in range(MB):
                    for piece in range(pieces):
                        line = micro * pieces + piece
                        mods[piece, pl.ds(first + micro, 1), :] = block[
                            line : line + 1, :model_width
                        ]
                return carry

            lax.fori_loop(0, 2 * groups * chips, unpack, 0)
            part[...] = jnp.zeros_like(part)
            rowsq_ref[matrices] = jnp.zeros_like(rowsq_ref[matrices])

        for piece in range(pieces):

            @pl.when(tick == piece_tick + piece)
            def _():
                every = acts_ref[...].reshape(groups * per_group, acts_ref.shape[2])
                mod = mods[piece].astype(low)
                mods_ref[piece] = mod
                value = mul(every, mod, TN)[:rows]
                square = value * value + TINY
                folded = square[:, :128]
                for start in range(128, model_width, 128):
                    folded = folded + square[:, start : start + 128]
                rowsq_ref[matrices] = rowsq_ref[matrices] + folded
                sums = jnp.sum(square, axis=0, keepdims=True)
                split = model_width // CHUNK
                for index in range(split):
                    line = total + piece * split + index
                    stats[line : line + 1] = sums[:, index * CHUNK : (index + 1) * CHUNK]
                mine = mods[piece, pl.ds(pl.multiple_of(grp * per_group, 8), per_group), :]
                back = mul(
                    mine.astype(low), ada_ref[:, piece * model_width : (piece + 1) * model_width], NT
                )
                part[:, :rows] = part[:, :rows] + back

        @pl.when(tick == cond_tick)
        def _():
            cond_across().start()

        @pl.when(tick == cond_tick + 2)
        def _():
            cond_across().wait_recv()
            cond_ref[me] = part[...] + part_in[...]
            cond_beside(me).start()

        @pl.when(tick == cond_tick + 4)
        def _():
            cond_beside(me ^ 1).wait_recv()
            for k in range(1, chips):
                cond_chip(k, chip).start()

        @pl.when(tick == cond_tick + 6)
        def _():
            for k in range(1, chips):
                cond_chip(k, chip ^ k).wait_recv()

    def beside_the_sum_sent():
        for k in range(1, chips):
            chip_spread(k, chip).wait_send()
            cond_chip(k, chip).wait_send()
        for side in range(2):
            for step in range(groups - 1):
                row = grp - step if side == 0 else grp + step
                came = (row >= 0) if side == 0 else (row < groups)

                @pl.when(came & exists(side))
                def _():
                    for copy in line_spread(side, step, row):
                        copy.wait_send()

        swap_spread(core).wait_send()
        cond_across().wait_send()
        cond_beside(me).wait_send()

    send_kind = jnp.where(depth == 0, 1, 0)
    lag3 = 1 + HOP * (middle - depth)
    lag5 = 1 + HOP * (middle + 1 + depth)
    held = HOP * (middle - 1) + 1
    rowsq_ref[...] = jnp.zeros_like(rowsq_ref)
    stats[...] = jnp.zeros_like(stats)
    stats[stats.shape[0] - 1 :] = tail_ref[...]
    spread[core, grp, chip] = pack_ref[...]
    acts_ref[grp] = act_ref[...]
    for k in range(1, chips):
        chip_spread(k, chip).start()
    fetch(0)
    fetch(1)

    def step(tick, carry):
        item0 = tick

        @pl.when(item0 < total)
        def _():
            slot = item0 % SLOTS

            @pl.when(item0 >= SLOTS)
            def _():
                copy1(item0 - SLOTS).wait_send()

            @pl.when(item0 + 2 < total)
            def _():
                fetch(item0 + 2)

            arrived(item0)
            matrix = which(item0)

            def product(shard):
                value = 0.0
                for micro in range(MB):
                    value = value + jnp.dot(
                        left_refs[micro][matrix, shard],
                        right_buf[item0 % 3, micro],
                        preferred_element_type=high,
                    )
                return value

            def multiply(k, carry):
                send1[slot, k] = product(2 * k + 1 - core).astype(low)
                keep1[item0 % 2, k] = product(2 * k + core)
                return carry

            lax.fori_loop(0, chips, multiply, 0)
            copy1(item0).start()

        item1 = tick - 1

        @pl.when((item1 >= 0) & (item1 < total))
        def _():
            slot = item1 % SLOTS
            copy1(item1).wait_recv()

            @pl.when(item1 >= SLOTS)
            def _():
                for k in range(1, chips):
                    copy2(item1 - SLOTS, k).wait_send()

            for k in range(1, chips):
                other = chip ^ k
                send2[slot, k - 1] = (
                    keep1[item1 % 2, other] + recv1[slot, other].astype(high)
                ).astype(low)
                copy2(item1, k).start()
            keep2[item1 % (HOP + 1)] = keep1[item1 % 2, chip] + recv1[slot, chip].astype(high)

        item2 = tick - 1 - HOP

        @pl.when((item2 >= 0) & (item2 < total))
        def _():
            slot = item2 % SLOTS
            value = keep2[item2 % (HOP + 1)]
            for k in range(1, chips):
                copy2(item2, k).wait_recv()
                value = value + recv2[slot, k - 1].astype(high)
            keep3[item2 % held] = value

        item3 = tick - lag3

        @pl.when((item3 >= 0) & (item3 < total))
        def _():
            slot = item3 % SLOTS

            @pl.when(item3 >= SLOTS)
            def _():
                copy3(item3 - SLOTS, send_kind).wait_send()

            @pl.when(has_outer)
            def _():
                copy3(item3, 0).wait_recv()
                send3[slot] = (keep3[item3 % held] + recv3[0, slot].astype(high)).astype(low)

            @pl.when(jnp.logical_not(has_outer))
            def _():
                send3[slot] = keep3[item3 % held].astype(low)

            copy3(item3, send_kind).start()

        item5 = tick - lag5

        @pl.when((item5 >= 0) & (item5 < total))
        def _():
            slot = item5 % ends
            other = item5 % SLOTS

            @pl.when(item5 >= ends)
            def _():
                wait_out(item5 - ends)

                @pl.when(has_outer)
                def _():
                    copy5(item5 - ends).wait_send()

            @pl.when(depth == 0)
            def _():
                copy3(item5, 1).wait_recv()
                final[slot] = (send3[other].astype(high) + recv3[1, other].astype(high)).astype(low)

            @pl.when(depth > 0)
            def _():
                copy5(item5).wait_recv()
                final[slot] = recv5[slot]

            @pl.when(has_outer)
            def _():
                copy5(item5).start()

            start_out(item5)
            value = final[slot].astype(high)
            square = value * value + TINY
            folded = square[:, :128]
            for start in range(128, CHUNK, 128):
                folded = folded + square[:, start : start + 128]
            matrix = which(item5)
            rowsq_ref[matrix] = rowsq_ref[matrix] + folded
            stats[pl.ds(item5, 1), :] = jnp.sum(square, axis=0, keepdims=True)

        beside_the_sum(tick)
        return carry

    lax.fori_loop(0, total + 1 + 2 * HOP * middle, step, 0)

    beside = remote(stats, stats_in, (stat_sem.at[0, 0], stat_sem.at[1, 0]), sibling)
    beside.start()
    beside.wait_recv()
    stats_all[chip] = stats[...] + stats_in[...]

    def stat_chip(k, owner):
        region = stats_all.at[owner]
        return remote(region, region, (stat_sem.at[0, k], stat_sem.at[1, k]), chip_peer(k))

    for k in range(1, chips):
        stat_chip(k, chip).start()
    for k in range(1, chips):
        stat_chip(k, chip ^ k).wait_recv()
    value = stats_all[0]
    for owner in range(1, chips):
        value = value + stats_all[owner]
    stats_ref[...] = value

    def drain(offset, carry):
        item = total - SLOTS + offset
        copy1(item).wait_send()
        for k in range(1, chips):
            copy2(item, k).wait_send()
        copy3(item, send_kind).wait_send()
        return carry

    lax.fori_loop(0, SLOTS, drain, 0)

    def drain_out(offset, carry):
        item = total - ends + offset
        wait_out(item)

        @pl.when(has_outer)
        def _():
            copy5(item).wait_send()

        return carry

    lax.fori_loop(0, ends, drain_out, 0)
    beside_the_sum_sent()
    beside.wait_send()
    for k in range(1, chips):
        stat_chip(k, chip).wait_send()


def reduce_grads(lefts, rights, packed, act, ada, tail):
    shards = lax.axis_size("shard")
    groups = lax.axis_size("grp")
    chips = shards // 2
    middle = groups // 2
    ends = 2 * groups
    matrices, _, rows, tokens = lefts[0].shape
    widths = [right.shape[1] for right in rights[0]]
    firsts = [sum(widths[:index]) // CHUNK for index in range(matrices)]
    model_width = shards * rows
    pieces = ada.shape[1] // model_width
    lines = sum(widths) // CHUNK + ada.shape[1] // CHUNK + 1
    low, high = jnp.bfloat16, jnp.float32
    block = (rows, CHUNK)
    near = pl.BlockSpec(memory_space=pltpu.VMEM)
    far = pl.BlockSpec(memory_space=pl.ANY)
    every = groups * act.shape[0]
    return pl.pallas_call(
        functools.partial(reduce_kernel, shards, groups, firsts, pieces),
        out_shape=[jax.ShapeDtypeStruct((rows, width), low) for width in widths]
        + [
            jax.ShapeDtypeStruct((matrices + 1, rows, 128), high),
            jax.ShapeDtypeStruct((lines, CHUNK), high),
            jax.ShapeDtypeStruct(packed.shape, high),
            jax.ShapeDtypeStruct((pieces, every, model_width), low),
            jax.ShapeDtypeStruct((groups,) + act.shape, low),
            jax.ShapeDtypeStruct((shards,) + act.shape, high),
        ],
        in_specs=[near] * MB + [far] * (MB * matrices) + [near] * 4,
        out_specs=[far] * matrices + [near] * 6,
        scratch_shapes=[
            pltpu.VMEM((3, MB, tokens, CHUNK), low),
            pltpu.VMEM((SLOTS, chips) + block, low),
            pltpu.VMEM((2, chips) + block, high),
            pltpu.VMEM((SLOTS, chips) + block, low),
            pltpu.VMEM((SLOTS, chips - 1) + block, low),
            pltpu.VMEM((SLOTS, chips - 1) + block, low),
            pltpu.VMEM((HOP + 1,) + block, high),
            pltpu.VMEM((HOP * (middle - 1) + 1,) + block, high),
            pltpu.VMEM((SLOTS,) + block, low),
            pltpu.VMEM((2, SLOTS) + block, low),
            pltpu.VMEM((ends,) + block, low),
            pltpu.VMEM((ends,) + block, low),
            pltpu.VMEM((2, groups, chips) + packed.shape, low),
            pltpu.VMEM((pieces, every, model_width), high),
            pltpu.VMEM(act.shape, high),
            pltpu.VMEM(act.shape, high),
            pltpu.VMEM((lines, CHUNK), high),
            pltpu.VMEM((lines, CHUNK), high),
            pltpu.VMEM((chips, lines, CHUNK), high),
            pltpu.SemaphoreType.DMA((3, MB)),
            pltpu.SemaphoreType.DMA((2, SLOTS)),
            pltpu.SemaphoreType.DMA((2, SLOTS, chips - 1)),
            pltpu.SemaphoreType.DMA((2, 2, SLOTS)),
            pltpu.SemaphoreType.DMA((2, ends)),
            pltpu.SemaphoreType.DMA((ends,)),
            pltpu.SemaphoreType.DMA((2, chips - 1)),
            pltpu.SemaphoreType.DMA((2, 2, groups, 2)),
            pltpu.SemaphoreType.DMA((2,)),
            pltpu.SemaphoreType.DMA((2, chips + 1)),
            pltpu.SemaphoreType.DMA((2, chips)),
        ],
        compiler_params=pltpu.CompilerParams(
            collective_id=1, has_side_effects=True, vmem_limit_bytes=56 * 1024 * 1024
        ),
        cost_estimate=pl.CostEstimate(flops=0, bytes_accessed=600_000_000, transcendentals=0),
        name="reduce_grads",
    )(*lefts, *[right for group in rights for right in group], packed, act, ada, tail)


def mul(left, right, form=(((1,), (0,)), ((), ()))):
    return lax.dot_general(left, right, form, preferred_element_type=jnp.float32)


def halves(value):
    upper = value.astype(jnp.bfloat16)
    return upper, (value - upper.astype(jnp.float32)).astype(jnp.bfloat16)


def mul_split(value, right, form=(((1,), (0,)), ((), ()))):
    upper, lower = halves(value)
    return mul(upper, right, form) + mul(lower, right, form)


def by_rows(work, init=0, size=ROWS):
    def step(index, carry):
        return work(pl.ds(pl.multiple_of(index * size, size), size), carry)

    return lax.fori_loop(0, LEN // size, step, init)


def aligned(start, size):
    return pl.ds(pl.multiple_of(start, 128), size)


def rms_rate(value):
    return lax.rsqrt(jnp.mean(value * value, axis=-1, keepdims=True) + EPS)


def turn(value, cosines, first, second):
    width = value.shape[1]
    quarter = HEAD_DIM // 4
    ahead = pltpu.roll(value, width - quarter, 1)
    behind = pltpu.roll(value, quarter, 1)
    return value * cosines, ahead * first + behind * second


def window(head, model_width):
    tile = jnp.minimum(head * HEAD_DIM // 128, model_width // 128 - 2)
    lane = lax.broadcasted_iota(jnp.int32, (1, 256), 1) + tile * 128 - head * HEAD_DIM
    mask = ((lane >= 0) & (lane < HEAD_DIM)).astype(jnp.bfloat16)
    return aligned(tile * 128, 256), mask


def ring_of(weights, ring, sems, order, count):
    def copy(item):
        slot = item % RING
        return pltpu.make_async_copy(weights.at[order(item)], ring.at[slot], sems.at[slot])

    def begin():
        for item in range(RING):
            copy(item).start()

    def ready(item):
        copy(item).wait()
        return item % RING

    def release(item):
        @pl.when(item + RING < count)
        def _():
            copy(item + RING).start()

    return begin, ready, release


def forward_kernel(
    active,
    live,
    x_ref,
    weights,
    mod_ref,
    bias_ref,
    gain_ref,
    cos_ref,
    first_ref,
    second_ref,
    member_ref,
    *rest,
    aliased,
):
    rest = rest[aliased:]
    out_ref, leave_ref, left_out, hid_out, low_out, prob_out, high_out, gu_out = rest[:8]
    (
        ring,
        a_buf,
        qkv,
        low_buf,
        prob,
        high_buf,
        gu_buf,
        hid,
        left,
        acc,
        out_buf,
        leave_buf,
        ring_sem,
        out_sem,
    ) = rest[8:]
    model_width = x_ref.shape[1]
    low, high = jnp.bfloat16, jnp.float32
    heads = model_width // HEAD_DIM
    chunks = weights.shape[0]
    wide = CHUNK

    @pl.when(active[0] == 1)
    def _():
        begin, ready, release = ring_of(weights, ring, ring_sem, lambda item: item, chunks)
        begin()
        copies = []

        def send(source, target):
            copy = pltpu.make_async_copy(source, target, out_sem.at[len(copies)])
            copy.start()
            copies.append(copy)

        shift1, scale1, gate1 = mod_ref[0:1], mod_ref[1:2], mod_ref[2:3]
        shift2, scale2, gate2 = mod_ref[3:4], mod_ref[4:5], mod_ref[5:6]

        def enter(rows, carry):
            x = x_ref[rows].astype(high)
            a_buf[rows] = (x * rms_rate(x) * (1.0 + scale1) + shift1).astype(low)
            return carry

        by_rows(enter)

        def project(item, carry):
            slot = ready(item)
            cols = aligned(item * wide, wide)
            qkv[:, cols] = mul(a_buf[...], ring[slot]) + bias_ref[:, cols]
            release(item)
            return carry

        qkv_chunks = 3 * model_width // wide
        lax.fori_loop(0, qkv_chunks, project, 0)
        left[0] = a_buf[...].T
        send(left.at[0], left_out.at[0])

        member = member_ref[...]
        for index in range(2):
            base = index * model_width
            cols = slice(base, base + model_width)
            raw = qkv[:, cols]
            rate = lax.rsqrt(mul_split(raw * raw, member) * (1.0 / HEAD_DIM) + EPS)
            acc[...] = mul_split(rate, member, NT)

            def turned(rows, carry):
                unit = qkv[rows, cols] * acc[rows]
                high_buf[rows, cols] = unit
                gained = unit * gain_ref[index : index + 1]
                straight, crossed = turn(gained, cos_ref[rows], first_ref[rows], second_ref[rows])
                low_buf[rows, cols] = (straight + crossed).astype(low)
                return carry

            by_rows(turned)
            high_buf[:, 5 * model_width + index * PAD : 5 * model_width + (index + 1) * PAD] = rate

        low_buf[:, 2 * model_width :] = qkv[:, 2 * model_width :].astype(low)
        send(low_buf, low_out)
        acc[...] = jnp.zeros_like(acc)

        def attend(head, carry):
            cols, mask = window(head, model_width)
            tile = cols.start
            q = low_buf[:, cols] * mask
            k = low_buf[:, aligned(model_width + tile, 256)]
            v = low_buf[:, aligned(2 * model_width + tile, 256)] * mask
            scores = mul(k, q, NT) * HEAD_DIM ** (-0.5)
            weight = jnp.exp(scores - jnp.max(scores, axis=0, keepdims=True))
            share = (weight * (1.0 / jnp.sum(weight, axis=0, keepdims=True))).astype(low)
            prob[head] = share
            acc[:, cols] = acc[:, cols] + mul(share, v, TN)
            return carry

        lax.fori_loop(0, heads, attend, 0, unroll=2)
        send(prob, prob_out)
        a_buf[...] = acc[...].astype(low)
        left[1] = a_buf[...].T
        send(left.at[1], left_out.at[1])

        out_chunks = model_width // wide

        def mix(index, carry):
            item = qkv_chunks + index
            slot = ready(item)
            cols = aligned(index * wide, wide)
            acc[:, cols] = mul(a_buf[...], ring[slot]) + bias_ref[
                :, aligned(3 * model_width + index * wide, wide)
            ]
            release(item)
            return carry

        lax.fori_loop(0, out_chunks, mix, 0)

        proj_cols = slice(2 * model_width, 3 * model_width)
        middle_cols = slice(3 * model_width, 4 * model_width)
        ffn_cols = slice(4 * model_width, 5 * model_width)

        def between(rows, carry):
            proj = acc[rows]
            high_buf[rows, proj_cols] = proj
            middle = x_ref[rows].astype(high) + gate1 * proj
            high_buf[rows, middle_cols] = middle
            a_buf[rows] = (middle * rms_rate(middle) * (1.0 + scale2) + shift2).astype(low)
            return carry

        by_rows(between)
        left[2] = a_buf[...].T
        send(left.at[2], left_out.at[2])

        gate_chunks = FF // wide

        def widen(index, carry):
            item = qkv_chunks + out_chunks + 2 * index
            cols = aligned(index * wide, wide)
            slot = ready(item)
            gate = mul(a_buf[...], ring[slot])
            release(item)
            slot = ready(item + 1)
            up = mul(a_buf[...], ring[slot])
            release(item + 1)
            gu_buf[:, cols] = gate
            gu_buf[:, aligned(FF + index * wide, wide)] = up
            hid[:, cols] = (gate * (1.0 / (1.0 + jnp.exp(-gate))) * up).astype(low)
            return carry

        lax.fori_loop(0, gate_chunks, widen, 0)
        send(gu_buf, gu_out)
        send(hid, hid_out)
        acc[...] = jnp.zeros_like(acc)

        def narrow(index, carry):
            item = qkv_chunks + out_chunks + 2 * gate_chunks + index
            slot = ready(item)
            acc[...] += mul(hid[:, aligned(index * wide, wide)], ring[slot], NT)
            release(item)
            return carry

        lax.fori_loop(0, gate_chunks, narrow, 0)

        def leave(rows, carry):
            ffn = acc[rows]
            high_buf[rows, ffn_cols] = ffn
            result = high_buf[rows, middle_cols] + gate2 * ffn
            leave_buf[rows] = result.astype(low)
            out_buf[rows] = (result * live[0]).astype(low)
            return carry

        by_rows(leave)
        send(leave_buf, leave_ref)
        send(out_buf, out_ref)
        send(high_buf, high_out)
        for copy in copies:
            copy.wait()


def layer_shapes(model_width):
    low, high = jnp.bfloat16, jnp.float32
    return [
        ((LEN, model_width), low),
        ((LEN, model_width), low),
        ((4, model_width, LEN), low),
        ((LEN, FF), low),
        ((LEN, 3 * model_width), low),
        ((HEADS, LEN, LEN), low),
        ((LEN, 5 * model_width + 2 * PAD), high),
        ((LEN, 2 * FF), high),
    ]


def run_forward(active, live, x, weights, mod, bias, gain, tables, member, kept):
    model_width = x.shape[1]
    low, high = jnp.bfloat16, jnp.float32
    shapes = layer_shapes(model_width)
    flag = pl.BlockSpec(memory_space=pltpu.SMEM)
    near = pl.BlockSpec(memory_space=pltpu.VMEM)
    far = pl.BlockSpec(memory_space=pl.ANY)
    kept = [] if kept is None else list(kept)
    return pl.pallas_call(
        functools.partial(forward_kernel, aliased=len(kept)),
        out_shape=[jax.ShapeDtypeStruct(shape, kind) for shape, kind in shapes],
        in_specs=[flag, flag, near, far] + [near] * 7 + [far] * len(kept),
        out_specs=[far] * len(shapes),
        input_output_aliases={11 + index: index for index in range(len(kept))},
        scratch_shapes=[
            pltpu.VMEM((RING, model_width, CHUNK), low),
            pltpu.VMEM((LEN, model_width), low),
            pltpu.VMEM((LEN, 3 * model_width), high),
            pltpu.VMEM((LEN, 3 * model_width), low),
            pltpu.VMEM((HEADS, LEN, LEN), low),
            pltpu.VMEM((LEN, 5 * model_width + 2 * PAD), high),
            pltpu.VMEM((LEN, 2 * FF), high),
            pltpu.VMEM((LEN, FF), low),
            pltpu.VMEM((3, model_width, LEN), low),
            pltpu.VMEM((LEN, model_width), high),
            pltpu.VMEM((LEN, model_width), low),
            pltpu.VMEM((LEN, model_width), low),
            pltpu.SemaphoreType.DMA((RING,)),
            pltpu.SemaphoreType.DMA((10,)),
        ],
        compiler_params=pltpu.CompilerParams(vmem_limit_bytes=56 * 1024 * 1024),
        cost_estimate=pl.CostEstimate(flops=0, bytes_accessed=80_000_000, transcendentals=0),
        name="layer_forward",
    )(active, live, x, weights, mod, bias, gain, *tables, member, *kept)


def backward_kernel(
    active,
    live,
    dy_ref,
    x_ref,
    weights,
    mod_ref,
    gain_ref,
    cos_ref,
    first_ref,
    second_ref,
    member_ref,
    low_in,
    prob_in,
    high_in,
    gu_in,
    *rest,
    aliased,
):
    rest = rest[aliased:]
    dx_out, left_out, dqkv_out, dproj_out, dgu_out, dmod_out, sums_out = rest[:7]
    (
        ring,
        dy,
        low_buf,
        prob,
        high_buf,
        gu_buf,
        dgu,
        dqkv,
        small,
        left,
        acc,
        middle_grad,
        mixed_grad,
        turned_q,
        turned_k,
        turned_v,
        dmod,
        sums,
        ring_sem,
        in_sem,
        out_sem,
    ) = rest[7:]
    model_width = x_ref.shape[1]
    low, high = jnp.bfloat16, jnp.float32
    heads = model_width // HEAD_DIM
    chunks = weights.shape[0]
    wide = CHUNK
    qkv_chunks = 3 * model_width // wide
    out_chunks = model_width // wide
    gate_chunks = FF // wide
    base = qkv_chunks + out_chunks

    def order(item):
        index = item // 3
        kind = item % 3
        ffn_item = jnp.where(
            kind == 0, base + 2 * gate_chunks + index, base + 2 * index + kind - 1
        )
        late = item - 3 * gate_chunks
        other = jnp.where(late < out_chunks, qkv_chunks + late, late - out_chunks)
        return jnp.where(late < 0, ffn_item, other)

    @pl.when(active[0] == 1)
    def _():
        begin, ready, release = ring_of(weights, ring, ring_sem, order, chunks)
        loads = [
            pltpu.make_async_copy(source, target, in_sem.at[index])
            for index, (source, target) in enumerate(
                ((high_in, high_buf), (gu_in, gu_buf), (low_in, low_buf), (prob_in, prob))
            )
        ]
        loads[0].start()
        loads[1].start()
        begin()
        loads[2].start()
        loads[3].start()
        copies = []

        def send(source, target):
            copy = pltpu.make_async_copy(source, target, out_sem.at[len(copies)])
            copy.start()
            copies.append(copy)

        scale1, gate1 = mod_ref[1:2], mod_ref[2:3]
        scale2, gate2 = mod_ref[4:5], mod_ref[5:6]
        proj_cols = slice(2 * model_width, 3 * model_width)
        middle_cols = slice(3 * model_width, 4 * model_width)
        ffn_cols = slice(4 * model_width, 5 * model_width)
        nothing = jnp.zeros((1, model_width), high)

        def total(value):
            return jnp.sum(value, axis=0, keepdims=True)

        loads[0].wait()

        def enter(rows, gate_sum):
            incoming = dy_ref[rows].astype(high) * live[0]
            dy[rows] = incoming
            small[rows] = (gate2 * incoming).astype(low)
            return gate_sum + total(incoming * high_buf[rows, ffn_cols])

        dmod[5:6] = by_rows(enter, nothing)
        left[...] = small[...].T
        send(left, left_out.at[3])
        acc[...] = jnp.zeros_like(acc)
        loads[1].wait()

        def ffn_back(index, carry):
            item = 3 * index
            slot = ready(item)
            d_hid = mul(small[...], ring[slot])
            release(item)
            cols = aligned(index * wide, wide)
            cols_up = aligned(FF + index * wide, wide)
            gate = gu_buf[:, cols]
            sigma = 1.0 / (1.0 + jnp.exp(-gate))
            gated = gate * sigma
            d_gate = (d_hid * gu_buf[:, cols_up] * (sigma + gated * (1.0 - sigma))).astype(low)
            d_up = (d_hid * gated).astype(low)
            dgu[:, cols] = d_gate
            dgu[:, cols_up] = d_up
            slot = ready(item + 1)
            part = mul(d_gate, ring[slot], NT)
            release(item + 1)
            slot = ready(item + 2)
            acc[...] += part + mul(d_up, ring[slot], NT)
            release(item + 2)
            return carry

        lax.fori_loop(0, gate_chunks, ffn_back, 0)
        send(dgu, dgu_out)

        def between(rows, carry):
            scale_sum, shift_sum, gate_sum = carry
            middle = high_buf[rows, middle_cols]
            rate = rms_rate(middle)
            unit = middle * rate
            back = acc[rows]
            d_unit = back * (1.0 + scale2)
            grad = dy[rows] + rate * (
                d_unit - unit * jnp.mean(d_unit * unit, axis=-1, keepdims=True)
            )
            middle_grad[rows] = grad
            d_proj = (gate1 * grad).astype(low)
            small[rows] = d_proj
            return (
                scale_sum + total(back * unit),
                shift_sum + total(back),
                gate_sum + total(grad * high_buf[rows, proj_cols]),
            )

        scale_sum, shift_sum, gate_sum = by_rows(between, (nothing,) * 3)
        dmod[4:5] = scale_sum
        dmod[3:4] = shift_sum
        dmod[2:3] = gate_sum
        send(small, dproj_out)

        def proj_sum(rows, carry):
            return carry + total(small[rows].astype(high))

        sums[3:4] = by_rows(proj_sum, nothing)
        acc[...] = jnp.zeros_like(acc)

        def mixed_back(index, carry):
            item = 3 * gate_chunks + index
            slot = ready(item)
            acc[...] += mul(small[:, aligned(index * wide, wide)], ring[slot], NT)
            release(item)
            return carry

        lax.fori_loop(0, out_chunks, mixed_back, 0)
        mixed_grad[...] = acc[...].astype(low)
        loads[2].wait()
        loads[3].wait()
        for buffer in (turned_q, turned_k, turned_v):
            buffer[...] = jnp.zeros_like(buffer)

        def attend_back(head, carry):
            cols, mask = window(head, model_width)
            tile = cols.start
            q = low_buf[:, cols] * mask
            k = low_buf[:, aligned(model_width + tile, 256)] * mask
            v = low_buf[:, aligned(2 * model_width + tile, 256)]
            d_mixed = mixed_grad[:, cols] * mask
            share = prob[head]
            d_share = mul(v, d_mixed, NT)
            wide_share = share.astype(high)
            product = wide_share * d_share
            d_score = (product - wide_share * jnp.sum(product, axis=0, keepdims=True)).astype(low)
            turned_v[:, cols] = turned_v[:, cols] + mul(share, d_mixed)
            turned_k[:, cols] = turned_k[:, cols] + mul(d_score, q)
            turned_q[:, cols] = turned_q[:, cols] + mul(d_score, k, TN)
            return carry

        lax.fori_loop(0, heads, attend_back, 0, unroll=2)
        member = member_ref[...]
        for index, turned in enumerate((turned_q, turned_k)):
            cols = slice(index * model_width, (index + 1) * model_width)

            def unturn(rows, gain_sum):
                straight, crossed = turn(
                    turned[rows] * HEAD_DIM ** (-0.5),
                    cos_ref[rows],
                    first_ref[rows],
                    second_ref[rows],
                )
                d_norm = straight - crossed
                unit = high_buf[rows, cols]
                d_unit = d_norm * gain_ref[index : index + 1]
                turned[rows] = d_unit
                acc[rows] = d_unit * unit
                return gain_sum + total(d_norm * unit)

            sums[4 + index : 5 + index] = by_rows(unturn, nothing)
            level = mul_split(acc[...], member) * (1.0 / HEAD_DIM)
            rate = high_buf[:, 5 * model_width + index * PAD : 5 * model_width + (index + 1) * PAD]
            acc[...] = mul_split(rate * level, member, NT)
            dy[...] = mul_split(rate, member, NT)

            def unscale(rows, carry):
                d_raw = dy[rows] * turned[rows] - high_buf[rows, cols] * acc[rows]
                d_low = d_raw.astype(low)
                dqkv[rows, cols] = d_low
                return carry + total(d_low.astype(high))

            sums[index : index + 1] = by_rows(unscale, nothing)

        def values(rows, carry):
            d_low = turned_v[rows].astype(low)
            dqkv[rows, 2 * model_width :] = d_low
            return carry + total(d_low.astype(high))

        sums[2:3] = by_rows(values, nothing)
        send(dqkv, dqkv_out)
        acc[...] = jnp.zeros_like(acc)

        def project_back(index, carry):
            item = 3 * gate_chunks + out_chunks + index
            slot = ready(item)
            acc[...] += mul(dqkv[:, aligned(index * wide, wide)], ring[slot], NT)
            release(item)
            return carry

        lax.fori_loop(0, qkv_chunks, project_back, 0)

        def leave(rows, carry):
            scale_sum, shift_sum = carry
            x = x_ref[rows].astype(high)
            rate = rms_rate(x)
            unit = x * rate
            back = acc[rows]
            d_unit = back * (1.0 + scale1)
            grad = middle_grad[rows] + rate * (
                d_unit - unit * jnp.mean(d_unit * unit, axis=-1, keepdims=True)
            )
            mixed_grad[rows] = grad.astype(low)
            return scale_sum + total(back * unit), shift_sum + total(back)

        scale_sum, shift_sum = by_rows(leave, (nothing,) * 2)
        dmod[1:2] = scale_sum
        dmod[0:1] = shift_sum
        send(mixed_grad, dx_out)
        send(dmod, dmod_out)
        send(sums, sums_out)
        for copy in copies:
            copy.wait()


def run_backward(active, live, dy, x, weights, mod, gain, tables, member, parts, left, kept):
    model_width = x.shape[1]
    low, high = jnp.bfloat16, jnp.float32
    shapes = [
        ((LEN, model_width), low),
        ((4, model_width, LEN), low),
        ((LEN, 3 * model_width), low),
        ((LEN, model_width), low),
        ((LEN, 2 * FF), low),
        ((8, model_width), high),
        ((8, model_width), high),
    ]
    flag = pl.BlockSpec(memory_space=pltpu.SMEM)
    near = pl.BlockSpec(memory_space=pltpu.VMEM)
    far = pl.BlockSpec(memory_space=pl.ANY)
    if kept is None:
        extra, aliases = [left], {15: 1}
    else:
        extra = list(kept)
        aliases = {15 + index: index for index in range(len(extra))}
    return pl.pallas_call(
        functools.partial(backward_kernel, aliased=len(extra)),
        out_shape=[jax.ShapeDtypeStruct(shape, kind) for shape, kind in shapes],
        in_specs=[flag, flag, near, near, far] + [near] * 6 + [far] * (4 + len(extra)),
        out_specs=[far] * len(shapes),
        input_output_aliases=aliases,
        scratch_shapes=[
            pltpu.VMEM((RING, model_width, CHUNK), low),
            pltpu.VMEM((LEN, model_width), high),
            pltpu.VMEM((LEN, 3 * model_width), low),
            pltpu.VMEM((HEADS, LEN, LEN), low),
            pltpu.VMEM((LEN, 5 * model_width + 2 * PAD), high),
            pltpu.VMEM((LEN, 2 * FF), high),
            pltpu.VMEM((LEN, 2 * FF), low),
            pltpu.VMEM((LEN, 3 * model_width), low),
            pltpu.VMEM((LEN, model_width), low),
            pltpu.VMEM((model_width, LEN), low),
            pltpu.VMEM((LEN, model_width), high),
            pltpu.VMEM((LEN, model_width), high),
            pltpu.VMEM((LEN, model_width), low),
            pltpu.VMEM((LEN, model_width), high),
            pltpu.VMEM((LEN, model_width), high),
            pltpu.VMEM((LEN, model_width), high),
            pltpu.VMEM((8, model_width), high),
            pltpu.VMEM((8, model_width), high),
            pltpu.SemaphoreType.DMA((RING,)),
            pltpu.SemaphoreType.DMA((4,)),
            pltpu.SemaphoreType.DMA((10,)),
        ],
        compiler_params=pltpu.CompilerParams(vmem_limit_bytes=56 * 1024 * 1024),
        cost_estimate=pl.CostEstimate(flops=0, bytes_accessed=120_000_000, transcendentals=0),
        name="layer_backward",
    )(active, live, dy, x, weights, mod, gain, *tables, member, *parts, *extra)


def body(
    start,
    out_grad,
    extra_images,
    timesteps,
    labels,
    embed_table,
    w_qkv,
    w_out,
    w_gu,
    w_ada,
    w_down,
    small_params,
    feature_moments,
    other_moments,
    small_moment,
):
    model_width = start.shape[-1]
    section_index = lax.axis_index("section")
    shard_index = lax.axis_index("shard")
    group_index = lax.axis_index("grp")
    sections = lax.axis_size("section")
    shards = lax.axis_size("shard")
    groups = lax.axis_size("grp")
    rows = w_qkv.shape[1]
    low = jnp.bfloat16
    high = jnp.float32
    widths = (3 * model_width, model_width, 2 * FF, FF)
    starts = (0, widths[0], widths[0] + widths[1], widths[0] + widths[1] + widths[2])
    gate_up = w_gu[0].reshape(rows, 2, FF // CHUNK, CHUNK).transpose(0, 2, 1, 3)
    own = jnp.concatenate(
        [w_qkv[0], w_out[0], gate_up.reshape(rows, 2 * FF), w_down[0].T], axis=1
    ).astype(low)
    own = own.reshape(rows, sum(widths) // CHUNK, CHUNK).transpose(1, 0, 2)
    weights = gather_rows(own).reshape(own.shape[0], model_width, CHUNK)
    ada_low = w_ada[0].astype(low)
    small_all = lax.all_gather(small_params[0].astype(low), "shard", axis=0, tiled=True)
    small_all = small_all.astype(high)
    bias = small_all[None, : 4 * model_width]
    b_ada = small_all[4 * model_width : 10 * model_width]
    gain = jnp.tile(small_all[10 * model_width :].reshape(2, HEAD_DIM), (1, HEADS))
    tables = rope_tables(model_width)
    member = head_members(model_width)
    half_cond = embed_table[timesteps] + embed_table[TIMESTEPS + labels]
    cond_all = lax.all_gather(half_cond, ("section", "shard"))
    cond_all = cond_all.reshape(sections, shards * MB, half_cond.shape[1])
    cond_all = cond_all.transpose(1, 0, 2).reshape(shards * MB, model_width)
    act_all = jax.nn.silu(cond_all).astype(low)
    condition = lax.dynamic_slice_in_dim(cond_all, shard_index * MB, MB, 0)
    act_low = lax.dynamic_slice_in_dim(act_all, shard_index * MB, MB, 0)
    act_columns = lax.dynamic_slice_in_dim(act_all, shard_index * rows, rows, 1)
    partial_mod = jnp.dot(act_columns, ada_low, preferred_element_type=high)
    modulation = lax.psum_scatter(partial_mod, "shard", scatter_dimension=0, tiled=True) + b_ada
    image_count = extra_images[0] + 1
    live = [(jnp.full((1,), micro) < image_count).astype(high) for micro in range(MB)]
    here = [jnp.full((1,), section_index == index, jnp.int32) for index in range(2)]
    mods = [modulation[micro].reshape(6, model_width) for micro in range(MB)]
    fixed = (gain, tables, member)
    kept = []
    received = []
    for micro in range(MB):
        result = run_forward(
            here[0], live[micro], start[micro], weights, mods[micro], bias, *fixed, None
        )
        kept.append(result)
        received.append(passed_along(result[1], "section", 1))
    for micro in range(MB):
        kept[micro] = run_forward(
            here[1], live[micro], received[micro], weights, mods[micro], bias, *fixed, kept[micro]
        )
    section_out = jnp.stack([result[0] for result in kept])
    grads_kept = []
    returned = []
    for micro in range(MB):
        result = run_backward(
            here[1],
            live[micro],
            out_grad[micro],
            received[micro],
            weights,
            mods[micro],
            *fixed,
            kept[micro][4:],
            kept[micro][2],
            None,
        )
        grads_kept.append(result)
        returned.append(passed_along(result[0], "section", -1))
    for micro in range(MB):
        grads_kept[micro] = run_backward(
            here[0],
            live[micro],
            returned[micro],
            start[micro],
            weights,
            mods[micro],
            *fixed,
            kept[micro][4:],
            None,
            grads_kept[micro],
        )
    section_in_grad = jnp.stack([result[0] for result in grads_kept])
    lefts = [result[1].reshape(4, shards, rows, LEN) for result in grads_kept]
    rights = [
        [result[2], result[3], result[4], kept[micro][3]]
        for micro, result in enumerate(grads_kept)
    ]
    sums = sum(result[6] for result in grads_kept)
    gains = jnp.sum(sums[4:6].reshape(2, HEADS, HEAD_DIM), axis=1)
    packed = jnp.concatenate([result[5][:6] for result in grads_kept] + [sums[:4]], axis=0)
    beside = jnp.pad(gains, ((0, packed.shape[0] - 2), (0, PAD - HEAD_DIM)))
    packed = jnp.concatenate([packed, beside], axis=1).astype(low)
    images = shards * MB
    act_rows = jnp.pad(act_columns, ((0, -images % 16), (0, -rows % 128)))
    tail = jnp.pad(jnp.sum(feature_moments[0], axis=1)[None], ((0, 0), (0, CHUNK - 5)))
    reduced = reduce_grads(lefts, rights, packed, act_rows, ada_low, tail)
    sum_low = reduced[:4]
    row_squares, stats, totals, all_mod, every_act, cond_parts = reduced[4:]
    small_vector = jnp.concatenate(
        [
            totals[12:16, :model_width].reshape(-1),
            (totals[:6] + totals[6:12])[:, :model_width].reshape(-1),
            totals[:2, model_width : model_width + HEAD_DIM].reshape(-1),
        ]
    )
    small_rows = small_params.shape[1]
    small_grad = lax.dynamic_slice_in_dim(small_vector, shard_index * small_rows, small_rows, 0)
    flat_act = every_act.reshape(-1, every_act.shape[2])[:, :rows]
    grad_ada = jnp.concatenate(
        [
            lax.dot_general(flat_act, all_mod[index], TN, preferred_element_type=high)
            for index in range(6)
        ],
        axis=1,
    )
    own_part = lax.dynamic_slice_in_dim(cond_parts, shard_index * MB, MB, 1)[:, :, :rows]
    act_grad = own_part.transpose(1, 0, 2).reshape(MB, model_width)
    sigma = jax.nn.sigmoid(condition)
    cond_term = act_grad * sigma * (1.0 + condition * (1.0 - sigma))
    cond_grad = lax.dynamic_slice_in_dim(
        cond_term, section_index * half_cond.shape[1], half_cond.shape[1], 1
    )

    wide = (widths[0], widths[1], widths[2], 6 * model_width, widths[3])
    order = (0, 1, 2, 4, 3)
    row_sums = jnp.sum(row_squares, axis=-1)
    row_means = jnp.stack([row_sums[index] / width for index, width in zip(order, wide)])
    feature_new = DECAY * feature_moments[0] + (1.0 - DECAY) * row_means
    column_flat = stats[:-1].reshape(-1)
    column_all = jnp.concatenate(
        [column_flat[: starts[3]], column_flat[sum(widths) :], column_flat[starts[3] : sum(widths)]]
    )
    ends = [sum(wide[: index + 1]) for index in range(5)]
    feature_total = jnp.stack(
        [
            DECAY * stats[-1, index]
            + (1.0 - DECAY) / wide[index] * jnp.sum(column_all[ends[index] - wide[index] : ends[index]])
            for index in range(5)
        ]
    )
    other_new = DECAY * other_moments[0] + (1.0 - DECAY) * column_all / model_width
    grads = [
        sum_low[0].astype(high),
        sum_low[1].astype(high),
        sum_low[2].astype(high),
        grad_ada,
        sum_low[3].astype(high),
    ]
    masters = (w_qkv[0], w_out[0], w_gu[0], w_ada[0], w_down[0].T)
    feature_scale = lax.rsqrt(feature_new / (feature_total / model_width)[:, None])
    other_scale = lax.rsqrt(other_new)
    new_wide = []
    lower = 0
    for index in range(5):
        upper = lower + wide[index]
        new_wide.append(
            masters[index]
            - RATE
            * grads[index]
            * feature_scale[index][:, None]
            * other_scale[None, lower:upper]
        )
        lower = upper
    small_new = DECAY * small_moment[0] + (1.0 - DECAY) * (small_grad * small_grad + TINY)
    new_small = small_params[0] - RATE_SMALL * small_grad * lax.rsqrt(small_new)
    return (
        section_out[None],
        section_in_grad[None],
        cond_grad,
        grads[0][None],
        grads[1][None],
        grads[2][None],
        grads[3][None],
        grads[4].T[None],
        small_grad[None],
        new_wide[0][None],
        new_wide[1][None],
        new_wide[2][None],
        new_wide[3][None],
        new_wide[4].T[None],
        new_small[None],
        feature_new[None],
        other_new[None],
        small_new[None],
    )


def solution(mesh):
    in_specs = (
        P(("grp", "shard"), None, None),
        P(("grp", "shard"), None, None),
        P(("grp", "shard")),
        P(("grp", "shard")),
        P(("grp", "shard")),
        P(None, "section"),
        P("section", "shard", None),
        P("section", "shard", None),
        P("section", "shard", None),
        P("section", "shard", None),
        P("section", None, "shard"),
        P("section", "shard"),
        P("section", None, "shard"),
        P("section", None),
        P("section", "shard"),
    )
    out_specs = (
        P("section", ("grp", "shard"), None, None),
        P("section", ("grp", "shard"), None, None),
        P(("grp", "shard"), "section"),
        P("section", "shard", None),
        P("section", "shard", None),
        P("section", "shard", None),
        P("section", "shard", None),
        P("section", None, "shard"),
        P("section", "shard"),
        P("section", "shard", None),
        P("section", "shard", None),
        P("section", "shard", None),
        P("section", "shard", None),
        P("section", None, "shard"),
        P("section", "shard"),
        P("section", None, "shard"),
        P("section", None),
        P("section", "shard"),
    )
    return jax.shard_map(body, mesh=mesh, in_specs=in_specs, out_specs=out_specs, check_vma=False)
```

```python
import functools

import jax
import jax.numpy as jnp
import numpy as np
from jax import lax
from jax.experimental import pallas as pl
from jax.experimental.pallas import tpu as pltpu
from jax.sharding import PartitionSpec as P

HEADS = 16
FF = 3072
GRID = 16
MB = 2
TIMESTEPS = 1000
HEAD_DIM = 72
LEN = 256


EPS = 1e-06
TINY = 1e-30
RATE = 0.04
RATE_SMALL = 0.05
DECAY = 0.5
CHUNK = 384
AHEAD = 3
LAG = 2
SLOTS = 6
HOP = 2
MESH = pl.DeviceIdType.MESH
RING = 10
ROWS = 32
NT = (((1,), (1,)), ((), ()))
TN = (((0,), (0,)), ((), ()))
PAD = 128
IN_SLOTS = 5
OUT_SLOTS = 4


def passed_along(block, axis, distance):
    devices = range(lax.axis_size(axis))
    route = [(i - distance, i) for i in devices if i - distance in devices]
    return lax.ppermute(block, axis, route)


def rope_tables(model_width):
    quarter = HEAD_DIM // 4
    tokens = np.arange(LEN)
    inverse = np.float32(10000.0) ** (-np.arange(quarter).astype(np.float32) / quarter)
    row_angle = (tokens // GRID).astype(np.float32)[:, None] * inverse[None, :]
    col_angle = (tokens % GRID).astype(np.float32)[:, None] * inverse[None, :]
    angles = np.concatenate([row_angle, row_angle, col_angle, col_angle], axis=1)
    lane = np.arange(HEAD_DIM) % (HEAD_DIM // 2)
    sines = np.sin(angles)
    first = np.where(lane < quarter, -sines, 0.0)
    second = np.where(lane >= quarter, sines, 0.0)
    count = model_width // HEAD_DIM
    return tuple(
        jnp.asarray(np.tile(table, (1, count)), jnp.float32)
        for table in (np.cos(angles), first, second)
    )


def head_members(model_width):
    owner = np.arange(model_width)[:, None] // HEAD_DIM
    return jnp.asarray(owner == np.arange(PAD)[None, :], jnp.bfloat16)


def dot_back(incoming, matrix):
    return mul(incoming, matrix, NT)


def place():
    return lax.axis_index("section"), lax.axis_index("grp"), lax.axis_index("shard")


def gather_kernel(
    shards,
    bounds,
    cond_in,
    small_in,
    qkv_ref,
    out_ref,
    gu_ref,
    down_ref,
    ada_ref,
    all_ref,
    ada_low,
    acts_ref,
    mod_ref,
    small_ref,
    own,
    stage,
    ada_wide,
    cond,
    act,
    part,
    part_in,
    chip_out,
    chip_in,
    load_sem,
    ada_sem,
    here_sem,
    sib_sem,
    x_sem,
    z_sem,
    f_sem,
    cond_sem,
    small_sem,
    part_sem,
):
    sec, grp, me = place()
    chips = shards // 2
    core = me % 2
    chip = me // 2
    half = grp % 2
    rows = own.shape[1]
    count = own.shape[0] // 2
    low, high = jnp.bfloat16, jnp.float32
    sibling = (sec, grp, me ^ 1)
    across = (sec, grp ^ 1, me)
    opposite = (1 - sec, grp, me)

    def chip_peer(k):
        return (sec, grp, 2 * (chip ^ k) + core)

    barrier = pltpu.get_barrier_semaphore()
    pl.semaphore_signal(barrier, inc=1, device_id=sibling, device_id_type=MESH)
    pl.semaphore_signal(barrier, inc=1, device_id=across, device_id_type=MESH)
    pl.semaphore_signal(barrier, inc=1, device_id=opposite, device_id_type=MESH)
    for k in range(1, chips):
        pl.semaphore_signal(barrier, inc=1, device_id=chip_peer(k), device_id_type=MESH)
    ada_load = pltpu.make_async_copy(ada_ref, ada_wide, ada_sem)
    ada_load.start()

    def load(step, side, start):
        piece = 2 * step + side
        slot = (step % 2) * 2 + side
        target = stage.at[slot]
        if not start:
            pltpu.make_async_copy(
                qkv_ref.at[:, pl.ds(0, CHUNK)], target, load_sem.at[slot]
            ).wait()
            return
        sources = (qkv_ref, out_ref, gu_ref, down_ref)
        for index, source in enumerate(sources):
            local = piece - bounds[index]
            if index == 2:
                pairs = source.shape[1] // CHUNK // 2
                local = local // 2 + pairs * (local % 2)

            @pl.when((piece >= bounds[index]) & (piece < bounds[index + 1]))
            def _():
                begin = pl.multiple_of(local * CHUNK, CHUNK)
                pltpu.make_async_copy(
                    source.at[:, pl.ds(begin, CHUNK)], target, load_sem.at[slot]
                ).start()

    for side in range(2):
        load(0, side, True)
    pl.semaphore_wait(barrier, chips + 2)

    def remote(source, target, sems, device):
        return pltpu.make_async_remote_copy(
            src_ref=source,
            dst_ref=target,
            send_sem=sems[0],
            recv_sem=sems[1],
            device_id=device,
            device_id_type=MESH,
        )

    def pair(sems, *index):
        return sems.at[(0,) + index], sems.at[(1,) + index]

    def chip_copy(k, step, owner):
        piece = 2 * step + half
        return remote(
            own.at[piece], all_ref.at[piece, owner], pair(x_sem, k - 1, step), chip_peer(k)
        )

    def onward(k, step, side, sems, row, target, by_core):
        owner = 2 * (chip ^ k) + by_core
        region = all_ref.at[2 * step + side, owner]
        return remote(region, region, pair(sems, row, step), target)

    def beside(step, owner):
        both = pl.ds(2 * step, 2)
        return remote(own.at[both], all_ref.at[both, owner], pair(sib_sem, step), sibling)

    def here(step):
        both = pl.ds(2 * step, 2)
        return pltpu.make_async_copy(own.at[both], all_ref.at[both, me], here_sem.at[step])

    def cond_across():
        region = cond.at[me, sec]
        return remote(region, region, pair(cond_sem, 0), opposite)

    def cond_from_across():
        region = cond.at[me, 1 - sec]
        return remote(region, region, pair(cond_sem, 0), opposite)

    def cond_beside(owner):
        return remote(cond.at[owner], cond.at[owner], pair(cond_sem, 1), sibling)

    def cond_chip(k, owner):
        region = cond.at[pl.ds(2 * owner, 2)]
        return remote(region, region, pair(cond_sem, 1 + k), chip_peer(k))

    def small_beside(owner):
        return remote(small_ref.at[owner], small_ref.at[owner], pair(small_sem, 0), sibling)

    def small_chip(k, owner):
        region = small_ref.at[pl.ds(2 * owner, 2)]
        return remote(region, region, pair(small_sem, k), chip_peer(k))

    def part_beside(which_core):
        return remote(part.at[which_core], part_in, pair(part_sem, 0), sibling)

    def part_chip(k):
        return remote(
            chip_out.at[k - 1], chip_in.at[k - 1], pair(part_sem, k), chip_peer(k)
        )

    cond[me, sec] = cond_in[...]
    cond_across().start()
    small_ref[me] = small_in[...]
    small_beside(me).start()
    half_width = cond_in.shape[1]
    ada_chunks = ada_low.shape[1] // CHUNK
    model_width = act.shape[1]
    thirds = 3

    def modulate(step):
        @pl.when(step == 1)
        def _():
            cond_from_across().wait_recv()
            cond_beside(me).start()
            small_beside(me ^ 1).wait_recv()
            for k in range(1, chips):
                small_chip(k, chip).start()

        @pl.when(step == 2)
        def _():
            cond_beside(me ^ 1).wait_recv()
            for k in range(1, chips):
                cond_chip(k, chip).start()

        @pl.when(step == 4)
        def _():
            for k in range(1, chips):
                cond_chip(k, chip ^ k).wait_recv()
                small_chip(k, chip ^ k).wait_recv()
            act[...] = jnp.zeros_like(act)
            width = model_width // 2
            for owner in range(shards):
                for section in range(2):
                    value = cond[owner, section, :MB, :width]
                    act[owner * MB : (owner + 1) * MB, section * width : (section + 1) * width] = (
                        value * (1.0 / (1.0 + jnp.exp(-value)))
                    )
            shape = (model_width, acts_ref.shape[1])
            column = lax.broadcasted_iota(jnp.int32, shape, 1)
            wanted = (lax.broadcasted_iota(jnp.int32, shape, 0) == column + me * rows) & (
                column < rows
            )
            acts_ref[...] = mul(
                act[...].astype(low), wanted.astype(high).astype(low)
            ).astype(low)
            part[...] = jnp.zeros_like(part)
            ada_load.wait()

        for group in range(ada_chunks // thirds):

            @pl.when(step == 5 + group)
            def _():
                for index in range(thirds):
                    begin = (group * thirds + index) * CHUNK
                    cols = slice(begin, begin + CHUNK)
                    narrow = ada_wide[:, cols].astype(low)
                    ada_low[:, cols] = narrow
                    product = mul(acts_ref[:, :rows], narrow)
                    for owner in range(shards):
                        first = owner // 2 * MB
                        part[owner % 2, first : first + MB, cols] = product[
                            owner * MB : (owner + 1) * MB
                        ]

        ready = 5 + ada_chunks // thirds

        @pl.when(step == ready)
        def _():
            part_beside(1 - core).start()

        @pl.when(step == ready + 1)
        def _():
            part_beside(core).wait_recv()
            part_in[...] = part_in[...] + part[core]
            for k in range(1, chips):
                for image in range(MB):
                    line = pl.ds((chip ^ k) * MB + image, 1)
                    chip_out[k - 1, image : image + 1] = part_in[line, :]
                part_chip(k).start()

        @pl.when(step == ready + 3)
        def _():
            for k in range(1, chips):
                part_chip(k).wait_recv()
            for image in range(MB):
                value = part_in[pl.ds(chip * MB + image, 1), :]
                for k in range(1, chips):
                    value = value + chip_in[k - 1, image : image + 1]
                mod_ref[image : image + 1] = value

    def relay(step, carry):
        @pl.when(step < count)
        def _():
            @pl.when(step + 1 < count)
            def _():
                for side in range(2):
                    load(step + 1, side, True)

            for side in range(2):
                load(step, side, False)
                own[2 * step + side] = stage[(step % 2) * 2 + side].astype(low)
            for k in range(1, chips):
                chip_copy(k, step, me).start()
            here(step).start()
            beside(step, me).start()

        came = step - AHEAD

        @pl.when((came >= 0) & (came < count))
        def _():
            for k in range(1, chips):
                chip_copy(k, came, 2 * (chip ^ k) + core).wait_recv()
                onward(k, came, half, z_sem, k - 1, across, core).start()
                onward(k, came, half, f_sem, 2 * (k - 1), sibling, core).start()
                chip_copy(k, came, me).wait_send()

        passed = step - AHEAD - LAG

        @pl.when(passed >= 0)
        def _():
            for k in range(1, chips):
                onward(k, passed, 1 - half, z_sem, k - 1, across, core).wait_recv()
                onward(k, passed, 1 - half, f_sem, 2 * (k - 1) + 1, sibling, core).start()
                onward(k, passed, half, z_sem, k - 1, across, core).wait_send()

        modulate(step)
        return carry

    lax.fori_loop(0, count + AHEAD + LAG, relay, 0)

    def finish(step, carry):
        for k in range(1, chips):
            for side, row in ((half, 2 * (k - 1)), (1 - half, 2 * (k - 1) + 1)):
                onward(k, step, side, f_sem, row, sibling, core).wait_send()
                onward(k, step, side, f_sem, row, sibling, 1 - core).wait_recv()
        beside(step, me).wait_send()
        beside(step, me ^ 1).wait_recv()
        here(step).wait()
        return carry

    lax.fori_loop(0, count, finish, 0)
    cond_across().wait_send()
    cond_beside(me).wait_send()
    small_beside(me).wait_send()
    part_beside(1 - core).wait_send()
    for k in range(1, chips):
        cond_chip(k, chip).wait_send()
        small_chip(k, chip).wait_send()
        part_chip(k).wait_send()


def gather_rows(cond, small, w_qkv, w_out, w_gu, w_down, w_ada):
    shards = lax.axis_size("shard")
    chips = shards // 2
    rows = w_qkv.shape[0]
    model_width = rows * shards
    widths = [matrix.shape[1] for matrix in (w_qkv, w_out, w_gu, w_down)]
    chunks = sum(widths) // CHUNK
    bounds = [sum(widths[:index]) // CHUNK for index in range(5)]
    count = chunks // 2
    low, high = jnp.bfloat16, jnp.float32
    images = shards * MB
    act_shape = (images + -images % 16, rows + -rows % 128)
    side = chips * MB + -(chips * MB) % 8
    ada_width = w_ada.shape[1]
    near = pl.BlockSpec(memory_space=pltpu.VMEM)
    far = pl.BlockSpec(memory_space=pl.ANY)
    return pl.pallas_call(
        functools.partial(gather_kernel, shards, bounds),
        out_shape=[
            jax.ShapeDtypeStruct((chunks, shards, rows, CHUNK), low),
            jax.ShapeDtypeStruct((rows, ada_width), low),
            jax.ShapeDtypeStruct(act_shape, low),
            jax.ShapeDtypeStruct((MB, ada_width), high),
            jax.ShapeDtypeStruct((shards,) + small.shape, high),
        ],
        in_specs=[near, near] + [far] * 5,
        out_specs=[far] + [near] * 4,
        scratch_shapes=[
            pltpu.VMEM((chunks, rows, CHUNK), low),
            pltpu.VMEM((4, rows, CHUNK), high),
            pltpu.VMEM((rows, ada_width), high),
            pltpu.VMEM((shards, 2) + cond.shape, high),
            pltpu.VMEM((act_shape[0], model_width), high),
            pltpu.VMEM((2, side, ada_width), high),
            pltpu.VMEM((side, ada_width), high),
            pltpu.VMEM((chips - 1, 8, ada_width), high),
            pltpu.VMEM((chips - 1, 8, ada_width), high),
            pltpu.SemaphoreType.DMA((4,)),
            pltpu.SemaphoreType.DMA,
            pltpu.SemaphoreType.DMA((count,)),
            pltpu.SemaphoreType.DMA((2, count)),
            pltpu.SemaphoreType.DMA((2, chips - 1, count)),
            pltpu.SemaphoreType.DMA((2, chips - 1, count)),
            pltpu.SemaphoreType.DMA((2, 2 * (chips - 1), count)),
            pltpu.SemaphoreType.DMA((2, chips + 1)),
            pltpu.SemaphoreType.DMA((2, chips)),
            pltpu.SemaphoreType.DMA((2, chips)),
        ],
        compiler_params=pltpu.CompilerParams(
            collective_id=0, has_side_effects=True, vmem_limit_bytes=60 * 1024 * 1024
        ),
        cost_estimate=pl.CostEstimate(flops=0, bytes_accessed=300_000_000, transcendentals=0),
        name="gather_rows",
    )(cond, small, w_qkv, w_out, w_gu, w_down, w_ada)


def reduce_kernel(shards, groups, firsts, pieces, *refs):
    matrices = len(firsts)
    left_refs, refs = refs[:MB], refs[MB:]
    right_refs, refs = refs[: MB * matrices], refs[MB * matrices :]
    pack_ref, act_ref, ada_ref, tail_ref, refs = *refs[:4], refs[4:]
    sum_refs, refs = refs[:matrices], refs[matrices:]
    (
        rowsq_ref,
        stats_ref,
        total_ref,
        mods_ref,
        acts_ref,
        cond_ref,
        right_buf,
        send1,
        keep1,
        recv1,
        send2,
        recv2,
        keep2,
        keep3,
        send3,
        recv3,
        final,
        recv5,
        spread,
        mods,
        part,
        part_in,
        stats,
        stats_in,
        stats_all,
        right_sem,
        sem1,
        sem2,
        sem3,
        sem5,
        out_sem,
        chip_sem,
        line_sem,
        swap_sem,
        cond_sem,
        stat_sem,
    ) = refs
    chips = shards // 2
    ends = 2 * groups
    rows = rowsq_ref.shape[1]
    bounds = list(firsts) + [sum(ref.shape[1] for ref in sum_refs) // CHUNK]
    total = bounds[-1]
    model_width = mods.shape[2]
    per_group = acts_ref.shape[1]
    low, high = jnp.bfloat16, jnp.float32
    sec, grp, me = place()
    core = me % 2
    chip = me // 2
    middle = groups // 2
    lower = grp < middle
    depth = jnp.where(lower, middle - 1 - grp, grp - middle)
    inner = jnp.where(lower, grp + 1, grp - 1)
    outer = jnp.where(lower, grp - 1, grp + 1)
    has_outer = depth < middle - 1
    sibling = (sec, grp, me ^ 1)
    across = (1 - sec, grp, me)

    def chip_peer(k):
        return (sec, grp, 2 * (chip ^ k) + core)

    barrier = pltpu.get_barrier_semaphore()
    pl.semaphore_signal(barrier, inc=1, device_id=sibling, device_id_type=MESH)
    pl.semaphore_signal(barrier, inc=1, device_id=across, device_id_type=MESH)
    for k in range(1, chips):
        pl.semaphore_signal(barrier, inc=1, device_id=chip_peer(k), device_id_type=MESH)
    pl.semaphore_signal(barrier, inc=1, device_id=(sec, inner, me), device_id_type=MESH)

    @pl.when(has_outer)
    def _():
        pl.semaphore_signal(barrier, inc=1, device_id=(sec, outer, me), device_id_type=MESH)

    pl.semaphore_wait(barrier, chips + 2 + jnp.where(has_outer, 1, 0))

    def which(item):
        matrix = 0
        for first in firsts[1:]:
            matrix = matrix + jnp.where(item >= first, 1, 0)
        return matrix

    def in_matrix(item, matrix):
        return (item >= bounds[matrix]) & (item < bounds[matrix + 1])

    def columns(item, matrix):
        return pl.ds(pl.multiple_of((item - firsts[matrix]) * CHUNK, CHUNK), CHUNK)

    def fetch(item):
        slot = item % 3
        for matrix in range(matrices):

            @pl.when(in_matrix(item, matrix))
            def _():
                for micro in range(MB):
                    pltpu.make_async_copy(
                        right_refs[micro * matrices + matrix].at[:, columns(item, matrix)],
                        right_buf.at[slot, micro],
                        right_sem.at[slot, micro],
                    ).start()

    def arrived(item):
        for micro in range(MB):
            slot = item % 3
            pltpu.make_async_copy(
                right_refs[0].at[:, pl.ds(0, CHUNK)],
                right_buf.at[slot, micro],
                right_sem.at[slot, micro],
            ).wait()

    def remote(source, target, sems, device):
        return pltpu.make_async_remote_copy(
            src_ref=source,
            dst_ref=target,
            send_sem=sems[0],
            recv_sem=sems[1],
            device_id=device,
            device_id_type=MESH,
        )

    def copy1(item):
        slot = item % SLOTS
        sems = (sem1.at[0, slot], sem1.at[1, slot])
        return remote(send1.at[slot], recv1.at[slot], sems, sibling)

    def copy2(item, k):
        slot = item % SLOTS
        sems = (sem2.at[0, slot, k - 1], sem2.at[1, slot, k - 1])
        return remote(send2.at[slot, k - 1], recv2.at[slot, k - 1], sems, chip_peer(k))

    def copy3(item, kind):
        slot = item % SLOTS
        sems = (sem3.at[0, 0, slot], sem3.at[1, kind, slot])
        return remote(send3.at[slot], recv3.at[kind, slot], sems, (sec, inner, me))

    def copy5(item):
        slot = item % ends
        sems = (sem5.at[0, slot], sem5.at[1, slot])
        return remote(final.at[slot], recv5.at[slot], sems, (sec, outer, me))

    def start_out(item):
        slot = item % ends
        for matrix in range(matrices):

            @pl.when(in_matrix(item, matrix))
            def _():
                pltpu.make_async_copy(
                    final.at[slot], sum_refs[matrix].at[:, columns(item, matrix)], out_sem.at[slot]
                ).start()

    def wait_out(item):
        slot = item % ends
        pltpu.make_async_copy(
            final.at[slot], sum_refs[0].at[:, pl.ds(0, CHUNK)], out_sem.at[slot]
        ).wait()

    def chip_spread(k, owner):
        region = spread.at[core, grp, owner]
        sems = (chip_sem.at[0, k - 1], chip_sem.at[1, k - 1])
        return remote(region, region, sems, chip_peer(k))

    def line_spread(side, step, row):
        target = (sec, grp + 1 - 2 * side, me)
        region = spread.at[core, row]
        second = acts_ref.at[row]
        return (
            remote(
                region, region, (line_sem.at[0, side, step, 0], line_sem.at[1, side, step, 0]), target
            ),
            remote(
                second, second, (line_sem.at[0, side, step, 1], line_sem.at[1, side, step, 1]), target
            ),
        )

    def swap_spread(which_core):
        region = spread.at[which_core]
        return remote(region, region, (swap_sem.at[0], swap_sem.at[1]), sibling)

    def cond_across():
        return remote(part, part_in, (cond_sem.at[0, 0], cond_sem.at[1, 0]), across)

    def cond_beside(owner):
        region = cond_ref.at[owner]
        return remote(region, region, (cond_sem.at[0, 1], cond_sem.at[1, 1]), sibling)

    def cond_chip(k, owner):
        region = cond_ref.at[pl.ds(2 * owner, 2)]
        sems = (cond_sem.at[0, 1 + k], cond_sem.at[1, 1 + k])
        return remote(region, region, sems, chip_peer(k))

    def exists(side):
        return (grp < groups - 1) if side == 0 else (grp > 0)

    swap_tick = 2 + 2 * groups
    piece_tick = swap_tick + 2
    cond_tick = piece_tick + pieces

    def beside_the_sum(tick):
        @pl.when(tick == 2)
        def _():
            for k in range(1, chips):
                chip_spread(k, chip ^ k).wait_recv()
            for side in range(2):

                @pl.when(exists(side))
                def _():
                    for copy in line_spread(side, 0, grp):
                        copy.start()

        for step in range(1, groups):

            @pl.when(tick == 2 + 2 * step)
            def _():
                for side in range(2):
                    row = grp - step if side == 0 else grp + step
                    came = (row >= 0) if side == 0 else (row < groups)

                    @pl.when(came)
                    def _():
                        for copy in line_spread(side, step - 1, row):
                            copy.wait_recv()

                    @pl.when(came & exists(side))
                    def _():
                        for copy in line_spread(side, step, row):
                            copy.start()

        @pl.when(tick == swap_tick)
        def _():
            swap_spread(core).start()

        @pl.when(tick == piece_tick)
        def _():
            swap_spread(1 - core).wait_recv()
            mods[...] = jnp.zeros_like(mods)
            total_ref[...] = jnp.zeros_like(total_ref)

            def unpack(index, carry):
                origin = index // (groups * chips)
                row = (index // chips) % groups
                owner = index % chips
                block = spread[origin, row, owner].astype(high)
                total_ref[...] = total_ref[...] + block
                first = row * per_group + (2 * owner + origin) * MB
                for micro in range(MB):
                    for piece in range(pieces):
                        line = micro * pieces + piece
                        mods[piece, pl.ds(first + micro, 1), :] = block[
                            line : line + 1, :model_width
                        ]
                return carry

            lax.fori_loop(0, 2 * groups * chips, unpack, 0)
            part[...] = jnp.zeros_like(part)
            rowsq_ref[matrices] = jnp.zeros_like(rowsq_ref[matrices])

        for piece in range(pieces):

            @pl.when(tick == piece_tick + piece)
            def _():
                every = acts_ref[...].reshape(groups * per_group, acts_ref.shape[2])
                mod = mods[piece].astype(low)
                mods_ref[piece] = mod
                value = mul(every, mod, TN)[:rows]
                square = value * value + TINY
                folded = square[:, :128]
                for start in range(128, model_width, 128):
                    folded = folded + square[:, start : start + 128]
                rowsq_ref[matrices] = rowsq_ref[matrices] + folded
                sums = jnp.sum(square, axis=0, keepdims=True)
                split = model_width // CHUNK
                for index in range(split):
                    line = total + piece * split + index
                    stats[line : line + 1] = sums[:, index * CHUNK : (index + 1) * CHUNK]
                mine = mods[piece, pl.ds(pl.multiple_of(grp * per_group, 8), per_group), :]
                back = mul(
                    mine.astype(low), ada_ref[:, piece * model_width : (piece + 1) * model_width], NT
                )
                part[:, :rows] = part[:, :rows] + back

        @pl.when(tick == cond_tick)
        def _():
            cond_across().start()

        @pl.when(tick == cond_tick + 2)
        def _():
            cond_across().wait_recv()
            cond_ref[me] = part[...] + part_in[...]
            cond_beside(me).start()

        @pl.when(tick == cond_tick + 4)
        def _():
            cond_beside(me ^ 1).wait_recv()
            for k in range(1, chips):
                cond_chip(k, chip).start()

        @pl.when(tick == cond_tick + 6)
        def _():
            for k in range(1, chips):
                cond_chip(k, chip ^ k).wait_recv()

    def beside_the_sum_sent():
        for k in range(1, chips):
            chip_spread(k, chip).wait_send()
            cond_chip(k, chip).wait_send()
        for side in range(2):
            for step in range(groups - 1):
                row = grp - step if side == 0 else grp + step
                came = (row >= 0) if side == 0 else (row < groups)

                @pl.when(came & exists(side))
                def _():
                    for copy in line_spread(side, step, row):
                        copy.wait_send()

        swap_spread(core).wait_send()
        cond_across().wait_send()
        cond_beside(me).wait_send()

    send_kind = jnp.where(depth == 0, 1, 0)
    lag3 = 1 + HOP * (middle - depth)
    lag5 = 1 + HOP * (middle + 1 + depth)
    held = HOP * (middle - 1) + 1
    rowsq_ref[...] = jnp.zeros_like(rowsq_ref)
    stats[...] = jnp.zeros_like(stats)
    stats[stats.shape[0] - 1 :] = tail_ref[...]
    spread[core, grp, chip] = pack_ref[...]
    acts_ref[grp] = act_ref[...]
    for k in range(1, chips):
        chip_spread(k, chip).start()
    fetch(0)
    fetch(1)

    def step(tick, carry):
        item0 = tick

        @pl.when(item0 < total)
        def _():
            slot = item0 % SLOTS

            @pl.when(item0 >= SLOTS)
            def _():
                copy1(item0 - SLOTS).wait_send()

            @pl.when(item0 + 2 < total)
            def _():
                fetch(item0 + 2)

            arrived(item0)
            matrix = which(item0)

            def product(shard):
                value = 0.0
                for micro in range(MB):
                    value = value + jnp.dot(
                        left_refs[micro][matrix, shard],
                        right_buf[item0 % 3, micro],
                        preferred_element_type=high,
                    )
                return value

            def multiply(k, carry):
                send1[slot, k] = product(2 * k + 1 - core).astype(low)
                keep1[item0 % 2, k] = product(2 * k + core)
                return carry

            lax.fori_loop(0, chips, multiply, 0)
            copy1(item0).start()

        item1 = tick - 1

        @pl.when((item1 >= 0) & (item1 < total))
        def _():
            slot = item1 % SLOTS
            copy1(item1).wait_recv()

            @pl.when(item1 >= SLOTS)
            def _():
                for k in range(1, chips):
                    copy2(item1 - SLOTS, k).wait_send()

            for k in range(1, chips):
                other = chip ^ k
                send2[slot, k - 1] = (
                    keep1[item1 % 2, other] + recv1[slot, other].astype(high)
                ).astype(low)
                copy2(item1, k).start()
            keep2[item1 % (HOP + 1)] = keep1[item1 % 2, chip] + recv1[slot, chip].astype(high)

        item2 = tick - 1 - HOP

        @pl.when((item2 >= 0) & (item2 < total))
        def _():
            slot = item2 % SLOTS
            value = keep2[item2 % (HOP + 1)]
            for k in range(1, chips):
                copy2(item2, k).wait_recv()
                value = value + recv2[slot, k - 1].astype(high)
            keep3[item2 % held] = value

        item3 = tick - lag3

        @pl.when((item3 >= 0) & (item3 < total))
        def _():
            slot = item3 % SLOTS

            @pl.when(item3 >= SLOTS)
            def _():
                copy3(item3 - SLOTS, send_kind).wait_send()

            @pl.when(has_outer)
            def _():
                copy3(item3, 0).wait_recv()
                send3[slot] = (keep3[item3 % held] + recv3[0, slot].astype(high)).astype(low)

            @pl.when(jnp.logical_not(has_outer))
            def _():
                send3[slot] = keep3[item3 % held].astype(low)

            copy3(item3, send_kind).start()

        item5 = tick - lag5

        @pl.when((item5 >= 0) & (item5 < total))
        def _():
            slot = item5 % ends
            other = item5 % SLOTS

            @pl.when(item5 >= ends)
            def _():
                wait_out(item5 - ends)

                @pl.when(has_outer)
                def _():
                    copy5(item5 - ends).wait_send()

            @pl.when(depth == 0)
            def _():
                copy3(item5, 1).wait_recv()
                final[slot] = (send3[other].astype(high) + recv3[1, other].astype(high)).astype(low)

            @pl.when(depth > 0)
            def _():
                copy5(item5).wait_recv()
                final[slot] = recv5[slot]

            @pl.when(has_outer)
            def _():
                copy5(item5).start()

            start_out(item5)
            value = final[slot].astype(high)
            square = value * value + TINY
            folded = square[:, :128]
            for start in range(128, CHUNK, 128):
                folded = folded + square[:, start : start + 128]
            matrix = which(item5)
            rowsq_ref[matrix] = rowsq_ref[matrix] + folded
            stats[pl.ds(item5, 1), :] = jnp.sum(square, axis=0, keepdims=True)

        beside_the_sum(tick)
        return carry

    lax.fori_loop(0, total + 1 + 2 * HOP * middle, step, 0)

    beside = remote(stats, stats_in, (stat_sem.at[0, 0], stat_sem.at[1, 0]), sibling)
    beside.start()
    beside.wait_recv()
    stats_all[chip] = stats[...] + stats_in[...]

    def stat_chip(k, owner):
        region = stats_all.at[owner]
        return remote(region, region, (stat_sem.at[0, k], stat_sem.at[1, k]), chip_peer(k))

    for k in range(1, chips):
        stat_chip(k, chip).start()
    for k in range(1, chips):
        stat_chip(k, chip ^ k).wait_recv()
    value = stats_all[0]
    for owner in range(1, chips):
        value = value + stats_all[owner]
    stats_ref[...] = value

    def drain(offset, carry):
        item = total - SLOTS + offset
        copy1(item).wait_send()
        for k in range(1, chips):
            copy2(item, k).wait_send()
        copy3(item, send_kind).wait_send()
        return carry

    lax.fori_loop(0, SLOTS, drain, 0)

    def drain_out(offset, carry):
        item = total - ends + offset
        wait_out(item)

        @pl.when(has_outer)
        def _():
            copy5(item).wait_send()

        return carry

    lax.fori_loop(0, ends, drain_out, 0)
    beside_the_sum_sent()
    beside.wait_send()
    for k in range(1, chips):
        stat_chip(k, chip).wait_send()


def reduce_grads(lefts, rights, packed, act, ada, tail):
    shards = lax.axis_size("shard")
    groups = lax.axis_size("grp")
    chips = shards // 2
    middle = groups // 2
    ends = 2 * groups
    matrices, _, rows, tokens = lefts[0].shape
    widths = [right.shape[1] for right in rights[0]]
    firsts = [sum(widths[:index]) // CHUNK for index in range(matrices)]
    model_width = shards * rows
    pieces = ada.shape[1] // model_width
    lines = sum(widths) // CHUNK + ada.shape[1] // CHUNK + 1
    low, high = jnp.bfloat16, jnp.float32
    block = (rows, CHUNK)
    near = pl.BlockSpec(memory_space=pltpu.VMEM)
    far = pl.BlockSpec(memory_space=pl.ANY)
    every = groups * act.shape[0]
    return pl.pallas_call(
        functools.partial(reduce_kernel, shards, groups, firsts, pieces),
        out_shape=[jax.ShapeDtypeStruct((rows, width), low) for width in widths]
        + [
            jax.ShapeDtypeStruct((matrices + 1, rows, 128), high),
            jax.ShapeDtypeStruct((lines, CHUNK), high),
            jax.ShapeDtypeStruct(packed.shape, high),
            jax.ShapeDtypeStruct((pieces, every, model_width), low),
            jax.ShapeDtypeStruct((groups,) + act.shape, low),
            jax.ShapeDtypeStruct((shards,) + act.shape, high),
        ],
        in_specs=[near] * MB + [far] * (MB * matrices) + [near] * 4,
        out_specs=[far] * matrices + [near] * 6,
        scratch_shapes=[
            pltpu.VMEM((3, MB, tokens, CHUNK), low),
            pltpu.VMEM((SLOTS, chips) + block, low),
            pltpu.VMEM((2, chips) + block, high),
            pltpu.VMEM((SLOTS, chips) + block, low),
            pltpu.VMEM((SLOTS, chips - 1) + block, low),
            pltpu.VMEM((SLOTS, chips - 1) + block, low),
            pltpu.VMEM((HOP + 1,) + block, high),
            pltpu.VMEM((HOP * (middle - 1) + 1,) + block, high),
            pltpu.VMEM((SLOTS,) + block, low),
            pltpu.VMEM((2, SLOTS) + block, low),
            pltpu.VMEM((ends,) + block, low),
            pltpu.VMEM((ends,) + block, low),
            pltpu.VMEM((2, groups, chips) + packed.shape, low),
            pltpu.VMEM((pieces, every, model_width), high),
            pltpu.VMEM(act.shape, high),
            pltpu.VMEM(act.shape, high),
            pltpu.VMEM((lines, CHUNK), high),
            pltpu.VMEM((lines, CHUNK), high),
            pltpu.VMEM((chips, lines, CHUNK), high),
            pltpu.SemaphoreType.DMA((3, MB)),
            pltpu.SemaphoreType.DMA((2, SLOTS)),
            pltpu.SemaphoreType.DMA((2, SLOTS, chips - 1)),
            pltpu.SemaphoreType.DMA((2, 2, SLOTS)),
            pltpu.SemaphoreType.DMA((2, ends)),
            pltpu.SemaphoreType.DMA((ends,)),
            pltpu.SemaphoreType.DMA((2, chips - 1)),
            pltpu.SemaphoreType.DMA((2, 2, groups, 2)),
            pltpu.SemaphoreType.DMA((2,)),
            pltpu.SemaphoreType.DMA((2, chips + 1)),
            pltpu.SemaphoreType.DMA((2, chips)),
        ],
        compiler_params=pltpu.CompilerParams(
            collective_id=1, has_side_effects=True, vmem_limit_bytes=60 * 1024 * 1024
        ),
        cost_estimate=pl.CostEstimate(flops=0, bytes_accessed=600_000_000, transcendentals=0),
        name="reduce_grads",
    )(*lefts, *[right for group in rights for right in group], packed, act, ada, tail)


def mul(left, right, form=(((1,), (0,)), ((), ()))):
    return lax.dot_general(left, right, form, preferred_element_type=jnp.float32)


def halves(value):
    upper = value.astype(jnp.bfloat16)
    return upper, (value - upper.astype(jnp.float32)).astype(jnp.bfloat16)


def mul_split(value, right, form=(((1,), (0,)), ((), ()))):
    upper, lower = halves(value)
    return mul(upper, right, form) + mul(lower, right, form)


def by_rows(work, init=0, size=ROWS):
    def step(index, carry):
        return work(pl.ds(pl.multiple_of(index * size, size), size), carry)

    return lax.fori_loop(0, LEN // size, step, init)


def aligned(start, size):
    return pl.ds(pl.multiple_of(start, 128), size)


def rms_rate(value):
    return lax.rsqrt(jnp.mean(value * value, axis=-1, keepdims=True) + EPS)


def turn(value, cosines, first, second):
    width = value.shape[1]
    quarter = HEAD_DIM // 4
    ahead = pltpu.roll(value, width - quarter, 1)
    behind = pltpu.roll(value, quarter, 1)
    return value * cosines, ahead * first + behind * second


def window(head, model_width):
    tile = jnp.minimum(head * HEAD_DIM // 128, model_width // 128 - 2)
    lane = lax.broadcasted_iota(jnp.int32, (1, 256), 1) + tile * 128 - head * HEAD_DIM
    mask = ((lane >= 0) & (lane < HEAD_DIM)).astype(jnp.bfloat16)
    return aligned(tile * 128, 256), mask


def ring_of(weights, ring, sems, order, count):
    def copy(item):
        slot = item % RING
        return pltpu.make_async_copy(weights.at[order(item)], ring.at[slot], sems.at[slot])

    def begin():
        for item in range(RING):
            copy(item).start()

    def ready(item):
        copy(item).wait()
        return item % RING

    def release(item):
        @pl.when(item + RING < count)
        def _():
            copy(item + RING).start()

    return begin, ready, release


def forward_kernel(
    active,
    live,
    x_ref,
    weights,
    mod_ref,
    bias_ref,
    gain_ref,
    cos_ref,
    first_ref,
    second_ref,
    member_ref,
    *rest,
    aliased,
):
    rest = rest[aliased:]
    out_ref, leave_ref, left_out, hid_out, low_out, prob_out, high_out, gu_out = rest[:8]
    (
        ring,
        a_buf,
        qkv,
        low_buf,
        prob,
        high_buf,
        gu_buf,
        hid,
        left,
        acc,
        out_buf,
        leave_buf,
        ring_sem,
        out_sem,
    ) = rest[8:]
    model_width = x_ref.shape[1]
    low, high = jnp.bfloat16, jnp.float32
    heads = model_width // HEAD_DIM
    chunks = weights.shape[0]
    wide = CHUNK

    @pl.when(active[0] == 1)
    def _():
        begin, ready, release = ring_of(weights, ring, ring_sem, lambda item: item, chunks)
        begin()
        copies = []

        def send(source, target):
            copy = pltpu.make_async_copy(source, target, out_sem.at[len(copies)])
            copy.start()
            copies.append(copy)

        shift1, scale1, gate1 = mod_ref[0:1], mod_ref[1:2], mod_ref[2:3]
        shift2, scale2, gate2 = mod_ref[3:4], mod_ref[4:5], mod_ref[5:6]

        def enter(rows, carry):
            x = x_ref[rows].astype(high)
            a_buf[rows] = (x * rms_rate(x) * (1.0 + scale1) + shift1).astype(low)
            return carry

        by_rows(enter)

        def project(item, carry):
            slot = ready(item)
            cols = aligned(item * wide, wide)
            qkv[:, cols] = mul(a_buf[...], ring[slot]) + bias_ref[:, cols]
            release(item)
            return carry

        qkv_chunks = 3 * model_width // wide
        lax.fori_loop(0, qkv_chunks, project, 0)
        left[0] = a_buf[...].T
        send(left.at[0], left_out.at[0])

        member = member_ref[...]
        for index in range(2):
            base = index * model_width
            cols = slice(base, base + model_width)
            raw = qkv[:, cols]
            rate = lax.rsqrt(mul_split(raw * raw, member) * (1.0 / HEAD_DIM) + EPS)
            acc[...] = mul_split(rate, member, NT)

            def turned(rows, carry):
                unit = qkv[rows, cols] * acc[rows]
                high_buf[rows, cols] = unit
                gained = unit * gain_ref[index : index + 1]
                straight, crossed = turn(gained, cos_ref[rows], first_ref[rows], second_ref[rows])
                low_buf[rows, cols] = (straight + crossed).astype(low)
                return carry

            by_rows(turned)
            high_buf[:, 5 * model_width + index * PAD : 5 * model_width + (index + 1) * PAD] = rate

        low_buf[:, 2 * model_width :] = qkv[:, 2 * model_width :].astype(low)
        send(low_buf, low_out)
        acc[...] = jnp.zeros_like(acc)

        def attend(head, carry):
            cols, mask = window(head, model_width)
            tile = cols.start
            q = low_buf[:, cols] * mask
            k = low_buf[:, aligned(model_width + tile, 256)]
            v = low_buf[:, aligned(2 * model_width + tile, 256)] * mask
            scores = mul(k, q, NT) * HEAD_DIM ** (-0.5)
            weight = jnp.exp(scores - jnp.max(scores, axis=0, keepdims=True))
            share = (weight * (1.0 / jnp.sum(weight, axis=0, keepdims=True))).astype(low)
            prob[head] = share
            acc[:, cols] = acc[:, cols] + mul(share, v, TN)
            return carry

        lax.fori_loop(0, heads, attend, 0, unroll=2)
        send(prob, prob_out)
        a_buf[...] = acc[...].astype(low)
        left[1] = a_buf[...].T
        send(left.at[1], left_out.at[1])

        out_chunks = model_width // wide

        def mix(index, carry):
            item = qkv_chunks + index
            slot = ready(item)
            cols = aligned(index * wide, wide)
            acc[:, cols] = mul(a_buf[...], ring[slot]) + bias_ref[
                :, aligned(3 * model_width + index * wide, wide)
            ]
            release(item)
            return carry

        lax.fori_loop(0, out_chunks, mix, 0)

        proj_cols = slice(2 * model_width, 3 * model_width)
        middle_cols = slice(3 * model_width, 4 * model_width)
        ffn_cols = slice(4 * model_width, 5 * model_width)

        def between(rows, carry):
            proj = acc[rows]
            high_buf[rows, proj_cols] = proj
            middle = x_ref[rows].astype(high) + gate1 * proj
            high_buf[rows, middle_cols] = middle
            a_buf[rows] = (middle * rms_rate(middle) * (1.0 + scale2) + shift2).astype(low)
            return carry

        by_rows(between)
        left[2] = a_buf[...].T
        send(left.at[2], left_out.at[2])

        gate_chunks = FF // wide

        def widen(index, carry):
            item = qkv_chunks + out_chunks + 2 * index
            cols = aligned(index * wide, wide)
            slot = ready(item)
            gate = mul(a_buf[...], ring[slot])
            release(item)
            slot = ready(item + 1)
            up = mul(a_buf[...], ring[slot])
            release(item + 1)
            gu_buf[:, cols] = gate
            gu_buf[:, aligned(FF + index * wide, wide)] = up
            hid[:, cols] = (gate * (1.0 / (1.0 + jnp.exp(-gate))) * up).astype(low)
            return carry

        lax.fori_loop(0, gate_chunks, widen, 0)
        send(gu_buf, gu_out)
        send(hid, hid_out)
        acc[...] = jnp.zeros_like(acc)

        def narrow(index, carry):
            item = qkv_chunks + out_chunks + 2 * gate_chunks + index
            slot = ready(item)
            acc[...] += mul(hid[:, aligned(index * wide, wide)], ring[slot], NT)
            release(item)
            return carry

        lax.fori_loop(0, gate_chunks, narrow, 0)

        def leave(rows, carry):
            ffn = acc[rows]
            high_buf[rows, ffn_cols] = ffn
            result = high_buf[rows, middle_cols] + gate2 * ffn
            leave_buf[rows] = result.astype(low)
            out_buf[rows] = (result * live[0]).astype(low)
            return carry

        by_rows(leave)
        send(leave_buf, leave_ref)
        send(out_buf, out_ref)
        send(high_buf, high_out)
        for copy in copies:
            copy.wait()


def layer_shapes(model_width):
    low, high = jnp.bfloat16, jnp.float32
    return [
        ((LEN, model_width), low),
        ((LEN, model_width), low),
        ((4, model_width, LEN), low),
        ((LEN, FF), low),
        ((LEN, 3 * model_width), low),
        ((HEADS, LEN, LEN), low),
        ((LEN, 5 * model_width + 2 * PAD), high),
        ((LEN, 2 * FF), high),
    ]


def run_forward(active, live, x, weights, mod, bias, gain, tables, member, kept):
    model_width = x.shape[1]
    low, high = jnp.bfloat16, jnp.float32
    shapes = layer_shapes(model_width)
    flag = pl.BlockSpec(memory_space=pltpu.SMEM)
    near = pl.BlockSpec(memory_space=pltpu.VMEM)
    far = pl.BlockSpec(memory_space=pl.ANY)
    kept = [] if kept is None else list(kept)
    return pl.pallas_call(
        functools.partial(forward_kernel, aliased=len(kept)),
        out_shape=[jax.ShapeDtypeStruct(shape, kind) for shape, kind in shapes],
        in_specs=[flag, flag, near, far] + [near] * 7 + [far] * len(kept),
        out_specs=[far] * len(shapes),
        input_output_aliases={11 + index: index for index in range(len(kept))},
        scratch_shapes=[
            pltpu.VMEM((RING, model_width, CHUNK), low),
            pltpu.VMEM((LEN, model_width), low),
            pltpu.VMEM((LEN, 3 * model_width), high),
            pltpu.VMEM((LEN, 3 * model_width), low),
            pltpu.VMEM((HEADS, LEN, LEN), low),
            pltpu.VMEM((LEN, 5 * model_width + 2 * PAD), high),
            pltpu.VMEM((LEN, 2 * FF), high),
            pltpu.VMEM((LEN, FF), low),
            pltpu.VMEM((3, model_width, LEN), low),
            pltpu.VMEM((LEN, model_width), high),
            pltpu.VMEM((LEN, model_width), low),
            pltpu.VMEM((LEN, model_width), low),
            pltpu.SemaphoreType.DMA((RING,)),
            pltpu.SemaphoreType.DMA((10,)),
        ],
        compiler_params=pltpu.CompilerParams(vmem_limit_bytes=60 * 1024 * 1024),
        cost_estimate=pl.CostEstimate(flops=0, bytes_accessed=80_000_000, transcendentals=0),
        name="layer_forward",
    )(active, live, x, weights, mod, bias, gain, *tables, member, *kept)


def backward_kernel(
    active,
    live,
    dy_ref,
    x_ref,
    weights,
    mod_ref,
    gain_ref,
    cos_ref,
    first_ref,
    second_ref,
    member_ref,
    low_in,
    prob_in,
    high_in,
    gu_in,
    *rest,
    aliased,
):
    rest = rest[aliased:]
    dx_out, left_out, dqkv_out, dproj_out, dgu_out, dmod_out, sums_out = rest[:7]
    (
        ring,
        dy,
        low_buf,
        prob,
        high_buf,
        gu_buf,
        dgu,
        dqkv,
        small,
        left,
        acc,
        middle_grad,
        mixed_grad,
        turned_q,
        turned_k,
        turned_v,
        dmod,
        sums,
        ring_sem,
        in_sem,
        out_sem,
    ) = rest[7:]
    model_width = x_ref.shape[1]
    low, high = jnp.bfloat16, jnp.float32
    heads = model_width // HEAD_DIM
    chunks = weights.shape[0]
    wide = CHUNK
    qkv_chunks = 3 * model_width // wide
    out_chunks = model_width // wide
    gate_chunks = FF // wide
    base = qkv_chunks + out_chunks

    def order(item):
        index = item // 3
        kind = item % 3
        ffn_item = jnp.where(
            kind == 0, base + 2 * gate_chunks + index, base + 2 * index + kind - 1
        )
        late = item - 3 * gate_chunks
        other = jnp.where(late < out_chunks, qkv_chunks + late, late - out_chunks)
        return jnp.where(late < 0, ffn_item, other)

    @pl.when(active[0] == 1)
    def _():
        begin, ready, release = ring_of(weights, ring, ring_sem, order, chunks)
        loads = [
            pltpu.make_async_copy(source, target, in_sem.at[index])
            for index, (source, target) in enumerate(
                ((high_in, high_buf), (gu_in, gu_buf), (low_in, low_buf), (prob_in, prob))
            )
        ]
        loads[0].start()
        loads[1].start()
        begin()
        loads[2].start()
        loads[3].start()
        copies = []

        def send(source, target):
            copy = pltpu.make_async_copy(source, target, out_sem.at[len(copies)])
            copy.start()
            copies.append(copy)

        scale1, gate1 = mod_ref[1:2], mod_ref[2:3]
        scale2, gate2 = mod_ref[4:5], mod_ref[5:6]
        proj_cols = slice(2 * model_width, 3 * model_width)
        middle_cols = slice(3 * model_width, 4 * model_width)
        ffn_cols = slice(4 * model_width, 5 * model_width)
        nothing = jnp.zeros((1, model_width), high)

        def total(value):
            return jnp.sum(value, axis=0, keepdims=True)

        loads[0].wait()

        def enter(rows, gate_sum):
            incoming = dy_ref[rows].astype(high) * live[0]
            dy[rows] = incoming
            small[rows] = (gate2 * incoming).astype(low)
            return gate_sum + total(incoming * high_buf[rows, ffn_cols])

        dmod[5:6] = by_rows(enter, nothing)
        left[...] = small[...].T
        send(left, left_out.at[3])
        acc[...] = jnp.zeros_like(acc)
        loads[1].wait()

        def ffn_back(index, carry):
            item = 3 * index
            slot = ready(item)
            d_hid = mul(small[...], ring[slot])
            release(item)
            cols = aligned(index * wide, wide)
            cols_up = aligned(FF + index * wide, wide)
            gate = gu_buf[:, cols]
            sigma = 1.0 / (1.0 + jnp.exp(-gate))
            gated = gate * sigma
            d_gate = (d_hid * gu_buf[:, cols_up] * (sigma + gated * (1.0 - sigma))).astype(low)
            d_up = (d_hid * gated).astype(low)
            dgu[:, cols] = d_gate
            dgu[:, cols_up] = d_up
            slot = ready(item + 1)
            part = mul(d_gate, ring[slot], NT)
            release(item + 1)
            slot = ready(item + 2)
            acc[...] += part + mul(d_up, ring[slot], NT)
            release(item + 2)
            return carry

        lax.fori_loop(0, gate_chunks, ffn_back, 0)
        send(dgu, dgu_out)

        def between(rows, carry):
            scale_sum, shift_sum, gate_sum = carry
            middle = high_buf[rows, middle_cols]
            rate = rms_rate(middle)
            unit = middle * rate
            back = acc[rows]
            d_unit = back * (1.0 + scale2)
            grad = dy[rows] + rate * (
                d_unit - unit * jnp.mean(d_unit * unit, axis=-1, keepdims=True)
            )
            middle_grad[rows] = grad
            d_proj = (gate1 * grad).astype(low)
            small[rows] = d_proj
            return (
                scale_sum + total(back * unit),
                shift_sum + total(back),
                gate_sum + total(grad * high_buf[rows, proj_cols]),
            )

        scale_sum, shift_sum, gate_sum = by_rows(between, (nothing,) * 3)
        dmod[4:5] = scale_sum
        dmod[3:4] = shift_sum
        dmod[2:3] = gate_sum
        send(small, dproj_out)

        def proj_sum(rows, carry):
            return carry + total(small[rows].astype(high))

        sums[3:4] = by_rows(proj_sum, nothing)
        acc[...] = jnp.zeros_like(acc)

        def mixed_back(index, carry):
            item = 3 * gate_chunks + index
            slot = ready(item)
            acc[...] += mul(small[:, aligned(index * wide, wide)], ring[slot], NT)
            release(item)
            return carry

        lax.fori_loop(0, out_chunks, mixed_back, 0)
        mixed_grad[...] = acc[...].astype(low)
        loads[2].wait()
        loads[3].wait()
        for buffer in (turned_q, turned_k, turned_v):
            buffer[...] = jnp.zeros_like(buffer)

        def attend_back(head, carry):
            cols, mask = window(head, model_width)
            tile = cols.start
            q = low_buf[:, cols] * mask
            k = low_buf[:, aligned(model_width + tile, 256)] * mask
            v = low_buf[:, aligned(2 * model_width + tile, 256)]
            d_mixed = mixed_grad[:, cols] * mask
            share = prob[head]
            d_share = mul(v, d_mixed, NT)
            wide_share = share.astype(high)
            product = wide_share * d_share
            d_score = (product - wide_share * jnp.sum(product, axis=0, keepdims=True)).astype(low)
            turned_v[:, cols] = turned_v[:, cols] + mul(share, d_mixed)
            turned_k[:, cols] = turned_k[:, cols] + mul(d_score, q)
            turned_q[:, cols] = turned_q[:, cols] + mul(d_score, k, TN)
            return carry

        lax.fori_loop(0, heads, attend_back, 0, unroll=2)
        member = member_ref[...]
        for index, turned in enumerate((turned_q, turned_k)):
            cols = slice(index * model_width, (index + 1) * model_width)

            def unturn(rows, gain_sum):
                straight, crossed = turn(
                    turned[rows] * HEAD_DIM ** (-0.5),
                    cos_ref[rows],
                    first_ref[rows],
                    second_ref[rows],
                )
                d_norm = straight - crossed
                unit = high_buf[rows, cols]
                d_unit = d_norm * gain_ref[index : index + 1]
                turned[rows] = d_unit
                acc[rows] = d_unit * unit
                return gain_sum + total(d_norm * unit)

            sums[4 + index : 5 + index] = by_rows(unturn, nothing)
            level = mul_split(acc[...], member) * (1.0 / HEAD_DIM)
            rate = high_buf[:, 5 * model_width + index * PAD : 5 * model_width + (index + 1) * PAD]
            acc[...] = mul_split(rate * level, member, NT)
            dy[...] = mul_split(rate, member, NT)

            def unscale(rows, carry):
                d_raw = dy[rows] * turned[rows] - high_buf[rows, cols] * acc[rows]
                d_low = d_raw.astype(low)
                dqkv[rows, cols] = d_low
                return carry + total(d_low.astype(high))

            sums[index : index + 1] = by_rows(unscale, nothing)

        def values(rows, carry):
            d_low = turned_v[rows].astype(low)
            dqkv[rows, 2 * model_width :] = d_low
            return carry + total(d_low.astype(high))

        sums[2:3] = by_rows(values, nothing)
        send(dqkv, dqkv_out)
        acc[...] = jnp.zeros_like(acc)

        def project_back(index, carry):
            item = 3 * gate_chunks + out_chunks + index
            slot = ready(item)
            acc[...] += mul(dqkv[:, aligned(index * wide, wide)], ring[slot], NT)
            release(item)
            return carry

        lax.fori_loop(0, qkv_chunks, project_back, 0)

        def leave(rows, carry):
            scale_sum, shift_sum = carry
            x = x_ref[rows].astype(high)
            rate = rms_rate(x)
            unit = x * rate
            back = acc[rows]
            d_unit = back * (1.0 + scale1)
            grad = middle_grad[rows] + rate * (
                d_unit - unit * jnp.mean(d_unit * unit, axis=-1, keepdims=True)
            )
            mixed_grad[rows] = grad.astype(low)
            return scale_sum + total(back * unit), shift_sum + total(back)

        scale_sum, shift_sum = by_rows(leave, (nothing,) * 2)
        dmod[1:2] = scale_sum
        dmod[0:1] = shift_sum
        send(mixed_grad, dx_out)
        send(dmod, dmod_out)
        send(sums, sums_out)
        for copy in copies:
            copy.wait()


def run_backward(active, live, dy, x, weights, mod, gain, tables, member, parts, left, kept):
    model_width = x.shape[1]
    low, high = jnp.bfloat16, jnp.float32
    shapes = [
        ((LEN, model_width), low),
        ((4, model_width, LEN), low),
        ((LEN, 3 * model_width), low),
        ((LEN, model_width), low),
        ((LEN, 2 * FF), low),
        ((8, model_width), high),
        ((8, model_width), high),
    ]
    flag = pl.BlockSpec(memory_space=pltpu.SMEM)
    near = pl.BlockSpec(memory_space=pltpu.VMEM)
    far = pl.BlockSpec(memory_space=pl.ANY)
    if kept is None:
        extra, aliases = [left], {15: 1}
    else:
        extra = list(kept)
        aliases = {15 + index: index for index in range(len(extra))}
    return pl.pallas_call(
        functools.partial(backward_kernel, aliased=len(extra)),
        out_shape=[jax.ShapeDtypeStruct(shape, kind) for shape, kind in shapes],
        in_specs=[flag, flag, near, near, far] + [near] * 6 + [far] * (4 + len(extra)),
        out_specs=[far] * len(shapes),
        input_output_aliases=aliases,
        scratch_shapes=[
            pltpu.VMEM((RING, model_width, CHUNK), low),
            pltpu.VMEM((LEN, model_width), high),
            pltpu.VMEM((LEN, 3 * model_width), low),
            pltpu.VMEM((HEADS, LEN, LEN), low),
            pltpu.VMEM((LEN, 5 * model_width + 2 * PAD), high),
            pltpu.VMEM((LEN, 2 * FF), high),
            pltpu.VMEM((LEN, 2 * FF), low),
            pltpu.VMEM((LEN, 3 * model_width), low),
            pltpu.VMEM((LEN, model_width), low),
            pltpu.VMEM((model_width, LEN), low),
            pltpu.VMEM((LEN, model_width), high),
            pltpu.VMEM((LEN, model_width), high),
            pltpu.VMEM((LEN, model_width), low),
            pltpu.VMEM((LEN, model_width), high),
            pltpu.VMEM((LEN, model_width), high),
            pltpu.VMEM((LEN, model_width), high),
            pltpu.VMEM((8, model_width), high),
            pltpu.VMEM((8, model_width), high),
            pltpu.SemaphoreType.DMA((RING,)),
            pltpu.SemaphoreType.DMA((4,)),
            pltpu.SemaphoreType.DMA((10,)),
        ],
        compiler_params=pltpu.CompilerParams(vmem_limit_bytes=60 * 1024 * 1024),
        cost_estimate=pl.CostEstimate(flops=0, bytes_accessed=120_000_000, transcendentals=0),
        name="layer_backward",
    )(active, live, dy, x, weights, mod, gain, *tables, member, *parts, *extra)


def update_kernel(firsts, kinds, *refs):
    count = len(kinds)
    lows = [kind for kind in kinds if kind != "ada"]
    sums, refs = refs[: len(lows)], refs[len(lows) :]
    olds, refs = refs[:count], refs[count:]
    rowsq_ref, stats_ref, other_ref, feature_ref, mods_ref, acts_ref = refs[:6]
    grads, refs = refs[6 : 6 + count], refs[6 + count :]
    news, refs = refs[:count], refs[count:]
    (
        other_out,
        feature_out,
        low_buf,
        old_buf,
        grad_buf,
        new_buf,
        scales,
        in_sem,
        out_sem,
    ) = refs
    high = jnp.float32
    rows = rowsq_ref.shape[1]
    total = other_ref.shape[0]
    model_width = mods_ref.shape[2]
    bounds = list(firsts) + [total]
    source = {}
    line = 0
    for index, kind in enumerate(kinds):
        if kind != "ada":
            source[index] = line
            line += bounds[index + 1] - bounds[index]
    source[kinds.index("ada")] = line
    statistic = {index: lows.index(kind) for index, kind in enumerate(kinds) if kind != "ada"}
    statistic[kinds.index("ada")] = len(lows)

    def cols(item, index):
        return pl.ds(pl.multiple_of((item - firsts[index]) * CHUNK, CHUNK), CHUNK)

    def loads(item, index):
        slot = item % IN_SLOTS
        copies = [(olds[index].at[:, cols(item, index)], old_buf.at[slot])]
        if kinds[index] != "ada":
            copies.append(
                (sums[lows.index(kinds[index])].at[:, cols(item, index)], low_buf.at[slot])
            )
        return [
            pltpu.make_async_copy(start, end, in_sem.at[slot, number])
            for number, (start, end) in enumerate(copies)
        ]

    def stores(item, index):
        slot = item % OUT_SLOTS
        copies = (
            (grad_buf.at[slot], grads[index].at[:, cols(item, index)]),
            (new_buf.at[slot], news[index].at[:, cols(item, index)]),
        )
        return [
            pltpu.make_async_copy(start, end, out_sem.at[slot, number])
            for number, (start, end) in enumerate(copies)
        ]

    def each(item, work):
        for index in range(count):

            @pl.when((item >= bounds[index]) & (item < bounds[index + 1]))
            def _():
                work(index)

    def begin_loads(item):
        def work(index):
            for copy in loads(item, index):
                copy.start()

        each(item, work)

    def end_stores(item):
        def work(index):
            for copy in stores(item, index):
                copy.wait()

        each(item, work)

    for item in range(IN_SLOTS - 1):
        begin_loads(item)

    for index in range(count):
        width = (bounds[index + 1] - bounds[index]) * CHUNK
        row_sum = jnp.sum(rowsq_ref[statistic[index]], axis=1, keepdims=True)
        feature = DECAY * feature_ref[:, index : index + 1] + (1.0 - DECAY) / width * row_sum
        feature_out[:, index : index + 1] = feature
        lines = stats_ref[source[index] : source[index] + bounds[index + 1] - bounds[index]]
        squares = jnp.sum(jnp.sum(lines, axis=0, keepdims=True), axis=1, keepdims=True)
        last = stats_ref.shape[0] - 1
        mean = (
            DECAY * stats_ref[last : last + 1, index : index + 1]
            + (1.0 - DECAY) / width * squares
        ) / model_width
        scales[index] = lax.rsqrt(feature / mean) * RATE
        other_out[bounds[index] : bounds[index + 1]] = (
            DECAY * other_ref[bounds[index] : bounds[index + 1]]
            + (1.0 - DECAY) / model_width * lines
        )

    def step(item, carry):
        @pl.when(item + IN_SLOTS - 1 < total)
        def _():
            begin_loads(item + IN_SLOTS - 1)

        @pl.when(item >= OUT_SLOTS)
        def _():
            end_stores(item - OUT_SLOTS)

        place_in = item % IN_SLOTS
        place_out = item % OUT_SLOTS
        columns = lax.rsqrt(other_out[pl.ds(item, 1), :])

        def work(index):
            for copy in loads(item, index):
                copy.wait()
            if kinds[index] == "ada":
                local = item - firsts[index]
                split = model_width // CHUNK
                start = pl.multiple_of((local % split) * CHUNK, CHUNK)
                mod = mods_ref[local // split, :, pl.ds(start, CHUNK)]
                gradient = mul(acts_ref[...], mod, TN)[:rows]
            else:
                gradient = low_buf[place_in].astype(high)
            delta = gradient * scales[index] * columns
            grad_buf[place_out] = gradient
            new_buf[place_out] = old_buf[place_in] - delta
            for copy in stores(item, index):
                copy.start()

        each(item, work)
        return carry

    lax.fori_loop(0, total, step, 0)

    def drain(offset, carry):
        end_stores(total - OUT_SLOTS + offset)
        return carry

    lax.fori_loop(0, OUT_SLOTS, drain, 0)


def update_matrices(sums, olds, kinds, row_squares, stats, other, feature, mods, acts):
    high = jnp.float32
    rows = olds[0].shape[0]
    widths = [old.shape[1] for old in olds]
    firsts = [sum(widths[:index]) // CHUNK for index in range(len(widths))]
    near = pl.BlockSpec(memory_space=pltpu.VMEM)
    far = pl.BlockSpec(memory_space=pl.ANY)
    shapes = [jax.ShapeDtypeStruct(old.shape, high) for old in olds]
    return pl.pallas_call(
        functools.partial(update_kernel, firsts, kinds),
        out_shape=shapes
        + shapes
        + [
            jax.ShapeDtypeStruct(other.shape, high),
            jax.ShapeDtypeStruct(feature.shape, high),
        ],
        in_specs=[far] * (len(sums) + len(olds)) + [near] * 6,
        out_specs=[far] * (2 * len(olds)) + [near] * 2,
        scratch_shapes=[
            pltpu.VMEM((IN_SLOTS, rows, CHUNK), jnp.bfloat16),
            pltpu.VMEM((IN_SLOTS, rows, CHUNK), high),
            pltpu.VMEM((OUT_SLOTS, rows, CHUNK), high),
            pltpu.VMEM((OUT_SLOTS, rows, CHUNK), high),
            pltpu.VMEM((len(olds), rows, 1), high),
            pltpu.SemaphoreType.DMA((IN_SLOTS, 2)),
            pltpu.SemaphoreType.DMA((OUT_SLOTS, 2)),
        ],
        compiler_params=pltpu.CompilerParams(vmem_limit_bytes=60 * 1024 * 1024),
        cost_estimate=pl.CostEstimate(flops=0, bytes_accessed=90_000_000, transcendentals=0),
        name="update_matrices",
    )(*sums, *olds, row_squares, stats, other, feature, mods, acts)


def body(
    start,
    out_grad,
    extra_images,
    timesteps,
    labels,
    embed_table,
    w_qkv,
    w_out,
    w_gu,
    w_ada,
    w_down,
    small_params,
    feature_moments,
    other_moments,
    small_moment,
):
    model_width = start.shape[-1]
    section_index = lax.axis_index("section")
    shard_index = lax.axis_index("shard")
    shards = lax.axis_size("shard")
    rows = w_qkv.shape[1]
    low = jnp.bfloat16
    high = jnp.float32
    widths = (3 * model_width, model_width, 2 * FF, FF)
    starts = (0, widths[0], widths[0] + widths[1], widths[0] + widths[1] + widths[2])
    entries = lax.broadcasted_iota(jnp.int32, (MB, embed_table.shape[0]), 1)
    chosen = (entries == timesteps[:, None]) | (entries == TIMESTEPS + labels[:, None])
    half_cond = jnp.dot(chosen.astype(high), embed_table, precision=lax.Precision.HIGHEST)
    cond_block = jnp.pad(half_cond, ((0, 8 - MB), (0, -half_cond.shape[1] % 128)))
    small_rows = small_params.shape[1]
    small_block = jnp.pad(small_params[0], (0, -small_rows % 1024)).reshape(8, -1)
    weights, ada_low, act_rows, modulation, small_blocks = gather_rows(
        cond_block, small_block, w_qkv[0], w_out[0], w_gu[0], w_down[0].T, w_ada[0]
    )
    weights = weights.reshape(weights.shape[0], model_width, CHUNK)
    small_all = small_blocks.reshape(shards, -1)[:, :small_rows].reshape(-1)
    small_all = small_all.astype(low).astype(high)
    bias = small_all[None, : 4 * model_width]
    modulation = modulation + small_all[4 * model_width : 10 * model_width]
    gain = jnp.tile(small_all[10 * model_width :].reshape(2, HEAD_DIM), (1, HEADS))
    tables = rope_tables(model_width)
    member = head_members(model_width)
    image_count = extra_images[0] + 1
    live = [(jnp.full((1,), micro) < image_count).astype(high) for micro in range(MB)]
    here = [jnp.full((1,), section_index == index, jnp.int32) for index in range(2)]
    mods = [modulation[micro].reshape(6, model_width) for micro in range(MB)]
    fixed = (gain, tables, member)
    kept = []
    received = []
    for micro in range(MB):
        result = run_forward(
            here[0], live[micro], start[micro], weights, mods[micro], bias, *fixed, None
        )
        kept.append(result)
        received.append(passed_along(result[1], "section", 1))
    for micro in range(MB):
        kept[micro] = run_forward(
            here[1], live[micro], received[micro], weights, mods[micro], bias, *fixed, kept[micro]
        )
    section_out = jnp.stack([result[0] for result in kept])
    grads_kept = []
    returned = []
    for micro in range(MB):
        result = run_backward(
            here[1],
            live[micro],
            out_grad[micro],
            received[micro],
            weights,
            mods[micro],
            *fixed,
            kept[micro][4:],
            kept[micro][2],
            None,
        )
        grads_kept.append(result)
        returned.append(passed_along(result[0], "section", -1))
    for micro in range(MB):
        grads_kept[micro] = run_backward(
            here[0],
            live[micro],
            returned[micro],
            start[micro],
            weights,
            mods[micro],
            *fixed,
            kept[micro][4:],
            None,
            grads_kept[micro],
        )
    section_in_grad = jnp.stack([result[0] for result in grads_kept])
    lefts = [result[1].reshape(4, shards, rows, LEN) for result in grads_kept]
    rights = [
        [result[2], result[3], result[4], kept[micro][3]]
        for micro, result in enumerate(grads_kept)
    ]
    sums = sum(result[6] for result in grads_kept)
    gains = jnp.sum(sums[4:6].reshape(2, HEADS, HEAD_DIM), axis=1)
    packed = jnp.concatenate([result[5][:6] for result in grads_kept] + [sums[:4]], axis=0)
    beside = jnp.pad(gains, ((0, packed.shape[0] - 2), (0, PAD - HEAD_DIM)))
    packed = jnp.concatenate([packed, beside], axis=1).astype(low)
    tail = jnp.pad(jnp.sum(feature_moments[0], axis=1)[None], ((0, 0), (0, CHUNK - 5)))
    reduced = reduce_grads(lefts, rights, packed, act_rows, ada_low, tail)
    sum_low = reduced[:4]
    row_squares, stats, totals, all_mod, every_act, cond_parts = reduced[4:]
    small_vector = jnp.concatenate(
        [
            totals[12:16, :model_width].reshape(-1),
            (totals[:6] + totals[6:12])[:, :model_width].reshape(-1),
            totals[:2, model_width : model_width + HEAD_DIM].reshape(-1),
        ]
    )
    small_grad = lax.dynamic_slice_in_dim(small_vector, shard_index * small_rows, small_rows, 0)
    half = half_cond.shape[1]
    own_part = lax.dynamic_slice_in_dim(cond_parts, shard_index * MB, MB, 1)[:, :, :rows]
    act_grad = own_part.transpose(1, 0, 2).reshape(MB, model_width)
    act_grad = lax.dynamic_slice_in_dim(act_grad, section_index * half, half, 1)
    sigma = jax.nn.sigmoid(half_cond)
    cond_grad = act_grad * sigma * (1.0 + half_cond * (1.0 - sigma))
    kinds = ("qkv", "out", "gu", "ada", "down")
    lines = other_moments.shape[1] // CHUNK
    updated = update_matrices(
        sum_low,
        (w_qkv[0], w_out[0], w_gu[0], w_ada[0], w_down[0].T),
        kinds,
        row_squares,
        stats,
        other_moments.reshape(lines, CHUNK),
        feature_moments[0].T,
        all_mod,
        every_act.reshape(-1, every_act.shape[2]),
    )
    grads = [*updated[:4], updated[4].T]
    new_wide = [*updated[5:9], updated[9].T]
    other_new = updated[10].reshape(-1)
    feature_new = updated[11].T
    small_new = DECAY * small_moment[0] + (1.0 - DECAY) * (small_grad * small_grad + TINY)
    new_small = small_params[0] - RATE_SMALL * small_grad * lax.rsqrt(small_new)
    return (
        section_out[None],
        section_in_grad[None],
        cond_grad,
        *[grad[None] for grad in grads],
        small_grad[None],
        *[new[None] for new in new_wide],
        new_small[None],
        feature_new[None],
        other_new[None],
        small_new[None],
    )


def solution(mesh):
    in_specs = (
        P(("grp", "shard"), None, None),
        P(("grp", "shard"), None, None),
        P(("grp", "shard")),
        P(("grp", "shard")),
        P(("grp", "shard")),
        P(None, "section"),
        P("section", "shard", None),
        P("section", "shard", None),
        P("section", "shard", None),
        P("section", "shard", None),
        P("section", None, "shard"),
        P("section", "shard"),
        P("section", None, "shard"),
        P("section", None),
        P("section", "shard"),
    )
    out_specs = (
        P("section", ("grp", "shard"), None, None),
        P("section", ("grp", "shard"), None, None),
        P(("grp", "shard"), "section"),
        P("section", "shard", None),
        P("section", "shard", None),
        P("section", "shard", None),
        P("section", "shard", None),
        P("section", None, "shard"),
        P("section", "shard"),
        P("section", "shard", None),
        P("section", "shard", None),
        P("section", "shard", None),
        P("section", "shard", None),
        P("section", None, "shard"),
        P("section", "shard"),
        P("section", None, "shard"),
        P("section", None),
        P("section", "shard"),
    )
    return jax.shard_map(body, mesh=mesh, in_specs=in_specs, out_specs=out_specs, check_vma=False)
```
